32 devices in a mesh: groups: 2 (over x), tm: 16 (over z, y, core).
Axes of the slice: x: 2, y: 2, z: 4, core: 2. Of those that a mesh axis runs over, the one named last changes fastest.
Arguments:
- queries: bfloat16 [12288, 2240], P(('groups', 'tm')), parts along dimension 0, may hold values from -40 to 40
- keys: bfloat16 [12288, 2240], P(('groups', 'tm')), parts along dimension 0, may hold values from -6 to 6
- values: bfloat16 [12288, 2240], P(('groups', 'tm')), parts along dimension 0, may hold values from -6 to 6
- cross_queries: bfloat16 [12288, 2240], P(('groups', 'tm')), parts along dimension 0, may hold values from -540 to 540
- prompt_keys: bfloat16 [32, 128, 2240], P(('groups', 'tm')), parts along dimension 0, may hold values from -6 to 6
- prompt_values: bfloat16 [32, 128, 2240], P(('groups', 'tm')), parts along dimension 0, may hold values from -6 to 6
- caption_keys: bfloat16 [256, 2240], P('groups'), parts along dimension 0, may hold values from -6 to 6
- caption_values: bfloat16 [256, 2240], P('groups'), parts along dimension 0, may hold values from -6 to 6
- span_start: int32 [32], P('groups'), parts along dimension 0, may hold values from 0 to 15, as said below
- span_end: int32 [32], P('groups'), parts along dimension 0, may hold values from 1 to 16
- prompt_tokens: int32 [32], P('groups'), parts along dimension 0, may hold values from 80 to 128, as said below
- region_mask: int32 [32, 3], P('groups'), parts along dimension 0, may hold values 0 or 1
- out_gain: float32 [2240], replicated, may hold values from 0.5 to 1.5
Outputs:
- self_mixed: bfloat16 [12288, 2240], P(('groups', 'tm')), parts along dimension 0
- cross_mixed: bfloat16 [12288, 2240], P(('groups', 'tm')), parts along dimension 0
The draws below stay inside these ranges and needn't reach their ends.
There are 2 independent parts, one for each index of `groups`. The reference program is written for one: setup_inputs(seed, part) draws one part's arguments, and reference() takes and returns one part's arrays. A program takes and returns all parts, laid end to end along the dimension named above; an argument that names none is the same for every part. Nothing has to cross between parts.
Inputs may be any that keep to these rules, and one draw needn't show every extreme that they name: Prompt p applies to stretches span_start[p] to span_end[p] - 1, with p <= span_start[p] <= p + 1 and span_start[p] < span_end[p] <= p + 6; prompt 0 covers stretches 0 to 5. `prompt_tokens`: prompt 0 uses all 128 slots.
All inputs are finite; a program needn't handle non-finite values.
Results may differ from the reference program's by a relative error of at most 0.007.
Values may be sent and summed in bfloat16 or wider, within the bound.
No kernel may reach another device: no remote copies, remote signals or barrier semaphores. Data moves between devices by JAX's collectives and lax.ppermute only.
A program may use at most 128 MiB of HBM per device.

```python
import math
import jax
import jax.numpy as jnp
from jax import lax

D = 2240
HD = 32
TOK_DEV = 384
TILES = 3
STRETCHES = 16
TOKENS = 6144
SPAN = 6
PR_DEV = 1
PROMPTS = 16
PL = 128
GL = 128


def caption_base(key):
    return jnp.clip(jax.random.normal(jax.random.fold_in(key, 11), (GL, D), jnp.float32), -6.0, 6.0)


def draw_caption_keys(key, part):
    drawn = caption_base(key)
    return drawn.astype(jnp.bfloat16)


def draw_cross_queries(key, part):
    drawn = jnp.clip(jax.random.normal(jax.random.fold_in(key, 21), (TOKENS, D), jnp.float32), -6.0, 6.0)
    return drawn.astype(jnp.bfloat16)


def draw_queries(key, part):
    head_count = D // HD
    head_scale = jnp.exp(jax.random.uniform(jax.random.fold_in(key, 31), (head_count,), jnp.float32, 0.0, math.log(10.0)))
    drawn = jnp.clip(jax.random.normal(jax.random.fold_in(key, 33), (TOKENS, D), jnp.float32), -4.0, 4.0)
    column_scale = jnp.repeat(head_scale, HD)
    return (drawn * column_scale[None, :]).astype(jnp.bfloat16)


def span_pair(key):
    prompt_ids = jnp.arange(PROMPTS, dtype=jnp.int32)
    owner_ids = prompt_ids // PR_DEV
    offset = jax.random.randint(jax.random.fold_in(key, 41), (PROMPTS,), 0, 2, dtype=jnp.int32)
    offset = jnp.where(prompt_ids == 0, 0, offset)
    room_left = SPAN - offset
    partial_len = 1 + jax.random.randint(jax.random.fold_in(key, 42), (PROMPTS,), 0, 1 << 20, dtype=jnp.int32) % room_left
    full_reach = jax.random.randint(jax.random.fold_in(key, 43), (PROMPTS,), 0, 10, dtype=jnp.int32) < 7
    length = jnp.where(full_reach, room_left, partial_len)
    length = jnp.where(prompt_ids == 0, SPAN, length)
    begins = jnp.minimum(owner_ids + offset, STRETCHES - 1)
    finish = jnp.minimum(begins + length, STRETCHES)
    return (begins.astype(jnp.int32), finish.astype(jnp.int32))


def draw_span_start(key, part):
    return span_pair(key)[0]


def draw_span_end(key, part):
    return span_pair(key)[1]


def draw_prompt_tokens(key, part):
    least = PL * 5 // 8
    counts = jax.random.randint(jax.random.fold_in(key, 51), (PROMPTS,), least, PL + 1, dtype=jnp.int32)
    prompt_ids = jnp.arange(PROMPTS)
    counts = jnp.where(prompt_ids == 1, least, counts)
    return jnp.where(prompt_ids == 0, PL, counts).astype(jnp.int32)


def with_ends(result, key, low, high):
    dims = result.shape
    spot = [jax.random.randint(jax.random.fold_in(key, axis), (), 0, dims[axis]) for axis in range(len(dims))]
    result = result.at[tuple(spot)].set(low)
    longest = dims.index(max(dims))
    spot[longest] = (spot[longest] + 1) % dims[longest]
    return result.at[tuple(spot)].set(high)


def level_of(rng, extent, pieces, low, top_value):
    def one(position, shards_of):
        heights = jax.random.uniform(jax.random.fold_in(jax.random.fold_in(rng, 6), position), (shards_of,), jnp.float32, low / len(pieces), top_value / len(pieces))
        return jnp.repeat(jnp.exp(heights), extent[position] // shards_of).reshape((-1,) + (1,) * (len(extent) - position - 1))

    loudness = one(*pieces[0])
    for cut in pieces[1:]:
        loudness = loudness * one(*cut)
    return loudness


def scatter_about(own_key, extent, scale, bound, shards=(), kind=jnp.bfloat16):
    loudness = level_of(own_key, extent, shards, -0.22, 0.18) if shards else 1.0
    values = jax.random.normal(own_key, extent, jnp.float32) * scale * loudness
    return jnp.minimum(jnp.maximum(values, -bound), bound).astype(kind)


def setup_inputs(seed: int = 0, part: int = 0) -> dict:
    splits = jax.random.split(jax.random.key(seed), 14)
    own_keys = jax.random.split(jax.random.fold_in(splits[13], part), 14)
    return {
        "queries": draw_queries(jax.random.fold_in(jax.random.fold_in(splits[13], part), 71), part),
        "keys": scatter_about(own_keys[1], (TOKENS, D), 1.0, 6.0, ((0, 16),)),
        "values": scatter_about(own_keys[2], (TOKENS, D), 1.0, 6.0, ((0, 16),)),
        "cross_queries": draw_cross_queries(jax.random.fold_in(jax.random.fold_in(splits[13], part), 71), part),
        "prompt_keys": scatter_about(own_keys[4], (PROMPTS, PL, D), 1.0, 6.0, ((0, 16),)),
        "prompt_values": scatter_about(own_keys[5], (PROMPTS, PL, D), 1.0, 6.0, ((0, 16),)),
        "caption_keys": draw_caption_keys(jax.random.fold_in(jax.random.fold_in(splits[13], part), 71), part),
        "caption_values": scatter_about(own_keys[7], (GL, D), 1.0, 6.0),
        "span_start": draw_span_start(jax.random.fold_in(jax.random.fold_in(splits[13], part), 71), part),
        "span_end": draw_span_end(jax.random.fold_in(jax.random.fold_in(splits[13], part), 71), part),
        "prompt_tokens": draw_prompt_tokens(jax.random.fold_in(jax.random.fold_in(splits[13], part), 71), part),
        "region_mask": with_ends((jax.random.randint(own_keys[11], (PROMPTS, TILES), 0, 2) < 1).astype(jnp.int32), jax.random.fold_in(own_keys[11], 1), 0, 1),
        "out_gain": jnp.clip(1.0 + 0.1 * jax.random.normal(splits[12], (D,), jnp.float32), 0.5, 1.5),
    }


def prompt_tiles(owner_id, stretch_id, span_start, span_end, prompt_tokens, region_mask):
    first_row = jnp.maximum(owner_id, 0).astype(jnp.int32) * PR_DEV
    begins = lax.dynamic_slice_in_dim(span_start, first_row, PR_DEV, 0)
    finish = lax.dynamic_slice_in_dim(span_end, first_row, PR_DEV, 0)
    counts = lax.dynamic_slice_in_dim(prompt_tokens, first_row, PR_DEV, 0)
    regions = lax.dynamic_slice_in_dim(region_mask, first_row, PR_DEV, 0)
    covers = (owner_id >= 0) & (begins <= stretch_id) & (stretch_id < finish)
    live_keys = jnp.arange(PL, dtype=jnp.int32)[None, :] < counts[:, None]
    visible_set = covers[:, None, None] & (regions[:, :, None] == 1) & live_keys[:, None, :]
    return jnp.transpose(visible_set, (1, 0, 2)).reshape(regions.shape[1], PR_DEV * PL)

def per_token(tile_mask, tok_rows):
    tile_count, key_count = tile_mask.shape
    spread_out = jnp.broadcast_to(tile_mask[:, None, :], (tile_count, tok_rows // tile_count, key_count))
    return spread_out.reshape(tok_rows, key_count)

def reference(queries, keys, values, cross_queries, prompt_keys, prompt_values, caption_keys, caption_values, span_start, span_end, prompt_tokens, region_mask, out_gain):
    head_count = D // HD
    lifted_q = jnp.maximum(queries, 0).astype(jnp.float32).reshape(STRETCHES, TOK_DEV, head_count, HD)
    lifted_k = jnp.maximum(keys, 0).astype(jnp.float32).reshape(STRETCHES, TOK_DEV, head_count, HD)
    value_rows = values.astype(jnp.float32).reshape(STRETCHES, TOK_DEV, head_count, HD)
    stretch_state = jnp.einsum('crhd,crhe->chde', lifted_k, value_rows)
    running = jnp.cumsum(stretch_state, axis=0)
    prior_state = jnp.concatenate([jnp.zeros_like(stretch_state[:1]), running[:-1]], axis=0)
    whole_state = (prior_state + stretch_state).astype(jnp.bfloat16)
    whole_state = lax.optimization_barrier(whole_state).astype(jnp.float32)
    raw_mix = jnp.einsum('crhd,chde->crhe', lifted_q, whole_state).reshape(TOKENS, D)
    mean_square = lax.optimization_barrier(jnp.mean(raw_mix * raw_mix, axis=-1, keepdims=True))
    self_mixed = (raw_mix * lax.rsqrt(mean_square + 1e-05) * out_gain[None, :]).astype(jnp.bfloat16)
    caption_k = caption_keys.astype(jnp.float32).reshape(GL, head_count, HD)
    caption_v = caption_values.astype(jnp.float32).reshape(GL, head_count, HD)
    stretch_queries = cross_queries.reshape(STRETCHES, TOK_DEV, head_count, HD)
    score_scale = HD ** (-0.5)

    def one_stretch(packed):
        stretch_id, query_rows = packed
        query_rows = query_rows.astype(jnp.float32)
        owners = stretch_id - jnp.arange(SPAN, dtype=jnp.int32)

        def pick(owner_id):
            first_row = jnp.maximum(owner_id, 0).astype(jnp.int32) * PR_DEV
            picked_k = lax.dynamic_slice_in_dim(prompt_keys, first_row, PR_DEV, 0)
            picked_v = lax.dynamic_slice_in_dim(prompt_values, first_row, PR_DEV, 0)
            tile_mask = prompt_tiles(owner_id, stretch_id, span_start, span_end, prompt_tokens, region_mask)
            return (picked_k, picked_v, tile_mask)
        picked_k, picked_v, tile_masks = jax.vmap(pick)(owners)
        window = SPAN * PR_DEV * PL
        all_keys = jnp.concatenate([caption_k, picked_k.astype(jnp.float32).reshape(window, head_count, HD)], axis=0)
        all_values = jnp.concatenate([caption_v, picked_v.astype(jnp.float32).reshape(window, head_count, HD)], axis=0)
        tile_all = jnp.concatenate([jnp.ones((TILES, GL), dtype=bool), jnp.transpose(tile_masks, (1, 0, 2)).reshape(TILES, window)], axis=1)
        visible = per_token(tile_all, TOK_DEV)
        scores = jnp.einsum('rhd,khd->hrk', query_rows, all_keys) * score_scale
        scores = jnp.where(visible[None], scores, -1e+30)
        peak = lax.optimization_barrier(jnp.max(scores, axis=2))
        expo = jnp.where(visible[None], jnp.exp(scores - peak[:, :, None]), 0.0)
        denom = lax.optimization_barrier(jnp.sum(expo, axis=2))
        weights = lax.optimization_barrier(expo.astype(jnp.bfloat16)).astype(jnp.float32)
        summed = jnp.einsum('hrk,khd->rhd', weights, all_values)
        mixed_rows = summed / jnp.transpose(denom)[:, :, None]
        return mixed_rows.reshape(TOK_DEV, D).astype(jnp.bfloat16)
    cross_mixed = lax.map(one_stretch, (jnp.arange(STRETCHES, dtype=jnp.int32), stretch_queries))
    return (self_mixed, cross_mixed.reshape(TOKENS, D))
```

```python
import functools
import math

import jax
import jax.numpy as jnp
from jax import lax
from jax.experimental import pallas as pl
from jax.experimental.pallas import tpu as pltpu
from jax.sharding import PartitionSpec as P

HD = 32
SPAN = 6
QUAD = 128
LAYER = 4
BF = jnp.bfloat16
F32 = jnp.float32
EMPTY = -1e30
STEP = 3


def vmem():
    return pl.BlockSpec(memory_space=pltpu.VMEM)


def smem():
    return pl.BlockSpec(memory_space=pltpu.SMEM)


def anywhere():
    return pl.BlockSpec(memory_space=pl.ANY)


def cost(flops, moved, exps=0):
    return pl.CostEstimate(flops=flops, bytes_accessed=moved, transcendentals=exps)


def quad_rows(ref, q, width):
    if (q + 1) * QUAD <= width:
        return ref[q * QUAD : (q + 1) * QUAD, :]
    part = ref[q * QUAD : width, :]
    fill = jnp.zeros(((q + 1) * QUAD - width, part.shape[1]), part.dtype)
    return jnp.concatenate([part, fill], axis=0)


def turn_kernel(width, count_ref, *refs):
    half = len(refs) // 2
    rows = lax.broadcasted_iota(jnp.int32, (QUAD, QUAD), 0)
    for place in range(half):
        keys_ref, out_ref = refs[place], refs[half + place]
        used = count_ref[place]
        for q in range(out_ref.shape[0]):
            turned = jnp.transpose(quad_rows(keys_ref, q, width).astype(F32))
            turned = jnp.where(rows < used, turned, turned[0:1, :])
            out_ref[q] = turned.astype(BF)


def turn_keys(counts, *blocks):
    width, slots = blocks[0].shape
    quads = -(-width // QUAD)
    return pl.pallas_call(
        functools.partial(turn_kernel, width),
        in_specs=[smem()] + [vmem()] * len(blocks),
        out_specs=[vmem()] * len(blocks),
        out_shape=[jax.ShapeDtypeStruct((quads, slots, QUAD), BF)] * len(blocks),
        cost_estimate=cost(0, 4 * len(blocks) * width * slots),
        compiler_params=pltpu.CompilerParams(vmem_limit_bytes=16 << 20),
        name="turn_keys",
    )(counts, *blocks)


def attend_kernel(setup, meta_ref, query_ref, *refs):
    count, first, last, held, prompts, width, tokens, tiles = setup
    tile = tokens // tiles
    quads = -(-width // QUAD)
    rounds = quads // STEP
    key_hbm, value_hbm = refs[:count], refs[count : 2 * count]
    refs = refs[2 * count :]
    if not first:
        peak_in, denom_in, total_in = refs[:3]
        refs = refs[3:]
    if last:
        out_ref = refs[0]
        refs = refs[1:]
    else:
        peak_out, denom_out, total_out = refs[:3]
        refs = refs[3:]
    (keys, vals, marks, spread, peak, denom, total, s_a, s_b, p_a, p_b, f_a, f_b, work, used, sems) = refs
    scale = math.log2(math.e) / math.sqrt(HD)
    stretch = meta_ref[0]

    found = jnp.int32(0)
    wanted = []
    for b, owner in enumerate(held(stretch)):
        if owner is None:
            any_seen = jnp.bool_(True)
            used[b] = jnp.int32(QUAD)
            for i in range(tiles):
                work[found] = jnp.int32(b * tiles + i)
                found = found + 1
        else:
            safe = jnp.clip(owner, 0, prompts - 1)
            covers = (
                (owner >= 0)
                & (meta_ref[1 + safe] <= stretch)
                & (stretch < meta_ref[1 + prompts + safe])
            )
            used[b] = meta_ref[1 + 2 * prompts + safe]
            any_seen = jnp.bool_(False)
            for i in range(tiles):
                seen = covers & (meta_ref[1 + (3 + i) * prompts + safe] == 1)
                work[found] = jnp.int32(b * tiles + i)
                found = found + seen.astype(jnp.int32)
                any_seen = any_seen | seen
        wanted.append(any_seen)

        @pl.when(any_seen)
        def _():
            pltpu.make_async_copy(key_hbm[b], keys.at[b], sems.at[2 * b]).start()
            pltpu.make_async_copy(value_hbm[b], vals.at[b, pl.ds(0, width)], sems.at[2 * b + 1]).start()

    zero = jnp.zeros((HD, tile), BF)
    for q in range(quads):
        rows = quad_rows(query_ref, q, width)
        for i in range(tiles):
            part = rows[:, i * tile : (i + 1) * tile]
            for h in range(QUAD // HD):
                piece = part[h * HD : (h + 1) * HD]
                pair = [piece, zero] if h % 2 == 0 else [zero, piece]
                spread[i, q, h * HD : (h + 1) * HD, :] = jnp.concatenate(pair, axis=1)
    if first:
        peak[...] = jnp.full(peak.shape, EMPTY, F32)
        denom[...] = jnp.zeros(denom.shape, F32)
        total[...] = jnp.zeros(total.shape, F32)
    else:
        peak[...] = peak_in[...]
        denom[...] = denom_in[...]
        total[...] = total_in[...]

    lanes = lax.broadcasted_iota(jnp.int32, (16, QUAD), 1)
    for b in range(count):

        @pl.when(wanted[b])
        def _():
            marks[b] = jnp.where(lanes < used[b], 1.0, 0.0).astype(BF)
            pltpu.make_async_copy(key_hbm[b], keys.at[b], sems.at[2 * b]).wait()
            pltpu.make_async_copy(value_hbm[b], vals.at[b, pl.ds(0, width)], sems.at[2 * b + 1]).wait()
            if width < quads * QUAD:
                vals[b, width:, :] = jnp.zeros((quads * QUAD - width, QUAD), BF)

    items = found * rounds
    low_half = lax.broadcasted_iota(jnp.int32, (QUAD, QUAD), 1) < QUAD // 2
    row16 = lax.broadcasted_iota(jnp.int32, (16, QUAD), 0)

    def item(t):
        t = jnp.minimum(t, items - 1)
        j = t // rounds
        g = t - j * rounds
        e = work[j]
        b = e // tiles
        return b, e - b * tiles, g * STEP

    def score(t, s_to):
        b, i, q0 = item(t)
        for k in range(STEP):
            block = keys[b, q0 + k].astype(F32)
            both = jnp.concatenate(
                [jnp.where(low_half, block, 0.0), jnp.where(low_half, 0.0, block)], axis=0
            ).astype(BF)
            s_to[k] = jnp.dot(both, spread[i, q0 + k], preferred_element_type=F32)

    def weigh(t, s_from, p_to, f_to):
        _, i, q0 = item(t)
        olds = [peak[i, q0 + k] for k in range(STEP)]
        for k in range(STEP):
            news = []
            for pair in range(2):
                part = s_from[k, pair * QUAD : (pair + 1) * QUAD, :]
                old = olds[k][pair : pair + 1]
                new = jnp.maximum(old, jnp.max(part, axis=0, keepdims=True))
                p_to[k, pair * QUAD : (pair + 1) * QUAD, :] = jnp.exp2((part - new) * scale).astype(BF)
                news.append(new)
            new = jnp.concatenate(news, axis=0)
            f_to[k] = jnp.exp2((olds[k] - new) * scale)
            peak[i, q0 + k] = new

    def mix(t, p_from, f_from):
        b, i, q0 = item(t)
        mark = marks[b]
        many = jnp.concatenate([mark] * (QUAD // 16), axis=0)
        none = jnp.zeros((QUAD // 2, QUAD), BF)
        mark_f = mark.astype(F32)
        ones = jnp.concatenate(
            [jnp.where(row16 == 0, mark_f, 0.0), jnp.where(row16 == 1, mark_f, 0.0)], axis=1
        ).astype(BF)
        sums = [total[i, q0 + k] for k in range(STEP)]
        dens = [denom[i, q0 + k] for k in range(STEP)]
        facs = [f_from[k] for k in range(STEP)]
        for k in range(STEP):
            v = vals[b, pl.ds(pl.multiple_of((q0 + k) * QUAD, QUAD), QUAD), :] * many
            left = jnp.concatenate(
                [
                    jnp.concatenate([v[: QUAD // 2], none], axis=1),
                    jnp.concatenate([none, v[QUAD // 2 :]], axis=1),
                    ones,
                ],
                axis=0,
            )
            out = jnp.dot(left, p_from[k], preferred_element_type=F32)
            denom[i, q0 + k] = dens[k] * facs[k] + out[QUAD : QUAD + 2]
            for pair in range(2):
                r = pair * 2 * HD
                added = jnp.concatenate([out[r : r + HD, :tile], out[r + HD : r + 2 * HD, tile:]], axis=1)
                at = slice(pair * HD, (pair + 1) * HD)
                total[i, q0 + k, at, :] = sums[k][at] * facs[k][pair : pair + 1] + added

    def turn(t, s_to, s_from, p_to, f_to, p_from, f_from):
        mix(t, p_from, f_from)
        weigh(t + 1, s_from, p_to, f_to)
        score(t + 2, s_to)

    @pl.when(items > 0)
    def _():
        score(0, s_a)
        weigh(0, s_a, p_a, f_a)
        score(1, s_b)

        def body(k, carry):
            t = 2 * k
            turn(t, s_a, s_b, p_b, f_b, p_a, f_a)

            @pl.when(t + 1 < items)
            def _():
                turn(t + 1, s_b, s_a, p_a, f_a, p_b, f_b)

            return carry

        lax.fori_loop(0, (items + 1) // 2, body, 0)

    if not last:
        peak_out[...] = peak[...]
        denom_out[...] = denom[...]
        total_out[...] = total[...]
        return
    for q in range(quads):
        for i in range(tiles):
            for pair in range(2):
                mixed = total[i, q, pair * HD : (pair + 1) * HD, :] / denom[i, q, pair : pair + 1, :]
                for side in range(2):
                    r = q * QUAD + (2 * pair + side) * HD
                    if r < width:
                        out_ref[r : r + HD, i * tile : (i + 1) * tile] = mixed[
                            :, side * tile : (side + 1) * tile
                        ].astype(BF)


def attend(meta, queries, blocks, held, state, last, tiles, prompts):
    width, tokens = queries.shape
    tile = tokens // tiles
    quads = -(-width // QUAD)
    count = len(blocks)
    setup = (count, state is None, last, held, prompts, width, tokens, tiles)
    shapes = [
        jax.ShapeDtypeStruct((tiles, quads, 2, 2 * tile), F32),
        jax.ShapeDtypeStruct((tiles, quads, 2, 2 * tile), F32),
        jax.ShapeDtypeStruct((tiles, quads, 2 * HD, 2 * tile), F32),
    ]
    outs = [jax.ShapeDtypeStruct((width, tokens), BF)] if last else shapes
    states = [] if state is None else list(state)
    hold = lambda s, t: pltpu.VMEM(s, t)
    scratch = [
        hold((count, quads, QUAD, QUAD), BF),
        hold((count, quads * QUAD, QUAD), BF),
        hold((count, 16, QUAD), BF),
        hold((tiles, quads, QUAD, 2 * tile), BF),
        hold(shapes[0].shape, F32),
        hold(shapes[1].shape, F32),
        hold(shapes[2].shape, F32),
    ]
    scratch += [hold((STEP, 2 * QUAD, 2 * tile), F32)] * 2
    scratch += [hold((STEP, 2 * QUAD, 2 * tile), BF)] * 2
    scratch += [hold((STEP, 2, 2 * tile), F32)] * 2
    scratch += [
        pltpu.SMEM((count * tiles + 1,), jnp.int32),
        pltpu.SMEM((count,), jnp.int32),
        pltpu.SemaphoreType.DMA((2 * count,)),
    ]
    area = count * QUAD * tokens
    return pl.pallas_call(
        functools.partial(attend_kernel, setup),
        in_specs=[smem(), vmem()] + [anywhere()] * (2 * count) + [vmem()] * len(states),
        out_specs=[vmem()] * len(outs),
        out_shape=outs,
        scratch_shapes=scratch,
        cost_estimate=cost(4 * area * width, 4 * width * tokens, area * width // HD),
        compiler_params=pltpu.CompilerParams(vmem_limit_bytes=48 << 20),
        name="attend",
    )(meta, queries, *[b[0] for b in blocks], *[b[1] for b in blocks], *states)


def state_kernel(width, keys_ref, values_ref, out_ref, sent_ref):
    rows = lax.broadcasted_iota(jnp.int32, (QUAD, QUAD), 0) // HD
    columns = lax.broadcasted_iota(jnp.int32, (QUAD, QUAD), 1) // HD
    for q in range(out_ref.shape[0]):
        lifted = jnp.maximum(quad_rows(keys_ref, q, width), 0)
        grown = lax.dot_general(
            quad_rows(values_ref, q, width), lifted, (((1,), (1,)), ((), ())), preferred_element_type=F32
        )
        grown = jnp.where(rows == columns, grown, 0.0)
        folded = grown[0:HD] + grown[HD : 2 * HD] + grown[2 * HD : 3 * HD] + grown[3 * HD :]
        out_ref[q] = folded
        sent_ref[q] = folded.astype(BF)


def stretch_states(keys, values):
    width, tokens = keys.shape
    quads = -(-width // QUAD)
    shape = (quads, HD, QUAD)
    return pl.pallas_call(
        functools.partial(state_kernel, width),
        in_specs=[vmem()] * 2,
        out_specs=[vmem()] * 2,
        out_shape=[jax.ShapeDtypeStruct(shape, F32), jax.ShapeDtypeStruct(shape, BF)],
        cost_estimate=cost(2 * width * QUAD * tokens, 4 * width * tokens),
        compiler_params=pltpu.CompilerParams(vmem_limit_bytes=16 << 20),
        name="stretch_states",
    )(keys, values)


def norm_kernel(width, queries_ref, prior_ref, own_ref, gain_ref, out_ref, raw):
    rows = lax.broadcasted_iota(jnp.int32, (QUAD, QUAD), 0) // HD
    columns = lax.broadcasted_iota(jnp.int32, (QUAD, QUAD), 1) // HD
    quads, tokens = raw.shape[0], raw.shape[2]
    squares = jnp.zeros((1, tokens), F32)
    for q in range(quads):
        whole = (prior_ref[q] + own_ref[q]).astype(BF).astype(F32)
        wide = jnp.where(rows == columns, jnp.concatenate([whole] * (QUAD // HD), axis=0), 0.0).astype(BF)
        lifted = jnp.maximum(quad_rows(queries_ref, q, width), 0)
        part = jnp.dot(wide, lifted, preferred_element_type=F32)
        raw[q] = part
        squares = squares + jnp.sum(part * part, axis=0, keepdims=True)
    factor = lax.rsqrt(squares / width + 1e-05)
    for q in range(quads):
        size = min(QUAD, width - q * QUAD)
        gains = jnp.transpose(jnp.broadcast_to(gain_ref[q : q + 1, :], (QUAD, QUAD)))
        gains = jnp.concatenate([gains] * (tokens // QUAD), axis=1)
        mixed = (raw[q] * factor * gains).astype(BF)
        out_ref[q * QUAD : q * QUAD + size, :] = mixed[:size]


def self_mix(queries, prior, own, gain):
    width, tokens = queries.shape
    quads = -(-width // QUAD)
    return pl.pallas_call(
        functools.partial(norm_kernel, width),
        in_specs=[vmem()] * 4,
        out_specs=vmem(),
        out_shape=jax.ShapeDtypeStruct((width, tokens), BF),
        scratch_shapes=[pltpu.VMEM((quads, QUAD, tokens), F32)],
        cost_estimate=cost(2 * width * QUAD * tokens, 4 * width * tokens),
        compiler_params=pltpu.CompilerParams(vmem_limit_bytes=24 << 20),
        name="self_mix",
    )(queries, prior, own, jnp.pad(gain, (0, quads * QUAD - width)).reshape(quads, QUAD))


def sent(block, pairs):
    return lax.ppermute(block, "tm", pairs)


def prior_states(own, first_sent):
    size = lax.axis_size("tm")
    place = lax.axis_index("tm")
    prior = jnp.zeros_like(own)
    whole = own
    outgoing = first_sent
    hop = 1
    while hop < size:
        other = sent(outgoing, [(i, i ^ hop) for i in range(size)]).astype(F32)
        prior = prior + jnp.where((place & hop) != 0, other, 0.0)
        whole = whole + other
        outgoing = whole.astype(BF)
        hop *= 2
    return prior


def local(
    queries,
    keys,
    values,
    cross_queries,
    prompt_keys,
    prompt_values,
    caption_keys,
    caption_values,
    span_start,
    span_end,
    prompt_tokens,
    region_mask,
    out_gain,
):
    size = lax.axis_size("tm")
    place = lax.axis_index("tm").astype(jnp.int32)
    tiles = region_mask.shape[1]
    prompts = span_start.shape[0]
    meta = jnp.concatenate(
        [place[None], span_start, span_end, prompt_tokens, jnp.transpose(region_mask).reshape(-1)]
    )
    count_own = lax.dynamic_slice_in_dim(prompt_tokens, place, 1, 0)
    counts = jnp.concatenate([count_own, jnp.full((1,), QUAD, jnp.int32)])
    slots, width = prompt_keys.shape[1:]
    own_v = jnp.transpose(prompt_values.reshape(slots, width))
    own_k, caption_k = turn_keys(
        counts, jnp.transpose(prompt_keys.reshape(slots, width)), jnp.transpose(caption_keys)
    )
    caption_v = jnp.transpose(caption_values)

    layers = size // LAYER
    beside = [(i, i ^ 1) for i in range(size)]
    up = [(i, (i + LAYER) % size) for i in range(size)]
    across = [(LAYER * z + i, LAYER * z + i + 2) for z in range(layers) for i in (0, 1)]
    back = [(LAYER * z + i, LAYER * z + j) for z in range(layers) for i, j in ((2, 0), (3, 1), (1, 3))]
    onward = [(LAYER * z + 1, LAYER * z + 4) for z in range(layers - 1)]

    def both(block, pairs):
        v = sent(block[1], pairs)
        k = sent(block[0], pairs)
        return (k, v)

    own = (own_k, own_v)
    a = both(own, up)
    y = both(own, across)
    b = both(own, beside)
    ay = both(a, back)
    ax = both(a, beside)
    yx = both(y, beside)
    ayx = both(ay, beside)
    r5 = both(ay, onward)

    queries_t = jnp.transpose(cross_queries)
    spot = lambda c: c % LAYER
    held1 = lambda c: [None, c, jnp.where(c % 2 == 1, c - 1, -1)]
    held2 = lambda c: [
        jnp.where(spot(c) >= 2, c - 2, -1),
        jnp.where(spot(c) == 2, c - 1, jnp.where(spot(c) == 3, c - 3, -1)),
        c - LAYER,
        jnp.where(c >= LAYER, jnp.where(c % 2 == 0, c - 3, c - 5), -1),
    ]
    held3 = lambda c: [
        jnp.where(spot(c) < 2, c - 2, -1),
        jnp.where(
            spot(c) == 0, c - 1, jnp.where(spot(c) == 1, c - 3, jnp.where(spot(c) == 2, c - 5, -1))
        ),
        jnp.where(spot(c) == 0, c - 5, -1),
    ]
    call = functools.partial(attend, meta, queries_t, tiles=tiles, prompts=prompts)
    state = call([(caption_k, caption_v), own, b], held1, None, False)
    state = call([y, yx, a, ax], held2, state, False)
    cross_mixed = call([ay, ayx, r5], held3, state, True)[0]

    own_state, own_sent = stretch_states(jnp.transpose(keys), jnp.transpose(values))
    prior = prior_states(own_state, own_sent)
    self_mixed = self_mix(jnp.transpose(queries), prior, own_state, out_gain)
    return (jnp.transpose(self_mixed), jnp.transpose(cross_mixed))


def solution(mesh):
    in_specs = (
        P(("groups", "tm"), None),
        P(("groups", "tm"), None),
        P(("groups", "tm"), None),
        P(("groups", "tm"), None),
        P(("groups", "tm"), None, None),
        P(("groups", "tm"), None, None),
        P("groups", None),
        P("groups", None),
        P("groups"),
        P("groups"),
        P("groups"),
        P("groups", None),
        P(),
    )
    out_specs = (P(("groups", "tm"), None), P(("groups", "tm"), None))
    return jax.shard_map(local, mesh=mesh, in_specs=in_specs, out_specs=out_specs, check_vma=False)
```

```python
import functools
import math

import jax
import jax.numpy as jnp
from jax import lax
from jax.experimental import pallas as pl
from jax.experimental.pallas import tpu as pltpu
from jax.sharding import PartitionSpec as P

HD = 32
SPAN = 6
QUAD = 128
LAYER = 4
BF = jnp.bfloat16
F32 = jnp.float32
EMPTY = -1e30
STEP = 3
PARTS = 3
COPIES = 2
ROOM = 66_400_000


def vmem():
    return pl.BlockSpec(memory_space=pltpu.VMEM)


def smem():
    return pl.BlockSpec(memory_space=pltpu.SMEM)


def anywhere():
    return pl.BlockSpec(memory_space=pl.ANY)


def cost(flops, moved, exps=0):
    flops, moved = flops // 1000, moved // 1000
    return pl.CostEstimate(flops=flops, bytes_accessed=moved, transcendentals=exps)


def quad_rows(ref, q, width):
    if (q + 1) * QUAD <= width:
        return ref[q * QUAD : (q + 1) * QUAD, :]
    part = ref[q * QUAD : width, :]
    fill = jnp.zeros(((q + 1) * QUAD - width, part.shape[1]), part.dtype)
    return jnp.concatenate([part, fill], axis=0)


def part_rows(width, quads, part):
    low = part * (quads // PARTS) * QUAD
    return pl.ds(low, min(quads // PARTS * QUAD, width - low))


def turned_quad(keys, used, rows):
    turned = jnp.transpose(keys.astype(F32))
    return jnp.where(rows < used, turned, turned[0:1, :]).astype(BF)


def turn_kernel(tokens_ref, keys_hbm, out_hbm, keys, out, in_sems, out_sems):
    used = tokens_ref[lax.axis_index("tm")]
    width, quads = keys.shape[0], out.shape[0]
    every = quads // PARTS
    rows = lax.broadcasted_iota(jnp.int32, (QUAD, QUAD), 0)

    def move_in(part):
        at = part_rows(width, quads, part)
        return pltpu.make_async_copy(keys_hbm.at[at], keys.at[at], in_sems.at[part])

    def move_out(part):
        at = pl.ds(part * every, every)
        return pltpu.make_async_copy(out.at[at], out_hbm.at[at], out_sems.at[part])

    for part in range(PARTS):
        move_in(part).start()
    for q in range(quads):
        if q % every == 0:
            move_in(q // every).wait()
        out[q] = turned_quad(quad_rows(keys, q, width), used, rows)
        if q % every == every - 1:
            move_out(q // every).start()
    for part in range(PARTS):
        move_out(part).wait()


def turned_keys(tokens, keys):
    width, slots = keys.shape
    shape = (-(-width // QUAD), slots, QUAD)
    return pl.pallas_call(
        turn_kernel,
        in_specs=[smem(), anywhere()],
        out_specs=anywhere(),
        out_shape=jax.ShapeDtypeStruct(shape, BF),
        scratch_shapes=[
            pltpu.VMEM((width, slots), BF),
            pltpu.VMEM(shape, BF),
            pltpu.SemaphoreType.DMA((PARTS,)),
            pltpu.SemaphoreType.DMA((PARTS,)),
        ],
        cost_estimate=cost(0, 4 * width * slots),
        compiler_params=pltpu.CompilerParams(vmem_limit_bytes=ROOM),
        name="turned_keys",
    )(tokens, keys)


def no_kernel(*refs):
    del refs


def after(blocks, *tokens):
    return pl.pallas_call(
        no_kernel,
        in_specs=[anywhere()] * (len(blocks) + len(tokens)),
        out_specs=[anywhere()] * len(blocks),
        out_shape=[jax.ShapeDtypeStruct(block.shape, block.dtype) for block in blocks],
        input_output_aliases={place: place for place in range(len(blocks))},
        cost_estimate=cost(0, 0),
        name="after",
    )(*blocks, *tokens)


def across_kernel(waits, own_hbm, up_hbm, *refs):
    *refs, held, in_sems, out_sems = refs[waits:]
    summed = len(refs) > 2
    if summed:
        *states, across_hbm, _, sent_out = refs
    else:
        across_hbm, _ = refs
    lower = lax.axis_index("tm") % LAYER < LAYER // 2
    piece = own_hbm.shape[0] // COPIES

    def move_in(source, part):
        at = pl.ds(part * piece, piece)
        return pltpu.make_async_copy(source.at[at], held.at[at], in_sems.at[part])

    def move_out(part):
        at = pl.ds(part * piece, piece)
        return pltpu.make_async_copy(held.at[at], across_hbm.at[at], out_sems.at[part])

    @pl.when(lower)
    def _():
        for part in range(COPIES):
            move_in(own_hbm, part).start()

    @pl.when(jnp.logical_not(lower))
    def _():
        for part in range(COPIES):
            move_in(up_hbm, part).start()

    if summed:
        digit_step(states[0], states[1:], sent_out)
    for part in range(COPIES):
        move_in(up_hbm, part).wait()
        move_out(part).start()
    for part in range(COPIES):
        move_out(part).wait()


def to_cross(own, up, *tokens, states=()):
    shape = jax.ShapeDtypeStruct(own.shape, own.dtype)
    outs, out_specs = [shape, shape], [anywhere()] * 2
    if states:
        outs.append(jax.ShapeDtypeStruct(states[0].shape, BF))
        out_specs.append(vmem())
    return pl.pallas_call(
        functools.partial(across_kernel, len(tokens)),
        in_specs=[anywhere()] * (2 + len(tokens)) + [vmem()] * len(states),
        out_specs=out_specs,
        out_shape=outs,
        input_output_aliases={1: 1},
        scratch_shapes=[
            pltpu.VMEM(own.shape, own.dtype),
            pltpu.SemaphoreType.DMA((COPIES,)),
            pltpu.SemaphoreType.DMA((COPIES,)),
        ],
        cost_estimate=cost(0, 4 * own.size),
        compiler_params=pltpu.CompilerParams(vmem_limit_bytes=ROOM),
        name="to_cross",
    )(own, up, *tokens, *states)


def attend_kernel(setup, start_ref, end_ref, tokens_ref, region_ref, *refs):
    count, first, last, held, waits, prompts, width, tokens, tiles = setup
    tile = tokens // tiles
    quads = -(-width // QUAD)
    rounds = quads // STEP
    every = quads // PARTS
    query_refs, refs = refs[:PARTS], refs[PARTS:]
    if first:
        raw_keys, refs = refs[0], refs[1:]
    key_hbm = [None] * first + list(refs[: count - first])
    refs = refs[count - first :]
    value_hbm, refs = refs[:count], refs[count + waits :]
    if not first:
        level_in, total_in = refs[0], refs[1 : 1 + PARTS]
        refs = refs[1 + PARTS :]
    if last:
        out_ref, refs = refs[0], refs[1:]
    else:
        level_out, total_out = refs[0], refs[1 : 1 + PARTS]
        refs = refs[1 + PARTS :]
    keys, vals, marks, spread, level, total, s_a, s_b, p_a, p_b, f_a, f_b, work, found, used, ready, sems = refs
    scale = math.log2(math.e) / math.sqrt(HD)
    none = jnp.zeros((HD, tile), BF)
    i = pl.program_id(0)

    def copies(b):
        moves = [pltpu.make_async_copy(value_hbm[b], vals.at[b, pl.ds(0, width)], sems.at[b, 1])]
        if key_hbm[b] is not None:
            moves.append(pltpu.make_async_copy(key_hbm[b], keys.at[b], sems.at[b, 0]))
        return moves

    @pl.when(i == 0)
    def _():
        stretch = lax.axis_index("tm")
        wanted = []
        lengths = [jnp.int32(0)] * tiles
        for b, owner in enumerate(held(stretch)):
            if owner is None:
                seen = [jnp.int32(1)] * tiles
                used[b] = jnp.int32(QUAD)
            else:
                safe = jnp.clip(owner, 0, prompts - 1)
                covers = (
                    (owner >= 0)
                    & (start_ref[safe] <= stretch)
                    & (stretch < end_ref[safe])
                )
                used[b] = tokens_ref[safe]
                seen = [
                    (covers & (region_ref[t, safe] == 1)).astype(jnp.int32)
                    for t in range(tiles)
                ]
            for t in range(tiles):
                work[t * count + lengths[t]] = jnp.int32(b)
                lengths[t] = lengths[t] + seen[t]
            wanted.append(functools.reduce(jnp.add, seen) > 0)
            ready[b] = jnp.int32(0)

            @pl.when(wanted[b])
            def _():
                for move in copies(b):
                    move.start()

        for t in range(tiles):
            found[t] = lengths[t]
        for q in range(quads):
            for h in range(QUAD // HD):
                off = (1 - h % 2) * tile
                spread[q, h * HD : (h + 1) * HD, off : off + tile] = none
        lanes = lax.broadcasted_iota(jnp.int32, (16, QUAD), 1)
        rows = lax.broadcasted_iota(jnp.int32, (QUAD, QUAD), 0)
        for b in range(count):
            marks[b] = jnp.where(lanes < used[b], 1.0, 0.0).astype(BF)
            if width < quads * QUAD:
                vals[b, width:, :] = jnp.zeros((quads * QUAD - width, QUAD), BF)
            if key_hbm[b] is None:
                for q in range(quads):
                    keys[b, q] = turned_quad(quad_rows(raw_keys, q, width), QUAD, rows)

    def arrived(b):
        @pl.when(ready[b] == 0)
        def _():
            pltpu.make_async_copy(value_hbm[-1], vals.at[b, pl.ds(0, width)], sems.at[b, 1]).wait()
            ready[b] = jnp.int32(1)
            if key_hbm[-1] is None:
                return

            @pl.when(b >= first)
            def _():
                pltpu.make_async_copy(key_hbm[-1], keys.at[b], sems.at[b, 0]).wait()

    low_half = lax.broadcasted_iota(jnp.int32, (QUAD, QUAD), 1) < QUAD // 2
    row16 = lax.broadcasted_iota(jnp.int32, (16, QUAD), 0)
    zeros = jnp.zeros((QUAD // 2, QUAD), BF)

    def score(b, g, s_to):
        for k in range(STEP):
            block = keys[b, g * STEP + k].astype(F32)
            both = jnp.concatenate(
                [jnp.where(low_half, block, 0.0), jnp.where(low_half, 0.0, block)], axis=0
            ).astype(BF)
            s_to[k] = jnp.dot(both, spread[g * STEP + k], preferred_element_type=F32)

    def weigh(g, s_from, p_to, f_to):
        for k in range(STEP):
            q = g * STEP + k
            for pair in range(2):
                at = slice(pair * QUAD, (pair + 1) * QUAD)
                part = s_from[k, at, :]
                old = level[q, pair : pair + 1]
                new = jnp.maximum(old, jnp.max(part, axis=0, keepdims=True))
                p_to[k, at, :] = jnp.exp2((part - new) * scale).astype(BF)
                f_to[k, pair : pair + 1] = jnp.exp2((old - new) * scale)
                level[q, pair : pair + 1] = new

    def mix(b, many, ones, g, p_from, f_from):
        for k in range(STEP):
            q = g * STEP + k
            v = vals[b, q * QUAD : (q + 1) * QUAD, :] * many
            left = jnp.concatenate(
                [
                    jnp.concatenate([v[: QUAD // 2], zeros], axis=1),
                    jnp.concatenate([zeros, v[QUAD // 2 :]], axis=1),
                    ones,
                ],
                axis=0,
            )
            out = jnp.dot(left, p_from[k], preferred_element_type=F32)
            factor = f_from[k]
            level[q, 2:4] = level[q, 2:4] * factor + out[QUAD : QUAD + 2]
            for pair in range(2):
                r = pair * 2 * HD
                added = jnp.concatenate([out[r : r + HD, :tile], out[r + HD : r + 2 * HD, tile:]], axis=1)
                at = slice(pair * HD, (pair + 1) * HD)
                total[q, at, :] = total[q, at, :] * factor[pair : pair + 1] + added

    slots = [(s_a, p_a, f_a), (s_b, p_b, f_b)]
    n = found[i]
    if first:
        level[:, 0:2] = jnp.full((quads, 2, 2 * tile), EMPTY, F32)
        level[:, 2:4] = jnp.zeros((quads, 2, 2 * tile), F32)
        total[...] = jnp.zeros(total.shape, F32)
    else:
        level[...] = level_in[0]
        for part in range(PARTS):
            total[part * every : (part + 1) * every] = total_in[part][0]

    @pl.when(n > 0)
    def _():
        for r in range(0, quads * QUAD, HD):
            q, h = r // QUAD, r % QUAD // HD
            on = h % 2 * tile
            low = q // every * every * QUAD
            piece = query_refs[q // every][r - low : r - low + HD, :] if r < width else none
            spread[q, h * HD : (h + 1) * HD, on : on + tile] = piece
        b0 = work[i * count]
        arrived(b0)
        score(b0, 0, s_a)
        weigh(0, s_a, p_a, f_a)
        score(b0, 1, s_b)

        def entry(j, carry):
            b = work[i * count + j]
            later = work[i * count + jnp.minimum(j + 1, n - 1)]
            arrived(later)
            mark = marks[b]
            many = jnp.concatenate([mark] * (QUAD // 16), axis=0)
            mark = mark.astype(F32)
            ones = jnp.concatenate(
                [jnp.where(row16 == 0, mark, 0.0), jnp.where(row16 == 1, mark, 0.0)], axis=1
            ).astype(BF)
            for g in range(rounds):
                here, there = slots[g % 2], slots[(g + 1) % 2]
                score(b if g + 2 < rounds else later, (g + 2) % rounds, here[0])
                mix(b, many, ones, g, here[1], here[2])
                weigh((g + 1) % rounds, there[0], there[1], there[2])
            return carry

        lax.fori_loop(0, n, entry, 0)

    if last:
        for q in range(quads):
            scaled = 1.0 / level[q, 2:4]
            for pair in range(2):
                mixed = total[q, pair * HD : (pair + 1) * HD, :] * scaled[pair : pair + 1]
                for side in range(2):
                    r = q * QUAD + (2 * pair + side) * HD
                    if r < width:
                        out_ref[r : r + HD, :] = mixed[:, side * tile : (side + 1) * tile].astype(BF)
    else:
        level_out[0] = level[...]
        for part in range(PARTS):
            total_out[part][0] = total[part * every : (part + 1) * every]


def attend(spans, queries, blocks, held, state, last, waits=()):
    width, tokens = queries.shape
    quads = -(-width // QUAD)
    every = quads // PARTS
    count = len(blocks)
    tiles, prompts = spans[3].shape
    tile = tokens // tiles
    first = state is None
    setup = (count, int(first), last, held, len(waits), prompts, width, tokens, tiles)
    levels, totals = (quads, 4, 2 * tile), (every, 2 * HD, 2 * tile)
    state_shapes = [(tiles,) + shape for shape in (levels,) + (totals,) * PARTS]
    state_specs = [pl.BlockSpec((1,) + shape[1:], lambda i: (i, 0, 0, 0)) for shape in state_shapes]
    query_specs = [pl.BlockSpec((every * QUAD, tile), lambda i, p=p: (p, i)) for p in range(PARTS)]
    if last:
        outs = [jax.ShapeDtypeStruct((width, tokens), BF)]
        out_specs = [pl.BlockSpec((width, tile), lambda i: (0, i))]
    else:
        outs = [jax.ShapeDtypeStruct(shape, F32) for shape in state_shapes]
        out_specs = list(state_specs)
    raw = [blocks[0][0]] if first else []
    keys = [block[0] for block in blocks[int(first) :]]
    values = [block[1] for block in blocks]
    scratch = [
        pltpu.VMEM((count, quads, QUAD, QUAD), BF),
        pltpu.VMEM((count, quads * QUAD, QUAD), BF),
        pltpu.VMEM((count, 16, QUAD), BF),
        pltpu.VMEM((quads, QUAD, 2 * tile), BF),
        pltpu.VMEM(levels, F32),
        pltpu.VMEM((quads, 2 * HD, 2 * tile), F32),
    ]
    scratch += [pltpu.VMEM((STEP, 2 * QUAD, 2 * tile), F32)] * 2
    scratch += [pltpu.VMEM((STEP, 2 * QUAD, 2 * tile), BF)] * 2
    scratch += [pltpu.VMEM((STEP, 2, 2 * tile), F32)] * 2
    scratch += [
        pltpu.SMEM((count * tiles + 1,), jnp.int32),
        pltpu.SMEM((tiles,), jnp.int32),
        pltpu.SMEM((count,), jnp.int32),
        pltpu.SMEM((count,), jnp.int32),
        pltpu.SemaphoreType.DMA((count, 2)),
    ]
    area = count * QUAD * tokens
    return pl.pallas_call(
        functools.partial(attend_kernel, setup),
        grid=(tiles,),
        in_specs=[smem()] * 4
        + query_specs
        + [pl.BlockSpec(a.shape, lambda i: (0, 0)) for a in raw]
        + [anywhere()] * (len(keys) + len(values) + len(waits))
        + state_specs * (not first),
        out_specs=out_specs,
        out_shape=outs,
        scratch_shapes=scratch,
        cost_estimate=cost(40 * area * width, 4 * width * tokens, area * width // HD),
        compiler_params=pltpu.CompilerParams(vmem_limit_bytes=ROOM),
        name="attend",
    )(
        *spans,
        *[queries] * PARTS,
        *raw,
        *keys,
        *values,
        *waits,
        *([] if first else state),
    )


def state_kernel(keys_hbm, values_hbm, own_ref, sent_ref, keys, values, sems):
    rows = lax.broadcasted_iota(jnp.int32, (QUAD, QUAD), 0) // HD
    columns = lax.broadcasted_iota(jnp.int32, (QUAD, QUAD), 1) // HD
    width, quads = keys.shape[0], sent_ref.shape[0]

    def moves(part):
        at = part_rows(width, quads, part)
        return (
            pltpu.make_async_copy(keys_hbm.at[at], keys.at[at], sems.at[2 * part]),
            pltpu.make_async_copy(values_hbm.at[at], values.at[at], sems.at[2 * part + 1]),
        )

    for part in range(PARTS):
        for move in moves(part):
            move.start()
    for q in range(quads):
        if q % (quads // PARTS) == 0:
            for move in moves(q // (quads // PARTS)):
                move.wait()
        lifted = jnp.maximum(quad_rows(keys, q, width), 0)
        grown = lax.dot_general(
            quad_rows(values, q, width), lifted, (((1,), (1,)), ((), ())), preferred_element_type=F32
        )
        grown = jnp.where(rows == columns, grown, 0.0)
        folded = grown[0:HD] + grown[HD : 2 * HD] + grown[2 * HD : 3 * HD] + grown[3 * HD :]
        own_ref[q] = folded
        sent_ref[q] = folded.astype(BF)


def stretch_states(keys, values):
    width, tokens = keys.shape
    quads = -(-width // QUAD)
    shape = (quads, HD, QUAD)
    return pl.pallas_call(
        state_kernel,
        in_specs=[anywhere()] * 2,
        out_specs=[vmem()] * 2,
        out_shape=[jax.ShapeDtypeStruct(shape, F32), jax.ShapeDtypeStruct(shape, BF)],
        scratch_shapes=[
            pltpu.VMEM((width, tokens), BF),
            pltpu.VMEM((width, tokens), BF),
            pltpu.SemaphoreType.DMA((2 * PARTS,)),
        ],
        cost_estimate=cost(8 * width * QUAD * tokens, 4 * width * tokens),
        compiler_params=pltpu.CompilerParams(vmem_limit_bytes=ROOM),
        name="stretch_states",
    )(keys, values)


def lower_sum(hop, prior, partners):
    digit = lax.axis_index("tm") // hop % (len(partners) + 1)
    for d, partner in enumerate(partners, 1):
        prior = prior + jnp.where((digit ^ d) < digit, partner.astype(F32), 0.0)
    return prior


def digit_step(own_ref, partners, sent_out):
    for q in range(sent_out.shape[0]):
        whole = own_ref[q]
        for partner in partners:
            whole = whole + partner[q].astype(F32)
        sent_out[q] = whole.astype(BF)


def digit_kernel(own_ref, *refs):
    digit_step(own_ref, refs[:-2], refs[-1])


def digit_sums(own, partners, token):
    return pl.pallas_call(
        digit_kernel,
        in_specs=[vmem()] * (1 + len(partners)) + [anywhere()],
        out_specs=vmem(),
        out_shape=jax.ShapeDtypeStruct(own.shape, BF),
        cost_estimate=cost(0, 8 * own.size),
        compiler_params=pltpu.CompilerParams(vmem_limit_bytes=ROOM),
        name="digit_sums",
    )(own, *partners, token)


def digits_of(size):
    hop, digits = 1, []
    while hop < size:
        radix = 4 if size // hop % 4 == 0 else 2
        digits.append((hop, radix))
        hop *= radix
    return digits


def swapped(block, hop, radix):
    size = lax.axis_size("tm")
    return [sent(block, [(i, i ^ (d * hop)) for i in range(size)]) for d in range(1, radix)]


def norm_kernel(digits, queries_hbm, own_ref, gain_ref, *refs):
    partners, refs = refs[:-7], refs[-6:]
    out_hbm, queries, raw, out, in_sems, out_sems = refs
    rows = lax.broadcasted_iota(jnp.int32, (QUAD, QUAD), 0) // HD
    columns = lax.broadcasted_iota(jnp.int32, (QUAD, QUAD), 1) // HD
    width = queries.shape[0]
    quads, tokens = raw.shape[0], raw.shape[2]
    every = quads // PARTS

    def move_in(part):
        at = part_rows(width, quads, part)
        return pltpu.make_async_copy(queries_hbm.at[at], queries.at[at], in_sems.at[part])

    def move_out(part):
        at = part_rows(width, quads, part)
        return pltpu.make_async_copy(out.at[at], out_hbm.at[at], out_sems.at[part])

    for part in range(PARTS):
        move_in(part).start()
    squares = jnp.zeros((1, tokens), F32)
    for q in range(quads):
        if q % every == 0:
            move_in(q // every).wait()
        whole, rest = own_ref[q], partners
        for hop, radix in digits:
            whole = lower_sum(hop, whole, [partner[q] for partner in rest[: radix - 1]])
            rest = rest[radix - 1 :]
        whole = whole.astype(BF).astype(F32)
        wide = jnp.where(rows == columns, jnp.concatenate([whole] * (QUAD // HD), axis=0), 0.0).astype(BF)
        lifted = jnp.maximum(quad_rows(queries, q, width), 0)
        part = jnp.dot(wide, lifted, preferred_element_type=F32)
        raw[q] = part
        squares = squares + jnp.sum(part * part, axis=0, keepdims=True)
    factor = lax.rsqrt(squares / width + 1e-05)
    for q in range(quads):
        size = min(QUAD, width - q * QUAD)
        gains = jnp.transpose(jnp.broadcast_to(gain_ref[q : q + 1, :], (QUAD, QUAD)))
        gains = jnp.concatenate([gains] * (tokens // QUAD), axis=1)
        mixed = (raw[q] * factor * gains).astype(BF)
        out[q * QUAD : q * QUAD + size, :] = mixed[:size]
        if q % every == every - 1:
            move_out(q // every).start()
    for part in range(PARTS):
        move_out(part).wait()


def self_mix(queries, own, gain, partners, digits, token):
    width, tokens = queries.shape
    quads = -(-width // QUAD)
    return pl.pallas_call(
        functools.partial(norm_kernel, tuple(digits)),
        in_specs=[anywhere()] + [vmem()] * (2 + len(partners)) + [anywhere()],
        out_specs=anywhere(),
        out_shape=jax.ShapeDtypeStruct((width, tokens), BF),
        scratch_shapes=[
            pltpu.VMEM((width, tokens), BF),
            pltpu.VMEM((quads, QUAD, tokens), F32),
            pltpu.VMEM((width, tokens), BF),
            pltpu.SemaphoreType.DMA((PARTS,)),
            pltpu.SemaphoreType.DMA((PARTS,)),
        ],
        cost_estimate=cost(8 * width * QUAD * tokens, 4 * width * tokens),
        compiler_params=pltpu.CompilerParams(vmem_limit_bytes=ROOM),
        name="self_mix",
    )(queries, own, jnp.pad(gain, (0, quads * QUAD - width)).reshape(quads, QUAD), *partners, token)


def sent(block, pairs):
    return lax.ppermute(block, "tm", pairs)


def local(
    queries,
    keys,
    values,
    cross_queries,
    prompt_keys,
    prompt_values,
    caption_keys,
    caption_values,
    span_start,
    span_end,
    prompt_tokens,
    region_mask,
    out_gain,
):
    size = lax.axis_size("tm")
    slots, width = prompt_keys.shape[1:]
    spans = (span_start, span_end, prompt_tokens, jnp.transpose(region_mask))
    turned = lambda block: jnp.transpose(block.reshape(slots, width))
    queries_t = jnp.transpose(cross_queries)
    call = functools.partial(attend, spans, queries_t)

    bases = [LAYER * z for z in range(size // LAYER)]
    beside = [(i, i ^ 1) for i in range(size)]
    up = [(i, (i + LAYER) % size) for i in range(size)]
    swap = [(i, i ^ 2) for i in range(size)]
    onward = [(i, i + LAYER - 1) for i in range(size) if i % 2 and i + LAYER - 1 < size]
    further = [(i, i + 1) for i in range(size) if i % 2 and i + 1 < size]
    spot = lambda c: c % LAYER
    pick = lambda c, *ways: functools.reduce(
        lambda rest, way: jnp.where(spot(c) == way[0], c - way[1], rest), ways, -1
    )
    digits = digits_of(size)

    own_v = turned(prompt_values)
    up_v = sent(own_v, up)
    own_k = turned_keys(prompt_tokens, turned(prompt_keys))
    own_sums, going = stretch_states(jnp.transpose(keys), jnp.transpose(values))
    caption = (jnp.transpose(caption_keys), jnp.transpose(caption_values))
    state = call([caption], lambda c: [None], None, False, waits=[own_k, going])

    partners = swapped(going, *digits[0])
    own_v_beside = sent(own_v, beside)
    own_k_beside = sent(own_k, beside)
    across_v, up_v, going = to_cross(
        own_v, up_v, state[0], own_v_beside, own_k_beside, states=[own_sums, *partners]
    )
    swap_v = sent(across_v, swap)
    (late_k,) = after([own_k], state[0], own_k_beside)
    up_k = sent(late_k, up)
    up_v_beside = sent(up_v, beside)
    for digit in digits[1:-1]:
        partners += swapped(going, *digit)
        going = digit_sums(own_sums, partners, state[0])
    final = swapped(going, *digits[-1]) if len(digits) > 1 else []
    state = call([(late_k, own_v)], lambda c: [c], state, False, waits=[across_v])

    swap_v, up_v_beside = after([swap_v, up_v_beside], state[0])
    across_k, up_k = to_cross(late_k, up_k, state[0], swap_v, up_v_beside, *final[:2])
    swap_k = sent(across_k, swap)
    far_k = sent(up_k, further)
    far_v = sent(swap_v, onward)
    up_k_beside = sent(up_k, beside)
    state = call(
        [(own_k_beside, own_v_beside), (up_k, up_v), (up_k_beside, up_v_beside)],
        lambda c: [
            pick(c, (1, 1), (3, 1)),
            c - LAYER,
            pick(c, (0, 3), (2, 3), (1, 5), (3, 5)),
        ],
        state,
        False,
        waits=[across_k],
    )

    self_mixed = self_mix(jnp.transpose(queries), own_sums, out_gain, partners + final, digits, state[0])
    swap_k, swap_v = after([swap_k, swap_v], state[0], self_mixed, far_k, far_v)
    swap_v_beside = sent(swap_v, beside)
    swap_k_beside = sent(swap_k, beside)
    cross_mixed = call(
        [(swap_k, swap_v), (swap_k_beside, swap_v_beside), (far_k, far_v)],
        lambda c: [
            c - 2,
            pick(c, (0, 1), (1, 3), (2, 1), (3, 3)),
            pick(c, (0, 5), (2, 5)),
        ],
        state,
        True,
    )[0]
    return (jnp.transpose(self_mixed), jnp.transpose(cross_mixed))


def solution(mesh):
    in_specs = (
        P(("groups", "tm"), None),
        P(("groups", "tm"), None),
        P(("groups", "tm"), None),
        P(("groups", "tm"), None),
        P(("groups", "tm"), None, None),
        P(("groups", "tm"), None, None),
        P("groups", None),
        P("groups", None),
        P("groups"),
        P("groups"),
        P("groups"),
        P("groups", None),
        P(),
    )
    out_specs = (P(("groups", "tm"), None), P(("groups", "tm"), None))
    return jax.shard_map(local, mesh=mesh, in_specs=in_specs, out_specs=out_specs, check_vma=False)
```

```python
import functools
import math

import jax
import jax.numpy as jnp
from jax import lax
from jax.experimental import pallas as pl
from jax.experimental.pallas import tpu as pltpu
from jax.sharding import PartitionSpec as P

HD = 32
SPAN = 6
QUAD = 128
LAYER = 4
BF = jnp.bfloat16
F32 = jnp.float32
EMPTY = -1e30
STEP = 3
PARTS = 3
COPIES = 2
ROOM = 66_900_000


def vmem():
    return pl.BlockSpec(memory_space=pltpu.VMEM)


def smem():
    return pl.BlockSpec(memory_space=pltpu.SMEM)


def anywhere():
    return pl.BlockSpec(memory_space=pl.ANY)


def cost(flops, moved, exps=0):
    flops, moved = flops // 1000, moved // 1000
    return pl.CostEstimate(flops=flops, bytes_accessed=moved, transcendentals=exps)


def quad_rows(ref, q, width):
    if (q + 1) * QUAD <= width:
        return ref[q * QUAD : (q + 1) * QUAD, :]
    part = ref[q * QUAD : width, :]
    fill = jnp.zeros(((q + 1) * QUAD - width, part.shape[1]), part.dtype)
    return jnp.concatenate([part, fill], axis=0)


def part_rows(width, quads, part):
    low = part * (quads // PARTS) * QUAD
    return pl.ds(low, min(quads // PARTS * QUAD, width - low))


def turned_quad(keys, used, rows):
    turned = jnp.transpose(keys.astype(F32))
    return jnp.where(rows < used, turned, turned[0:1, :]).astype(BF)


def turn_kernel(tokens_ref, *refs):
    count = len(refs) // 5
    keys_hbm, out_hbm, keys, out, sems = (refs[count * k : count * (k + 1)] for k in range(5))
    width, quads = keys[0].shape[0], out[0].shape[0]
    every = quads // PARTS
    rows = lax.broadcasted_iota(jnp.int32, (QUAD, QUAD), 0)

    def move_in(n, part):
        at = part_rows(width, quads, part)
        return pltpu.make_async_copy(keys_hbm[n].at[at], keys[n].at[at], sems[n].at[0, part])

    def move_out(n, part):
        at = pl.ds(part * every, every)
        return pltpu.make_async_copy(out[n].at[at], out_hbm[n].at[at], sems[n].at[1, part])

    for n in range(count):
        for part in range(PARTS):
            move_in(n, part).start()
    for n in range(count):
        used = QUAD if n else tokens_ref[lax.axis_index("tm")]
        for q in range(quads):
            if q % every == 0:
                move_in(n, q // every).wait()
            out[n][q] = turned_quad(quad_rows(keys[n], q, width), used, rows)
            if q % every == every - 1:
                move_out(n, q // every).start()
    for n in range(count):
        for part in range(PARTS):
            move_out(n, part).wait()


def turned_keys(tokens, *keys):
    width, slots = keys[0].shape
    shape = (-(-width // QUAD), slots, QUAD)
    count = len(keys)
    return pl.pallas_call(
        turn_kernel,
        in_specs=[smem()] + [anywhere()] * count,
        out_specs=[anywhere()] * count,
        out_shape=[jax.ShapeDtypeStruct(shape, BF)] * count,
        scratch_shapes=[pltpu.VMEM((width, slots), BF)] * count
        + [pltpu.VMEM(shape, BF)] * count
        + [pltpu.SemaphoreType.DMA((2, PARTS))] * count,
        cost_estimate=cost(0, 4 * width * slots),
        compiler_params=pltpu.CompilerParams(vmem_limit_bytes=ROOM),
        name="turned_keys",
    )(tokens, *keys)


def no_kernel(*refs):
    del refs


def after(blocks, *tokens):
    return pl.pallas_call(
        no_kernel,
        in_specs=[anywhere()] * (len(blocks) + len(tokens)),
        out_specs=[anywhere()] * len(blocks),
        out_shape=[jax.ShapeDtypeStruct(block.shape, block.dtype) for block in blocks],
        input_output_aliases={place: place for place in range(len(blocks))},
        cost_estimate=cost(0, 0),
        name="after",
    )(*blocks, *tokens)


def across_kernel(waits, own_hbm, up_hbm, *refs):
    across_hbm, _, held, in_sems, out_sems = refs[waits:]
    lower = lax.axis_index("tm") % LAYER < LAYER // 2
    piece = own_hbm.shape[0] // COPIES

    def move_in(source, part):
        at = pl.ds(part * piece, piece)
        return pltpu.make_async_copy(source.at[at], held.at[at], in_sems.at[part])

    def move_out(part):
        at = pl.ds(part * piece, piece)
        return pltpu.make_async_copy(held.at[at], across_hbm.at[at], out_sems.at[part])

    @pl.when(lower)
    def _():
        for part in range(COPIES):
            move_in(own_hbm, part).start()

    @pl.when(jnp.logical_not(lower))
    def _():
        for part in range(COPIES):
            move_in(up_hbm, part).start()

    for part in range(COPIES):
        move_in(up_hbm, part).wait()
        move_out(part).start()
    for part in range(COPIES):
        move_out(part).wait()


def to_cross(own, up, *tokens):
    shape = jax.ShapeDtypeStruct(own.shape, own.dtype)
    return pl.pallas_call(
        functools.partial(across_kernel, len(tokens)),
        in_specs=[anywhere()] * (2 + len(tokens)),
        out_specs=[anywhere()] * 2,
        out_shape=[shape, shape],
        input_output_aliases={1: 1},
        scratch_shapes=[
            pltpu.VMEM(own.shape, own.dtype),
            pltpu.SemaphoreType.DMA((COPIES,)),
            pltpu.SemaphoreType.DMA((COPIES,)),
        ],
        cost_estimate=cost(0, 4 * own.size),
        compiler_params=pltpu.CompilerParams(vmem_limit_bytes=ROOM),
        name="to_cross",
    )(own, up, *tokens)


def attend_kernel(setup, start_ref, end_ref, tokens_ref, region_ref, *refs):
    count, first, last, held, waits, prompts, width, tokens, tiles = setup
    tile = tokens // tiles
    quads = -(-width // QUAD)
    rounds = quads // STEP
    query_hbm, refs = refs[0], refs[1:]
    key_hbm, refs = refs[:count], refs[count:]
    value_hbm, refs = refs[:count], refs[count + waits :]
    if not first:
        state_in, refs = refs[:2], refs[2:]
    if last:
        out_ref, refs = refs[0], refs[1:]
    else:
        state_out, refs = refs[:2], refs[2:]
    keys, vals, marks, queries, spread, levels, totals, level, total, *refs = refs
    s_a, s_b, p_a, p_b, f_a, f_b, work, found, used, ready, sems, tile_sems = refs
    scale = math.log2(math.e) / math.sqrt(HD)
    none = jnp.zeros((HD, tile), BF)
    i = pl.program_id(0)

    def copies(b, at):
        return (
            pltpu.make_async_copy(key_hbm[b], keys.at[at], sems.at[at, 0]),
            pltpu.make_async_copy(value_hbm[b], vals.at[at, pl.ds(0, width)], sems.at[at, 1]),
        )

    def query_move(t):
        columns = pl.ds(t * tile, tile)
        return pltpu.make_async_copy(query_hbm.at[:, columns], queries.at[t], tile_sems.at[t, 0])

    def state_moves(t, into):
        for place, held_here in enumerate((levels, totals)):
            if into:
                yield pltpu.make_async_copy(state_in[place].at[t], held_here.at[t], tile_sems.at[t, 1 + place])
            else:
                yield pltpu.make_async_copy(held_here.at[t], state_out[place].at[t], tile_sems.at[t, 3 + place])

    @pl.when(i == 0)
    def _():
        stretch = lax.axis_index("tm")
        wanted = []
        lengths = [jnp.int32(0)] * tiles
        for b, owner in enumerate(held(stretch)):
            if owner is None:
                seen = [jnp.int32(1)] * tiles
                used[b] = jnp.int32(QUAD)
            else:
                safe = jnp.clip(owner, 0, prompts - 1)
                covers = (
                    (owner >= 0)
                    & (start_ref[safe] <= stretch)
                    & (stretch < end_ref[safe])
                )
                used[b] = tokens_ref[safe]
                seen = [
                    (covers & (region_ref[t, safe] == 1)).astype(jnp.int32)
                    for t in range(tiles)
                ]
            for t in range(tiles):
                work[t * count + lengths[t]] = jnp.int32(b)
                lengths[t] = lengths[t] + seen[t]
            wanted.append(functools.reduce(jnp.add, seen) > 0)
            ready[b] = jnp.int32(0)

            @pl.when(wanted[b])
            def _():
                for move in copies(b, b):
                    move.start()

        for t in range(tiles):
            found[t] = lengths[t]

            @pl.when(lengths[t] > 0)
            def _():
                query_move(t).start()

            if not first:

                @pl.when((lengths[t] > 0) | last)
                def _():
                    for move in state_moves(t, True):
                        move.start()

        for q in range(quads):
            for h in range(QUAD // HD):
                off = (1 - h % 2) * tile
                spread[q, h * HD : (h + 1) * HD, off : off + tile] = none
        lanes = lax.broadcasted_iota(jnp.int32, (16, QUAD), 1)
        for b in range(count):
            marks[b] = jnp.where(lanes < used[b], 1.0, 0.0).astype(BF)
            if width < quads * QUAD:
                vals[b, width:, :] = jnp.zeros((quads * QUAD - width, QUAD), BF)

    def arrived(b):
        @pl.when(ready[b] == 0)
        def _():
            for move in copies(0, b):
                move.wait()
            ready[b] = jnp.int32(1)

    low_half = lax.broadcasted_iota(jnp.int32, (QUAD, QUAD), 1) < QUAD // 2
    row16 = lax.broadcasted_iota(jnp.int32, (16, QUAD), 0)
    zeros = jnp.zeros((QUAD // 2, QUAD), BF)

    def score(b, g, s_to):
        for k in range(STEP):
            block = keys[b, g * STEP + k].astype(F32)
            both = jnp.concatenate(
                [jnp.where(low_half, block, 0.0), jnp.where(low_half, 0.0, block)], axis=0
            ).astype(BF)
            s_to[k] = jnp.dot(both, spread[g * STEP + k], preferred_element_type=F32)

    def weigh(g, s_from, p_to, f_to):
        for k in range(STEP):
            q = g * STEP + k
            for pair in range(2):
                at = slice(pair * QUAD, (pair + 1) * QUAD)
                part = s_from[k, at, :]
                old = level[q, pair : pair + 1]
                new = jnp.maximum(old, jnp.max(part, axis=0, keepdims=True))
                p_to[k, at, :] = jnp.exp2((part - new) * scale).astype(BF)
                f_to[k, pair : pair + 1] = jnp.exp2((old - new) * scale)
                level[q, pair : pair + 1] = new

    def mix(b, many, ones, g, p_from, f_from):
        for k in range(STEP):
            q = g * STEP + k
            v = vals[b, q * QUAD : (q + 1) * QUAD, :] * many
            left = jnp.concatenate(
                [
                    jnp.concatenate([v[: QUAD // 2], zeros], axis=1),
                    jnp.concatenate([zeros, v[QUAD // 2 :]], axis=1),
                    ones,
                ],
                axis=0,
            )
            out = jnp.dot(left, p_from[k], preferred_element_type=F32)
            factor = f_from[k]
            level[q, 2:4] = level[q, 2:4] * factor + out[QUAD : QUAD + 2]
            for pair in range(2):
                r = pair * 2 * HD
                added = jnp.concatenate([out[r : r + HD, :tile], out[r + HD : r + 2 * HD, tile:]], axis=1)
                at = slice(pair * HD, (pair + 1) * HD)
                total[q, at, :] = total[q, at, :] * factor[pair : pair + 1] + added

    slots = [(s_a, p_a, f_a), (s_b, p_b, f_b)]
    n = found[i]
    if first:
        level[:, 0:2] = jnp.full((quads, 2, 2 * tile), EMPTY, F32)
        level[:, 2:4] = jnp.zeros((quads, 2, 2 * tile), F32)
        total[...] = jnp.zeros(total.shape, F32)
    else:

        @pl.when((n > 0) | last)
        def _():
            for move in state_moves(i, True):
                move.wait()
            level[...] = levels[i]
            total[...] = totals[i]

    @pl.when(n > 0)
    def _():
        query_move(i).wait()
        for r in range(0, quads * QUAD, HD):
            q, h = r // QUAD, r % QUAD // HD
            on = h % 2 * tile
            piece = queries[i, r : r + HD, :] if r < width else none
            spread[q, h * HD : (h + 1) * HD, on : on + tile] = piece
        b0 = work[i * count]
        arrived(b0)
        score(b0, 0, s_a)
        weigh(0, s_a, p_a, f_a)
        score(b0, 1, s_b)

        def entry(j, carry):
            b = work[i * count + j]
            later = work[i * count + jnp.minimum(j + 1, n - 1)]
            arrived(later)
            mark = marks[b]
            many = jnp.concatenate([mark] * (QUAD // 16), axis=0)
            mark = mark.astype(F32)
            ones = jnp.concatenate(
                [jnp.where(row16 == 0, mark, 0.0), jnp.where(row16 == 1, mark, 0.0)], axis=1
            ).astype(BF)
            for g in range(rounds):
                here, there = slots[g % 2], slots[(g + 1) % 2]
                score(b if g + 2 < rounds else later, (g + 2) % rounds, here[0])
                mix(b, many, ones, g, here[1], here[2])
                weigh((g + 1) % rounds, there[0], there[1], there[2])
            return carry

        lax.fori_loop(0, n, entry, 0)

    if last:
        for q in range(quads):
            scaled = 1.0 / level[q, 2:4]
            for pair in range(2):
                mixed = total[q, pair * HD : (pair + 1) * HD, :] * scaled[pair : pair + 1]
                for side in range(2):
                    r = q * QUAD + (2 * pair + side) * HD
                    if r < width:
                        out_ref[r : r + HD, :] = mixed[:, side * tile : (side + 1) * tile].astype(BF)
    else:

        @pl.when((n > 0) | first)
        def _():
            levels[i] = level[...]
            totals[i] = total[...]
            for move in state_moves(i, False):
                move.start()

        @pl.when(i == tiles - 1)
        def _():
            for t in range(tiles):

                @pl.when((found[t] > 0) | first)
                def _():
                    for move in state_moves(t, False):
                        move.wait()


def attend(spans, queries, blocks, held, state, last, waits=()):
    width, tokens = queries.shape
    quads = -(-width // QUAD)
    count = len(blocks)
    tiles, prompts = spans[3].shape
    tile = tokens // tiles
    first = state is None
    setup = (count, first, last, held, len(waits), prompts, width, tokens, tiles)
    level, total = (quads, 4, 2 * tile), (quads, 2 * HD, 2 * tile)
    aliases = {}
    if last:
        outs = [jax.ShapeDtypeStruct((width, tokens), BF)]
        out_specs = [pl.BlockSpec((width, tile), lambda i: (0, i))]
    else:
        outs = [jax.ShapeDtypeStruct((tiles,) + shape, F32) for shape in (level, total)]
        out_specs = [anywhere()] * 2
        if not first:
            at = 5 + 2 * count + len(waits)
            aliases = {at: 0, at + 1: 1}
    keys = [block[0] for block in blocks]
    values = [block[1] for block in blocks]
    scratch = [
        pltpu.VMEM((count, quads, QUAD, QUAD), BF),
        pltpu.VMEM((count, quads * QUAD, QUAD), BF),
        pltpu.VMEM((count, 16, QUAD), BF),
        pltpu.VMEM((tiles, width, tile), BF),
        pltpu.VMEM((quads, QUAD, 2 * tile), BF),
        pltpu.VMEM((tiles,) + level, F32),
        pltpu.VMEM((tiles,) + total, F32),
        pltpu.VMEM(level, F32),
        pltpu.VMEM(total, F32),
    ]
    scratch += [pltpu.VMEM((STEP, 2 * QUAD, 2 * tile), F32)] * 2
    scratch += [pltpu.VMEM((STEP, 2 * QUAD, 2 * tile), BF)] * 2
    scratch += [pltpu.VMEM((STEP, 2, 2 * tile), F32)] * 2
    scratch += [
        pltpu.SMEM((count * tiles + 1,), jnp.int32),
        pltpu.SMEM((tiles,), jnp.int32),
        pltpu.SMEM((count,), jnp.int32),
        pltpu.SMEM((count,), jnp.int32),
        pltpu.SemaphoreType.DMA((count, 2)),
        pltpu.SemaphoreType.DMA((tiles, 5)),
    ]
    area = count * QUAD * tokens
    return pl.pallas_call(
        functools.partial(attend_kernel, setup),
        grid=(tiles,),
        in_specs=[smem()] * 4 + [anywhere()] * (1 + 2 * count + len(waits) + (0 if first else 2)),
        out_specs=out_specs,
        out_shape=outs,
        scratch_shapes=scratch,
        input_output_aliases=aliases,
        cost_estimate=cost(40 * area * width, 4 * width * tokens, area * width // HD),
        compiler_params=pltpu.CompilerParams(vmem_limit_bytes=ROOM),
        name="attend",
    )(
        *spans,
        queries,
        *keys,
        *values,
        *waits,
        *([] if first else state),
    )


def state_kernel(keys_hbm, values_hbm, own_ref, sent_ref, keys, values, sems):
    rows = lax.broadcasted_iota(jnp.int32, (QUAD, QUAD), 0) // HD
    columns = lax.broadcasted_iota(jnp.int32, (QUAD, QUAD), 1) // HD
    width, quads = keys.shape[0], sent_ref.shape[0]

    def moves(part):
        at = part_rows(width, quads, part)
        return (
            pltpu.make_async_copy(keys_hbm.at[at], keys.at[at], sems.at[2 * part]),
            pltpu.make_async_copy(values_hbm.at[at], values.at[at], sems.at[2 * part + 1]),
        )

    for part in range(PARTS):
        for move in moves(part):
            move.start()
    for q in range(quads):
        if q % (quads // PARTS) == 0:
            for move in moves(q // (quads // PARTS)):
                move.wait()
        lifted = jnp.maximum(quad_rows(keys, q, width), 0)
        grown = lax.dot_general(
            quad_rows(values, q, width), lifted, (((1,), (1,)), ((), ())), preferred_element_type=F32
        )
        grown = jnp.where(rows == columns, grown, 0.0)
        folded = grown[0:HD] + grown[HD : 2 * HD] + grown[2 * HD : 3 * HD] + grown[3 * HD :]
        own_ref[q] = folded
        sent_ref[q] = folded.astype(BF)


def stretch_states(keys, values):
    width, tokens = keys.shape
    quads = -(-width // QUAD)
    shape = (quads, HD, QUAD)
    return pl.pallas_call(
        state_kernel,
        in_specs=[anywhere()] * 2,
        out_specs=[vmem()] * 2,
        out_shape=[jax.ShapeDtypeStruct(shape, F32), jax.ShapeDtypeStruct(shape, BF)],
        scratch_shapes=[
            pltpu.VMEM((width, tokens), BF),
            pltpu.VMEM((width, tokens), BF),
            pltpu.SemaphoreType.DMA((2 * PARTS,)),
        ],
        cost_estimate=cost(8 * width * QUAD * tokens, 4 * width * tokens),
        compiler_params=pltpu.CompilerParams(vmem_limit_bytes=ROOM),
        name="stretch_states",
    )(keys, values)


def lower_sum(hop, prior, partners):
    digit = lax.axis_index("tm") // hop % (len(partners) + 1)
    for d, partner in enumerate(partners, 1):
        prior = prior + jnp.where((digit ^ d) < digit, partner.astype(F32), 0.0)
    return prior


def digit_step(own_ref, partners, sent_out):
    for q in range(sent_out.shape[0]):
        whole = own_ref[q]
        for partner in partners:
            whole = whole + partner[q].astype(F32)
        sent_out[q] = whole.astype(BF)


def digit_kernel(own_ref, *refs):
    digit_step(own_ref, refs[:-2], refs[-1])


def digit_sums(own, partners, token):
    return pl.pallas_call(
        digit_kernel,
        in_specs=[vmem()] * (1 + len(partners)) + [anywhere()],
        out_specs=vmem(),
        out_shape=jax.ShapeDtypeStruct(own.shape, BF),
        cost_estimate=cost(0, 8 * own.size),
        compiler_params=pltpu.CompilerParams(vmem_limit_bytes=ROOM),
        name="digit_sums",
    )(own, *partners, token)


def digits_of(size):
    hop, digits = 1, []
    while hop < size:
        radix = LAYER if hop == 1 and size % LAYER == 0 else 2
        digits.append((hop, radix))
        hop *= radix
    return digits


def swapped(block, hop, radix):
    size = lax.axis_size("tm")
    return [sent(block, [(i, i ^ (d * hop)) for i in range(size)]) for d in range(1, radix)]


def norm_kernel(digits, queries_hbm, own_ref, gain_ref, *refs):
    partners, refs = refs[:-7], refs[-6:]
    out_hbm, queries, raw, out, in_sems, out_sems = refs
    rows = lax.broadcasted_iota(jnp.int32, (QUAD, QUAD), 0) // HD
    columns = lax.broadcasted_iota(jnp.int32, (QUAD, QUAD), 1) // HD
    width = queries.shape[0]
    quads, tokens = raw.shape[0], raw.shape[2]
    every = quads // PARTS

    def move_in(part):
        at = part_rows(width, quads, part)
        return pltpu.make_async_copy(queries_hbm.at[at], queries.at[at], in_sems.at[part])

    def move_out(part):
        at = part_rows(width, quads, part)
        return pltpu.make_async_copy(out.at[at], out_hbm.at[at], out_sems.at[part])

    for part in range(PARTS):
        move_in(part).start()
    squares = jnp.zeros((1, tokens), F32)
    for q in range(quads):
        if q % every == 0:
            move_in(q // every).wait()
        whole, rest = own_ref[q], partners
        for hop, radix in digits:
            whole = lower_sum(hop, whole, [partner[q] for partner in rest[: radix - 1]])
            rest = rest[radix - 1 :]
        whole = whole.astype(BF).astype(F32)
        wide = jnp.where(rows == columns, jnp.concatenate([whole] * (QUAD // HD), axis=0), 0.0).astype(BF)
        lifted = jnp.maximum(quad_rows(queries, q, width), 0)
        part = jnp.dot(wide, lifted, preferred_element_type=F32)
        raw[q] = part
        squares = squares + jnp.sum(part * part, axis=0, keepdims=True)
    factor = lax.rsqrt(squares / width + 1e-05)
    for q in range(quads):
        size = min(QUAD, width - q * QUAD)
        gain = gain_ref[:, q * QUAD : q * QUAD + size]
        if size < QUAD:
            gain = jnp.concatenate([gain, jnp.zeros((1, QUAD - size), F32)], axis=1)
        gains = jnp.transpose(jnp.broadcast_to(gain, (QUAD, QUAD)))
        gains = jnp.concatenate([gains] * (tokens // QUAD), axis=1)
        mixed = (raw[q] * factor * gains).astype(BF)
        out[q * QUAD : q * QUAD + size, :] = mixed[:size]
        if q % every == every - 1:
            move_out(q // every).start()
    for part in range(PARTS):
        move_out(part).wait()


def self_mix(queries, own, gain, partners, digits, token):
    width, tokens = queries.shape
    quads = -(-width // QUAD)
    return pl.pallas_call(
        functools.partial(norm_kernel, tuple(digits)),
        in_specs=[anywhere()] + [vmem()] * (2 + len(partners)) + [anywhere()],
        out_specs=anywhere(),
        out_shape=jax.ShapeDtypeStruct((width, tokens), BF),
        scratch_shapes=[
            pltpu.VMEM((width, tokens), BF),
            pltpu.VMEM((quads, QUAD, tokens), F32),
            pltpu.VMEM((width, tokens), BF),
            pltpu.SemaphoreType.DMA((PARTS,)),
            pltpu.SemaphoreType.DMA((PARTS,)),
        ],
        cost_estimate=cost(8 * width * QUAD * tokens, 4 * width * tokens),
        compiler_params=pltpu.CompilerParams(vmem_limit_bytes=ROOM),
        name="self_mix",
    )(queries, own, gain, *partners, token)


def sent(block, pairs):
    return lax.ppermute(block, "tm", pairs)


def local(
    queries,
    keys,
    values,
    cross_queries,
    prompt_keys,
    prompt_values,
    caption_keys,
    caption_values,
    span_start,
    span_end,
    prompt_tokens,
    region_mask,
    out_gain,
):
    size = lax.axis_size("tm")
    slots, width = prompt_keys.shape[1:]
    spans = (span_start, span_end, prompt_tokens, jnp.transpose(region_mask))
    turned = lambda block: jnp.transpose(block.reshape(slots, width))
    queries_t = jnp.transpose(cross_queries)
    call = functools.partial(attend, spans, queries_t)

    bases = [LAYER * z for z in range(size // LAYER)]
    beside = [(i, i ^ 1) for i in range(size)]
    up = [(i, (i + LAYER) % size) for i in range(size)]
    swap = [(i, i ^ 2) for i in range(size)]
    onward = [(i, i + LAYER - 1) for i in range(size) if i % 2 and i + LAYER - 1 < size]
    further = [(i, i + 1) for i in range(size) if i % 2 and i + 1 < size]
    spot = lambda c: c % LAYER
    pick = lambda c, *ways: functools.reduce(
        lambda rest, way: jnp.where(spot(c) == way[0], c - way[1], rest), ways, -1
    )
    digits = digits_of(size)

    own_v = turned(prompt_values)
    up_v = sent(own_v, up)
    own_k, caption_k = turned_keys(prompt_tokens, turned(prompt_keys), jnp.transpose(caption_keys))
    own_v_beside = sent(own_v, beside)
    own_sums, going = stretch_states(jnp.transpose(keys), jnp.transpose(values))
    partners = swapped(going, *digits[0])
    state = call([(caption_k, jnp.transpose(caption_values))], lambda c: [None], None, False, waits=[going])

    gain_row = out_gain.reshape(1, width)
    across_v, up_v = to_cross(own_v, up_v, state[0], own_v_beside, gain_row, *partners)
    swap_v = sent(across_v, swap)
    (late_k,) = after([own_k], state[0])
    up_k = sent(late_k, up)
    own_k_beside = sent(late_k, beside)
    up_v_beside = sent(up_v, beside)
    for digit in digits[1:-1]:
        partners += swapped(digit_sums(own_sums, partners, across_v), *digit)
    state = call(
        [(late_k, own_v), (own_k_beside, own_v_beside)],
        lambda c: [c, pick(c, (1, 1), (3, 1))],
        state,
        False,
        waits=[across_v],
    )

    (swap_v,) = after([swap_v], state[0])
    across_k, up_k = to_cross(late_k, up_k, state[0], up_v_beside, *partners)
    swap_k = sent(across_k, swap)
    far_k = sent(up_k, further)
    far_v = sent(swap_v, onward)
    up_k_beside = sent(up_k, beside)
    final = []
    if len(digits) > 1:
        final = swapped(digit_sums(own_sums, partners, across_k), *digits[-1])
    state = call(
        [(up_k, up_v), (up_k_beside, up_v_beside)],
        lambda c: [c - LAYER, pick(c, (0, 3), (2, 3), (1, 5), (3, 5))],
        state,
        False,
        waits=[across_k],
    )

    swap_k, swap_v = after([swap_k, swap_v], state[0], far_k, far_v, *final)
    swap_k_beside = sent(swap_k, beside)
    swap_v_beside = sent(swap_v, beside)
    self_mixed = self_mix(jnp.transpose(queries), own_sums, gain_row, partners + final, digits, swap_k)
    cross_mixed = call(
        [(swap_k, swap_v), (swap_k_beside, swap_v_beside), (far_k, far_v)],
        lambda c: [
            c - 2,
            pick(c, (0, 1), (1, 3), (2, 1), (3, 3)),
            pick(c, (0, 5), (2, 5)),
        ],
        state,
        True,
        waits=[self_mixed],
    )[0]
    return (jnp.transpose(self_mixed), jnp.transpose(cross_mixed))


def solution(mesh):
    in_specs = (
        P(("groups", "tm"), None),
        P(("groups", "tm"), None),
        P(("groups", "tm"), None),
        P(("groups", "tm"), None),
        P(("groups", "tm"), None, None),
        P(("groups", "tm"), None, None),
        P("groups", None),
        P("groups", None),
        P("groups"),
        P("groups"),
        P("groups"),
        P("groups", None),
        P(),
    )
    out_specs = (P(("groups", "tm"), None), P(("groups", "tm"), None))
    return jax.shard_map(local, mesh=mesh, in_specs=in_specs, out_specs=out_specs, check_vma=False)
```

```python
import functools
import math

import jax
import jax.numpy as jnp
from jax import lax
from jax.experimental import pallas as pl
from jax.experimental.pallas import tpu as pltpu
from jax.sharding import PartitionSpec as P

HD = 32
SPAN = 6
QUAD = 128
LAYER = 4
BF = jnp.bfloat16
F32 = jnp.float32
EMPTY = -1e30
STEP = 3
PARTS = 3
COPIES = 2
ROOM = 66_900_000


def vmem():
    return pl.BlockSpec(memory_space=pltpu.VMEM)


def smem():
    return pl.BlockSpec(memory_space=pltpu.SMEM)


def anywhere():
    return pl.BlockSpec(memory_space=pl.ANY)


def cost(flops, moved, exps=0):
    flops, moved = flops // 1000, moved // 1000
    return pl.CostEstimate(flops=flops, bytes_accessed=moved, transcendentals=exps)


def quad_rows(ref, q, width):
    if (q + 1) * QUAD <= width:
        return ref[q * QUAD : (q + 1) * QUAD, :]
    part = ref[q * QUAD : width, :]
    fill = jnp.zeros(((q + 1) * QUAD - width, part.shape[1]), part.dtype)
    return jnp.concatenate([part, fill], axis=0)


def part_rows(width, quads, part):
    low = part * (quads // PARTS) * QUAD
    return pl.ds(low, min(quads // PARTS * QUAD, width - low))


def turned_quad(keys, used, rows):
    turned = jnp.transpose(keys.astype(F32))
    return jnp.where(rows < used, turned, turned[0:1, :]).astype(BF)


def no_kernel(*refs):
    del refs


def after(blocks, *tokens):
    return pl.pallas_call(
        no_kernel,
        in_specs=[anywhere()] * (len(blocks) + len(tokens)),
        out_specs=[anywhere()] * len(blocks),
        out_shape=[jax.ShapeDtypeStruct(block.shape, block.dtype) for block in blocks],
        input_output_aliases={place: place for place in range(len(blocks))},
        cost_estimate=cost(0, 0),
        name="after",
    )(*blocks, *tokens)


def across_kernel(waits, own_hbm, up_hbm, *refs):
    across_hbm, _, held, in_sems, out_sems = refs[waits:]
    lower = lax.axis_index("tm") % LAYER < LAYER // 2
    piece = own_hbm.shape[0] // COPIES

    def move_in(source, part):
        at = pl.ds(part * piece, piece)
        return pltpu.make_async_copy(source.at[at], held.at[at], in_sems.at[part])

    def move_out(part):
        at = pl.ds(part * piece, piece)
        return pltpu.make_async_copy(held.at[at], across_hbm.at[at], out_sems.at[part])

    @pl.when(lower)
    def _():
        for part in range(COPIES):
            move_in(own_hbm, part).start()

    @pl.when(jnp.logical_not(lower))
    def _():
        for part in range(COPIES):
            move_in(up_hbm, part).start()

    for part in range(COPIES):
        move_in(up_hbm, part).wait()
        move_out(part).start()
    for part in range(COPIES):
        move_out(part).wait()


def to_cross(own, up, *tokens):
    shape = jax.ShapeDtypeStruct(own.shape, own.dtype)
    return pl.pallas_call(
        functools.partial(across_kernel, len(tokens)),
        in_specs=[anywhere()] * (2 + len(tokens)),
        out_specs=[anywhere()] * 2,
        out_shape=[shape, shape],
        input_output_aliases={1: 1},
        scratch_shapes=[
            pltpu.VMEM(own.shape, own.dtype),
            pltpu.SemaphoreType.DMA((COPIES,)),
            pltpu.SemaphoreType.DMA((COPIES,)),
        ],
        cost_estimate=cost(0, 4 * own.size),
        compiler_params=pltpu.CompilerParams(vmem_limit_bytes=ROOM),
        name="to_cross",
    )(own, up, *tokens)


def attend_kernel(setup, start_ref, end_ref, tokens_ref, region_ref, *refs):
    count, first, last, held, waits, prompts, width, tokens, tiles = setup
    tile = tokens // tiles
    quads = -(-width // QUAD)
    rounds = quads // STEP
    query_hbm, refs = refs[0], refs[1:]
    key_hbm, refs = refs[:count], refs[count:]
    value_hbm, refs = refs[:count], refs[count + waits :]
    if not first:
        state_in, refs = refs[:2], refs[2:]
    if last:
        out_ref, refs = refs[0], refs[1:]
    else:
        state_out, refs = refs[:2], refs[2:]
    keys, vals, marks, queries, spread, levels, totals, level, total, *refs = refs
    s_a, s_b, p_a, p_b, f_a, f_b, work, found, used, ready, sems, tile_sems = refs
    scale = math.log2(math.e) / math.sqrt(HD)
    none = jnp.zeros((HD, tile), BF)
    i = pl.program_id(0)

    def copies(b, at):
        return (
            pltpu.make_async_copy(key_hbm[b], keys.at[at], sems.at[at, 0]),
            pltpu.make_async_copy(value_hbm[b], vals.at[at, pl.ds(0, width)], sems.at[at, 1]),
        )

    def query_move(t):
        columns = pl.ds(t * tile, tile)
        return pltpu.make_async_copy(query_hbm.at[:, columns], queries.at[t], tile_sems.at[t, 0])

    def state_moves(t, into):
        for place, held_here in enumerate((levels, totals)):
            if into:
                yield pltpu.make_async_copy(state_in[place].at[t], held_here.at[t], tile_sems.at[t, 1 + place])
            else:
                yield pltpu.make_async_copy(held_here.at[t], state_out[place].at[t], tile_sems.at[t, 3 + place])

    @pl.when(i == 0)
    def _():
        if last:
            for move in state_moves(0, True):
                move.start()
        stretch = lax.axis_index("tm")
        wanted = []
        lengths = [jnp.int32(0)] * tiles
        for b, owner in enumerate(held(stretch)):
            if owner is None:
                seen = [jnp.int32(1)] * tiles
                used[b] = jnp.int32(QUAD)
            else:
                safe = jnp.clip(owner, 0, prompts - 1)
                covers = (
                    (owner >= 0)
                    & (start_ref[safe] <= stretch)
                    & (stretch < end_ref[safe])
                )
                used[b] = tokens_ref[safe]
                seen = [
                    (covers & (region_ref[t, safe] == 1)).astype(jnp.int32)
                    for t in range(tiles)
                ]
            for t in range(tiles):
                work[t * count + lengths[t]] = jnp.int32(b)
                lengths[t] = lengths[t] + seen[t]
            wanted.append(functools.reduce(jnp.add, seen) > 0)
            ready[b] = jnp.int32(0)

            @pl.when(wanted[b])
            def _():
                for move in copies(b, b):
                    move.start()

        for t in range(tiles):
            found[t] = lengths[t]

            @pl.when(lengths[t] > 0)
            def _():
                query_move(t).start()

            if not first and not (last and t == 0):

                @pl.when((lengths[t] > 0) | last)
                def _():
                    for move in state_moves(t, True):
                        move.start()

        for q in range(quads):
            for h in range(QUAD // HD):
                off = (1 - h % 2) * tile
                spread[q, h * HD : (h + 1) * HD, off : off + tile] = none
        lanes = lax.broadcasted_iota(jnp.int32, (16, QUAD), 1)
        for b in range(count):
            marks[b] = jnp.where(lanes < used[b], 1.0, 0.0).astype(BF)
            if width < quads * QUAD:
                vals[b, width:, :] = jnp.zeros((quads * QUAD - width, QUAD), BF)

    def arrived(b):
        @pl.when(ready[b] == 0)
        def _():
            for move in copies(0, b):
                move.wait()
            ready[b] = jnp.int32(1)

    low_half = lax.broadcasted_iota(jnp.int32, (QUAD, QUAD), 1) < QUAD // 2
    row16 = lax.broadcasted_iota(jnp.int32, (16, QUAD), 0)
    zeros = jnp.zeros((QUAD // 2, QUAD), BF)

    def score(b, g, s_to):
        for k in range(STEP):
            block = keys[b, g * STEP + k].astype(F32)
            both = jnp.concatenate(
                [jnp.where(low_half, block, 0.0), jnp.where(low_half, 0.0, block)], axis=0
            ).astype(BF)
            s_to[k] = jnp.dot(both, spread[g * STEP + k], preferred_element_type=F32)

    def weigh(g, s_from, p_to, f_to):
        for k in range(STEP):
            q = g * STEP + k
            for pair in range(2):
                at = slice(pair * QUAD, (pair + 1) * QUAD)
                part = s_from[k, at, :]
                old = level[q, pair : pair + 1]
                new = jnp.maximum(old, jnp.max(part, axis=0, keepdims=True))
                p_to[k, at, :] = jnp.exp2((part - new) * scale).astype(BF)
                f_to[k, pair : pair + 1] = jnp.exp2((old - new) * scale)
                level[q, pair : pair + 1] = new

    def mix(b, many, ones, g, p_from, f_from):
        for k in range(STEP):
            q = g * STEP + k
            v = vals[b, q * QUAD : (q + 1) * QUAD, :] * many
            left = jnp.concatenate(
                [
                    jnp.concatenate([v[: QUAD // 2], zeros], axis=1),
                    jnp.concatenate([zeros, v[QUAD // 2 :]], axis=1),
                    ones,
                ],
                axis=0,
            )
            out = jnp.dot(left, p_from[k], preferred_element_type=F32)
            factor = f_from[k]
            level[q, 2:4] = level[q, 2:4] * factor + out[QUAD : QUAD + 2]
            for pair in range(2):
                r = pair * 2 * HD
                added = jnp.concatenate([out[r : r + HD, :tile], out[r + HD : r + 2 * HD, tile:]], axis=1)
                at = slice(pair * HD, (pair + 1) * HD)
                total[q, at, :] = total[q, at, :] * factor[pair : pair + 1] + added

    slots = [(s_a, p_a, f_a), (s_b, p_b, f_b)]
    n = found[i]
    if first:
        level[:, 0:2] = jnp.full((quads, 2, 2 * tile), EMPTY, F32)
        level[:, 2:4] = jnp.zeros((quads, 2, 2 * tile), F32)
        total[...] = jnp.zeros(total.shape, F32)
    else:

        @pl.when((n > 0) | last)
        def _():
            for move in state_moves(i, True):
                move.wait()
            level[...] = levels[i]
            total[...] = totals[i]

    @pl.when(n > 0)
    def _():
        query_move(i).wait()
        for r in range(0, quads * QUAD, HD):
            q, h = r // QUAD, r % QUAD // HD
            on = h % 2 * tile
            piece = queries[i, r : r + HD, :] if r < width else none
            spread[q, h * HD : (h + 1) * HD, on : on + tile] = piece
        b0 = work[i * count]
        arrived(b0)
        score(b0, 0, s_a)
        weigh(0, s_a, p_a, f_a)
        score(b0, 1, s_b)

        def entry(j, carry):
            b = work[i * count + j]
            later = work[i * count + jnp.minimum(j + 1, n - 1)]
            arrived(later)
            mark = marks[b]
            many = jnp.concatenate([mark] * (QUAD // 16), axis=0)
            mark = mark.astype(F32)
            ones = jnp.concatenate(
                [jnp.where(row16 == 0, mark, 0.0), jnp.where(row16 == 1, mark, 0.0)], axis=1
            ).astype(BF)
            for g in range(rounds):
                here, there = slots[g % 2], slots[(g + 1) % 2]
                score(b if g + 2 < rounds else later, (g + 2) % rounds, here[0])
                mix(b, many, ones, g, here[1], here[2])
                weigh((g + 1) % rounds, there[0], there[1], there[2])
            return carry

        lax.fori_loop(0, n, entry, 0)

    if last:
        for q in range(quads):
            scaled = 1.0 / level[q, 2:4]
            for pair in range(2):
                mixed = total[q, pair * HD : (pair + 1) * HD, :] * scaled[pair : pair + 1]
                for side in range(2):
                    r = q * QUAD + (2 * pair + side) * HD
                    if r < width:
                        out_ref[r : r + HD, :] = mixed[:, side * tile : (side + 1) * tile].astype(BF)
    else:

        @pl.when((n > 0) | first)
        def _():
            levels[i] = level[...]
            totals[i] = total[...]
            for move in state_moves(i, False):
                move.start()

        @pl.when(i == tiles - 1)
        def _():
            for t in range(tiles):

                @pl.when((found[t] > 0) | first)
                def _():
                    for move in state_moves(t, False):
                        move.wait()


def attend(spans, queries, blocks, held, state, last, waits=()):
    width, tokens = queries.shape
    quads = -(-width // QUAD)
    count = len(blocks)
    tiles, prompts = spans[3].shape
    tile = tokens // tiles
    first = state is None
    setup = (count, first, last, held, len(waits), prompts, width, tokens, tiles)
    level, total = (quads, 4, 2 * tile), (quads, 2 * HD, 2 * tile)
    aliases = {}
    if last:
        outs = [jax.ShapeDtypeStruct((width, tokens), BF)]
        out_specs = [pl.BlockSpec((width, tile), lambda i: (0, i))]
    else:
        outs = [jax.ShapeDtypeStruct((tiles,) + shape, F32) for shape in (level, total)]
        out_specs = [anywhere()] * 2
        if not first:
            at = 5 + 2 * count + len(waits)
            aliases = {at: 0, at + 1: 1}
    keys = [block[0] for block in blocks]
    values = [block[1] for block in blocks]
    scratch = [
        pltpu.VMEM((count, quads, QUAD, QUAD), BF),
        pltpu.VMEM((count, quads * QUAD, QUAD), BF),
        pltpu.VMEM((count, 16, QUAD), BF),
        pltpu.VMEM((tiles, width, tile), BF),
        pltpu.VMEM((quads, QUAD, 2 * tile), BF),
        pltpu.VMEM((tiles,) + level, F32),
        pltpu.VMEM((tiles,) + total, F32),
        pltpu.VMEM(level, F32),
        pltpu.VMEM(total, F32),
    ]
    scratch += [pltpu.VMEM((STEP, 2 * QUAD, 2 * tile), F32)] * 2
    scratch += [pltpu.VMEM((STEP, 2 * QUAD, 2 * tile), BF)] * 2
    scratch += [pltpu.VMEM((STEP, 2, 2 * tile), F32)] * 2
    scratch += [
        pltpu.SMEM((count * tiles + 1,), jnp.int32),
        pltpu.SMEM((tiles,), jnp.int32),
        pltpu.SMEM((count,), jnp.int32),
        pltpu.SMEM((count,), jnp.int32),
        pltpu.SemaphoreType.DMA((count, 2)),
        pltpu.SemaphoreType.DMA((tiles, 5)),
    ]
    area = count * QUAD * tokens
    return pl.pallas_call(
        functools.partial(attend_kernel, setup),
        grid=(tiles,),
        in_specs=[smem()] * 4 + [anywhere()] * (1 + 2 * count + len(waits) + (0 if first else 2)),
        out_specs=out_specs,
        out_shape=outs,
        scratch_shapes=scratch,
        input_output_aliases=aliases,
        cost_estimate=cost(40 * area * width, 4 * width * tokens, area * width // HD),
        compiler_params=pltpu.CompilerParams(vmem_limit_bytes=ROOM),
        name="attend",
    )(
        *spans,
        queries,
        *keys,
        *values,
        *waits,
        *([] if first else state),
    )


def front_kernel(tokens_ref, *refs):
    sources, (own_ref, sent_ref), turned_hbm, refs = refs[:4], refs[4:6], refs[6:8], refs[8:]
    arrays, turned, (in_sems, out_sems) = refs[:4], refs[4:6], refs[6:]
    rows = lax.broadcasted_iota(jnp.int32, (QUAD, QUAD), 0)
    columns = lax.broadcasted_iota(jnp.int32, (QUAD, QUAD), 1)
    width, quads = arrays[0].shape[0], sent_ref.shape[0]
    every = quads // PARTS

    def move_in(n, part):
        at = part_rows(width, quads, part)
        return pltpu.make_async_copy(sources[n].at[at], arrays[n].at[at], in_sems.at[n, part])

    def move_out(n, part):
        at = pl.ds(part * every, every)
        return pltpu.make_async_copy(turned[n].at[at], turned_hbm[n].at[at], out_sems.at[n, part])

    for part in range(PARTS):
        for n in range(2):
            move_in(n, part).start()
    for n in range(2, 4):
        for part in range(PARTS):
            move_in(n, part).start()
    for n in range(2):
        used = QUAD if n else tokens_ref[lax.axis_index("tm")]
        for q in range(quads):
            if q % every == 0:
                move_in(2 + n, q // every).wait()
            turned[n][q] = turned_quad(quad_rows(arrays[2 + n], q, width), used, rows)
            if q % every == every - 1:
                move_out(n, q // every).start()
    for q in range(quads):
        if q % every == 0:
            for n in range(2):
                move_in(n, q // every).wait()
        lifted = jnp.maximum(quad_rows(arrays[0], q, width), 0)
        grown = lax.dot_general(
            quad_rows(arrays[1], q, width), lifted, (((1,), (1,)), ((), ())), preferred_element_type=F32
        )
        grown = jnp.where(rows // HD == columns // HD, grown, 0.0)
        folded = grown[0:HD] + grown[HD : 2 * HD] + grown[2 * HD : 3 * HD] + grown[3 * HD :]
        own_ref[q] = folded
        sent_ref[q] = folded.astype(BF)
    for n in range(2):
        for part in range(PARTS):
            move_out(n, part).wait()


def front(tokens, keys, values, prompt_keys, caption_keys):
    width = keys.shape[0]
    quads = -(-width // QUAD)
    arrays = (keys, values, prompt_keys, caption_keys)
    state, turned = (quads, HD, QUAD), (quads, QUAD, QUAD)
    return pl.pallas_call(
        front_kernel,
        in_specs=[smem()] + [anywhere()] * 4,
        out_specs=[vmem()] * 2 + [anywhere()] * 2,
        out_shape=[jax.ShapeDtypeStruct(state, F32), jax.ShapeDtypeStruct(state, BF)]
        + [jax.ShapeDtypeStruct(turned, BF)] * 2,
        scratch_shapes=[pltpu.VMEM(array.shape, BF) for array in arrays]
        + [pltpu.VMEM(turned, BF)] * 2
        + [pltpu.SemaphoreType.DMA((4, PARTS)), pltpu.SemaphoreType.DMA((2, PARTS))],
        cost_estimate=cost(8 * width * QUAD * keys.shape[1], 4 * keys.size),
        compiler_params=pltpu.CompilerParams(vmem_limit_bytes=ROOM),
        name="front",
    )(tokens, *arrays)


def lower_sum(hop, prior, partners):
    digit = lax.axis_index("tm") // hop % (len(partners) + 1)
    for d, partner in enumerate(partners, 1):
        prior = prior + jnp.where((digit ^ d) < digit, partner.astype(F32), 0.0)
    return prior


def digit_step(own_ref, partners, sent_out):
    for q in range(sent_out.shape[0]):
        whole = own_ref[q]
        for partner in partners:
            whole = whole + partner[q].astype(F32)
        sent_out[q] = whole.astype(BF)


def digit_kernel(own_ref, *refs):
    digit_step(own_ref, refs[:-2], refs[-1])


def digit_sums(own, partners, token):
    return pl.pallas_call(
        digit_kernel,
        in_specs=[vmem()] * (1 + len(partners)) + [anywhere()],
        out_specs=vmem(),
        out_shape=jax.ShapeDtypeStruct(own.shape, BF),
        cost_estimate=cost(0, 8 * own.size),
        compiler_params=pltpu.CompilerParams(vmem_limit_bytes=ROOM),
        name="digit_sums",
    )(own, *partners, token)


def digits_of(size):
    hop, digits = 1, []
    while hop < size:
        radix = LAYER if hop == 1 and size % LAYER == 0 else 2
        digits.append((hop, radix))
        hop *= radix
    return digits


def swapped(block, hop, radix):
    size = lax.axis_size("tm")
    return [sent(block, [(i, i ^ (d * hop)) for i in range(size)]) for d in range(1, radix)]


def norm_kernel(digits, queries_hbm, gain_hbm, own_hbm, *refs):
    count = sum(radix - 1 for _, radix in digits)
    partners_hbm, refs = refs[:count], refs[count + 1 :]
    out_hbm, queries, raw, out, gain_ref, own_ref, partners, in_sems, out_sems, state_sems = refs
    rows = lax.broadcasted_iota(jnp.int32, (QUAD, QUAD), 0) // HD
    columns = lax.broadcasted_iota(jnp.int32, (QUAD, QUAD), 1) // HD
    width = queries.shape[0]
    quads, tokens = raw.shape[0], raw.shape[2]
    every = quads // PARTS

    def move_in(part):
        at = part_rows(width, quads, part)
        return pltpu.make_async_copy(queries_hbm.at[at], queries.at[at], in_sems.at[part])

    def move_out(part):
        at = part_rows(width, quads, part)
        return pltpu.make_async_copy(out.at[at], out_hbm.at[at], out_sems.at[part])

    moves = [
        pltpu.make_async_copy(own_hbm, own_ref, state_sems.at[count]),
        pltpu.make_async_copy(gain_hbm, gain_ref, state_sems.at[count + 1]),
    ]
    for n in range(count):
        moves.append(pltpu.make_async_copy(partners_hbm[n], partners.at[n], state_sems.at[n]))
    for move in moves:
        move.start()
    for part in range(PARTS):
        move_in(part).start()
    for move in moves:
        move.wait()
    squares = jnp.zeros((1, tokens), F32)
    for q in range(quads):
        if q % every == 0:
            move_in(q // every).wait()
        whole, first = own_ref[q], 0
        for hop, radix in digits:
            whole = lower_sum(hop, whole, [partners[first + n, q] for n in range(radix - 1)])
            first += radix - 1
        whole = whole.astype(BF).astype(F32)
        wide = jnp.where(rows == columns, jnp.concatenate([whole] * (QUAD // HD), axis=0), 0.0).astype(BF)
        lifted = jnp.maximum(quad_rows(queries, q, width), 0)
        part = jnp.dot(wide, lifted, preferred_element_type=F32)
        raw[q] = part
        squares = squares + jnp.sum(part * part, axis=0, keepdims=True)
    factor = lax.rsqrt(squares / width + 1e-05)
    for q in range(quads):
        size = min(QUAD, width - q * QUAD)
        gain = gain_ref[:, q * QUAD : q * QUAD + size]
        if size < QUAD:
            gain = jnp.concatenate([gain, jnp.zeros((1, QUAD - size), F32)], axis=1)
        gains = jnp.transpose(jnp.broadcast_to(gain, (QUAD, QUAD)))
        gains = jnp.concatenate([gains] * (tokens // QUAD), axis=1)
        mixed = (raw[q] * factor * gains).astype(BF)
        out[q * QUAD : q * QUAD + size, :] = mixed[:size]
        if q % every == every - 1:
            move_out(q // every).start()
    for part in range(PARTS):
        move_out(part).wait()


def self_mix(queries, own, gain, partners, digits, token):
    width, tokens = queries.shape
    quads = -(-width // QUAD)
    return pl.pallas_call(
        functools.partial(norm_kernel, tuple(digits)),
        in_specs=[anywhere()] * (4 + len(partners)),
        out_specs=anywhere(),
        out_shape=jax.ShapeDtypeStruct((width, tokens), BF),
        scratch_shapes=[
            pltpu.VMEM((width, tokens), BF),
            pltpu.VMEM((quads, QUAD, tokens), F32),
            pltpu.VMEM((width, tokens), BF),
            pltpu.VMEM(gain.shape, F32),
            pltpu.VMEM(own.shape, F32),
            pltpu.VMEM((len(partners),) + own.shape, BF),
            pltpu.SemaphoreType.DMA((PARTS,)),
            pltpu.SemaphoreType.DMA((PARTS,)),
            pltpu.SemaphoreType.DMA((len(partners) + 2,)),
        ],
        cost_estimate=cost(8 * width * QUAD * tokens, 4 * width * tokens),
        compiler_params=pltpu.CompilerParams(vmem_limit_bytes=ROOM),
        name="self_mix",
    )(queries, gain, own, *partners, token)


def sent(block, pairs):
    return lax.ppermute(block, "tm", pairs)


def local(
    queries,
    keys,
    values,
    cross_queries,
    prompt_keys,
    prompt_values,
    caption_keys,
    caption_values,
    span_start,
    span_end,
    prompt_tokens,
    region_mask,
    out_gain,
):
    size = lax.axis_size("tm")
    slots, width = prompt_keys.shape[1:]
    spans = (span_start, span_end, prompt_tokens, jnp.transpose(region_mask))
    turned = lambda block: jnp.transpose(block.reshape(slots, width))
    queries_t = jnp.transpose(cross_queries)
    call = functools.partial(attend, spans, queries_t)

    bases = [LAYER * z for z in range(size // LAYER)]
    beside = [(i, i ^ 1) for i in range(size)]
    up = [(i, (i + LAYER) % size) for i in range(size)]
    swap = [(i, i ^ 2) for i in range(size)]
    onward = [(i, i + LAYER - 1) for i in range(size) if i % 2 and i + LAYER - 1 < size]
    further = [(i, i + 1) for i in range(size) if i % 2 and i + 1 < size]
    spot = lambda c: c % LAYER
    pick = lambda c, *ways: functools.reduce(
        lambda rest, way: jnp.where(spot(c) == way[0], c - way[1], rest), ways, -1
    )
    digits = digits_of(size)

    own_v = turned(prompt_values)
    up_v = sent(own_v, up)
    own_v_beside = sent(own_v, beside)
    own_sums, going, own_k, caption_k = front(
        prompt_tokens,
        jnp.transpose(keys),
        jnp.transpose(values),
        turned(prompt_keys),
        jnp.transpose(caption_keys),
    )
    partners = swapped(going, *digits[0])
    gain_row = out_gain.reshape(1, width)
    state = call([(caption_k, jnp.transpose(caption_values))], lambda c: [None], None, False, waits=[going])

    across_v, up_v = to_cross(own_v, up_v, state[0], own_v_beside, *partners)
    swap_v = sent(across_v, swap)
    (late_k,) = after([own_k], state[0])
    up_k = sent(late_k, up)
    own_k_beside = sent(late_k, beside)
    up_v_beside = sent(up_v, beside)
    for digit in digits[1:-1]:
        partners += swapped(digit_sums(own_sums, partners, across_v), *digit)
    state = call(
        [(late_k, own_v), (own_k_beside, own_v_beside)],
        lambda c: [c, pick(c, (1, 1), (3, 1))],
        state,
        False,
        waits=[across_v, gain_row],
    )

    (swap_v,) = after([swap_v], state[0])
    across_k, up_k = to_cross(late_k, up_k, state[0], up_v_beside, *partners)
    swap_k = sent(across_k, swap)
    far_k = sent(up_k, further)
    far_v = sent(swap_v, onward)
    up_k_beside = sent(up_k, beside)
    final = []
    if len(digits) > 1:
        final = swapped(digit_sums(own_sums, partners, across_k), *digits[-1])
    state = call(
        [(up_k, up_v), (up_k_beside, up_v_beside)],
        lambda c: [c - LAYER, pick(c, (0, 3), (2, 3), (1, 5), (3, 5))],
        state,
        False,
        waits=[across_k],
    )

    swap_k, swap_v = after([swap_k, swap_v], state[0], far_v, *final)
    swap_k_beside = sent(swap_k, beside)
    swap_v_beside = sent(swap_v, beside)
    self_mixed = self_mix(jnp.transpose(queries), own_sums, gain_row, partners + final, digits, swap_k)
    cross_mixed = call(
        [(swap_k, swap_v), (swap_k_beside, swap_v_beside), (far_k, far_v)],
        lambda c: [
            c - 2,
            pick(c, (0, 1), (1, 3), (2, 1), (3, 3)),
            pick(c, (0, 5), (2, 5)),
        ],
        state,
        True,
        waits=[self_mixed],
    )[0]
    return (jnp.transpose(self_mixed), jnp.transpose(cross_mixed))


def solution(mesh):
    in_specs = (
        P(("groups", "tm"), None),
        P(("groups", "tm"), None),
        P(("groups", "tm"), None),
        P(("groups", "tm"), None),
        P(("groups", "tm"), None, None),
        P(("groups", "tm"), None, None),
        P("groups", None),
        P("groups", None),
        P("groups"),
        P("groups"),
        P("groups"),
        P("groups", None),
        P(),
    )
    out_specs = (P(("groups", "tm"), None), P(("groups", "tm"), None))
    return jax.shard_map(local, mesh=mesh, in_specs=in_specs, out_specs=out_specs, check_vma=False)
```

```python
import functools
import math

import jax
import jax.numpy as jnp
from jax import lax
from jax.experimental import pallas as pl
from jax.experimental.pallas import tpu as pltpu
from jax.sharding import PartitionSpec as P

HD = 32
SPAN = 6
QUAD = 128
LAYER = 4
BF = jnp.bfloat16
F32 = jnp.float32
EMPTY = -1e30
STEP = 3
PARTS = 3
COPIES = 2
ROOM = 66_900_000


def vmem():
    return pl.BlockSpec(memory_space=pltpu.VMEM)


def smem():
    return pl.BlockSpec(memory_space=pltpu.SMEM)


def anywhere():
    return pl.BlockSpec(memory_space=pl.ANY)


def cost(flops, moved, exps=0):
    flops, moved = flops // 1000, moved // 1000
    return pl.CostEstimate(flops=flops, bytes_accessed=moved, transcendentals=exps)


def quad_rows(ref, q, width):
    if (q + 1) * QUAD <= width:
        return ref[q * QUAD : (q + 1) * QUAD, :]
    part = ref[q * QUAD : width, :]
    fill = jnp.zeros(((q + 1) * QUAD - width, part.shape[1]), part.dtype)
    return jnp.concatenate([part, fill], axis=0)


def part_rows(width, quads, part):
    low = part * (quads // PARTS) * QUAD
    return pl.ds(low, min(quads // PARTS * QUAD, width - low))


def turned_quad(keys, used, rows):
    turned = jnp.transpose(keys.astype(F32))
    return jnp.where(rows < used, turned, turned[0:1, :]).astype(BF)


def no_kernel(*refs):
    del refs


def after(blocks, *tokens):
    return pl.pallas_call(
        no_kernel,
        in_specs=[anywhere()] * (len(blocks) + len(tokens)),
        out_specs=[anywhere()] * len(blocks),
        out_shape=[jax.ShapeDtypeStruct(block.shape, block.dtype) for block in blocks],
        input_output_aliases={place: place for place in range(len(blocks))},
        cost_estimate=cost(0, 0),
        name="after",
    )(*blocks, *tokens)


def across_kernel(waits, count, own_hbm, up_hbm, *refs):
    states_hbm, refs = refs[waits : waits + count], refs[waits + count :]
    across_hbm, _, *refs = refs
    if count:
        sent_hbm, held, in_sems, out_sems, own_state, partners, sent_here, state_sems = refs
    else:
        held, in_sems, out_sems = refs
    lower = lax.axis_index("tm") % LAYER < LAYER // 2
    piece = own_hbm.shape[0] // COPIES

    def move_in(source, part):
        at = pl.ds(part * piece, piece)
        return pltpu.make_async_copy(source.at[at], held.at[at], in_sems.at[part])

    def move_out(part):
        at = pl.ds(part * piece, piece)
        return pltpu.make_async_copy(held.at[at], across_hbm.at[at], out_sems.at[part])

    @pl.when(lower)
    def _():
        for part in range(COPIES):
            move_in(own_hbm, part).start()

    @pl.when(jnp.logical_not(lower))
    def _():
        for part in range(COPIES):
            move_in(up_hbm, part).start()

    moves = []
    for n in range(count):
        into = partners.at[n - 1] if n else own_state
        moves.append(pltpu.make_async_copy(states_hbm[n], into, state_sems.at[n]))
    for move in moves:
        move.start()
    for part in range(COPIES):
        move_in(up_hbm, part).wait()
        move_out(part).start()
    for move in moves:
        move.wait()
    if count:
        digit_step(own_state, [partners.at[n] for n in range(count - 1)], sent_here)
        away = pltpu.make_async_copy(sent_here, sent_hbm, state_sems.at[count])
        away.start()
        away.wait()
    for part in range(COPIES):
        move_out(part).wait()


def to_cross(own, up, *tokens, states=()):
    shape = jax.ShapeDtypeStruct(own.shape, own.dtype)
    outs = [shape, shape]
    scratch = [
        pltpu.VMEM(own.shape, own.dtype),
        pltpu.SemaphoreType.DMA((COPIES,)),
        pltpu.SemaphoreType.DMA((COPIES,)),
    ]
    if states:
        state = states[0].shape
        outs.append(jax.ShapeDtypeStruct(state, BF))
        scratch += [
            pltpu.VMEM(state, F32),
            pltpu.VMEM((len(states) - 1,) + state, BF),
            pltpu.VMEM(state, BF),
            pltpu.SemaphoreType.DMA((len(states) + 1,)),
        ]
    return pl.pallas_call(
        functools.partial(across_kernel, len(tokens), len(states)),
        in_specs=[anywhere()] * (2 + len(tokens) + len(states)),
        out_specs=[anywhere()] * len(outs),
        out_shape=outs,
        input_output_aliases={1: 1},
        scratch_shapes=scratch,
        cost_estimate=cost(0, 4 * own.size),
        compiler_params=pltpu.CompilerParams(vmem_limit_bytes=ROOM),
        name="to_cross",
    )(own, up, *tokens, *states)


def attend_kernel(setup, start_ref, end_ref, tokens_ref, region_ref, *refs):
    count, first, last, held, waits, prompts, width, tokens, tiles = setup
    tile = tokens // tiles
    quads = -(-width // QUAD)
    rounds = quads // STEP
    query_hbm, refs = refs[0], refs[1:]
    key_hbm, refs = refs[:count], refs[count:]
    value_hbm, refs = refs[:count], refs[count + waits :]
    if not first:
        state_in, refs = refs[:2], refs[2:]
    if last:
        out_ref, refs = refs[0], refs[1:]
    else:
        state_out, refs = refs[:2], refs[2:]
    keys, vals, marks, queries, spread, levels, totals, level, total, *refs = refs
    s_a, s_b, p_a, p_b, f_a, f_b, work, found, used, ready, sems, tile_sems = refs
    scale = math.log2(math.e) / math.sqrt(HD)
    none = jnp.zeros((HD, tile), BF)
    i = pl.program_id(0)

    def copies(b, at):
        return (
            pltpu.make_async_copy(key_hbm[b], keys.at[at], sems.at[at, 0]),
            pltpu.make_async_copy(value_hbm[b], vals.at[at, pl.ds(0, width)], sems.at[at, 1]),
        )

    def query_move(t):
        columns = pl.ds(t * tile, tile)
        return pltpu.make_async_copy(query_hbm.at[:, columns], queries.at[t], tile_sems.at[t, 0])

    def state_moves(t, into):
        for place, held_here in enumerate((levels, totals)):
            if into:
                yield pltpu.make_async_copy(state_in[place].at[t], held_here.at[t], tile_sems.at[t, 1 + place])
            else:
                yield pltpu.make_async_copy(held_here.at[t], state_out[place].at[t], tile_sems.at[t, 3 + place])

    @pl.when(i == 0)
    def _():
        if last:
            for move in state_moves(0, True):
                move.start()
        stretch = lax.axis_index("tm")
        wanted = []
        lengths = [jnp.int32(0)] * tiles
        for b, owner in enumerate(held(stretch)):
            if owner is None:
                seen = [jnp.int32(1)] * tiles
                used[b] = jnp.int32(QUAD)
            else:
                safe = jnp.clip(owner, 0, prompts - 1)
                covers = (
                    (owner >= 0)
                    & (start_ref[safe] <= stretch)
                    & (stretch < end_ref[safe])
                )
                used[b] = tokens_ref[safe]
                seen = [
                    (covers & (region_ref[t, safe] == 1)).astype(jnp.int32)
                    for t in range(tiles)
                ]
            for t in range(tiles):
                work[t * count + lengths[t]] = jnp.int32(b)
                lengths[t] = lengths[t] + seen[t]
            wanted.append(functools.reduce(jnp.add, seen) > 0)
            ready[b] = jnp.int32(0)

            @pl.when(wanted[b])
            def _():
                for move in copies(b, b):
                    move.start()

        for t in range(tiles):
            found[t] = lengths[t]

            @pl.when(lengths[t] > 0)
            def _():
                query_move(t).start()

            if not first and not (last and t == 0):

                @pl.when((lengths[t] > 0) | last)
                def _():
                    for move in state_moves(t, True):
                        move.start()

        for q in range(quads):
            for h in range(QUAD // HD):
                off = (1 - h % 2) * tile
                spread[q, h * HD : (h + 1) * HD, off : off + tile] = none
        lanes = lax.broadcasted_iota(jnp.int32, (16, QUAD), 1)
        for b in range(count):
            marks[b] = jnp.where(lanes < used[b], 1.0, 0.0).astype(BF)
            if width < quads * QUAD:
                vals[b, width:, :] = jnp.zeros((quads * QUAD - width, QUAD), BF)

    def arrived(b):
        @pl.when(ready[b] == 0)
        def _():
            for move in copies(0, b):
                move.wait()
            ready[b] = jnp.int32(1)

    low_half = lax.broadcasted_iota(jnp.int32, (QUAD, QUAD), 1) < QUAD // 2
    row16 = lax.broadcasted_iota(jnp.int32, (16, QUAD), 0)
    zeros = jnp.zeros((QUAD // 2, QUAD), BF)

    def score(b, g, s_to):
        for k in range(STEP):
            block = keys[b, g * STEP + k].astype(F32)
            both = jnp.concatenate(
                [jnp.where(low_half, block, 0.0), jnp.where(low_half, 0.0, block)], axis=0
            ).astype(BF)
            s_to[k] = jnp.dot(both, spread[g * STEP + k], preferred_element_type=F32)

    def weigh(g, s_from, p_to, f_to):
        for k in range(STEP):
            q = g * STEP + k
            for pair in range(2):
                at = slice(pair * QUAD, (pair + 1) * QUAD)
                part = s_from[k, at, :]
                old = level[q, pair : pair + 1]
                new = jnp.maximum(old, jnp.max(part, axis=0, keepdims=True))
                p_to[k, at, :] = jnp.exp2((part - new) * scale).astype(BF)
                f_to[k, pair : pair + 1] = jnp.exp2((old - new) * scale)
                level[q, pair : pair + 1] = new

    def mix(b, many, ones, g, p_from, f_from):
        for k in range(STEP):
            q = g * STEP + k
            v = vals[b, q * QUAD : (q + 1) * QUAD, :] * many
            left = jnp.concatenate(
                [
                    jnp.concatenate([v[: QUAD // 2], zeros], axis=1),
                    jnp.concatenate([zeros, v[QUAD // 2 :]], axis=1),
                    ones,
                ],
                axis=0,
            )
            out = jnp.dot(left, p_from[k], preferred_element_type=F32)
            factor = f_from[k]
            level[q, 2:4] = level[q, 2:4] * factor + out[QUAD : QUAD + 2]
            for pair in range(2):
                r = pair * 2 * HD
                added = jnp.concatenate([out[r : r + HD, :tile], out[r + HD : r + 2 * HD, tile:]], axis=1)
                at = slice(pair * HD, (pair + 1) * HD)
                total[q, at, :] = total[q, at, :] * factor[pair : pair + 1] + added

    slots = [(s_a, p_a, f_a), (s_b, p_b, f_b)]
    n = found[i]
    if first:
        level[:, 0:2] = jnp.full((quads, 2, 2 * tile), EMPTY, F32)
        level[:, 2:4] = jnp.zeros((quads, 2, 2 * tile), F32)
        total[...] = jnp.zeros(total.shape, F32)
    else:

        @pl.when((n > 0) | last)
        def _():
            for move in state_moves(i, True):
                move.wait()
            level[...] = levels[i]
            total[...] = totals[i]

    @pl.when(n > 0)
    def _():
        query_move(i).wait()
        for r in range(0, quads * QUAD, HD):
            q, h = r // QUAD, r % QUAD // HD
            on = h % 2 * tile
            piece = queries[i, r : r + HD, :] if r < width else none
            spread[q, h * HD : (h + 1) * HD, on : on + tile] = piece
        b0 = work[i * count]
        arrived(b0)
        score(b0, 0, s_a)
        weigh(0, s_a, p_a, f_a)
        score(b0, 1, s_b)

        def entry(j, carry):
            b = work[i * count + j]
            later = work[i * count + jnp.minimum(j + 1, n - 1)]
            arrived(later)
            mark = marks[b]
            many = jnp.concatenate([mark] * (QUAD // 16), axis=0)
            mark = mark.astype(F32)
            ones = jnp.concatenate(
                [jnp.where(row16 == 0, mark, 0.0), jnp.where(row16 == 1, mark, 0.0)], axis=1
            ).astype(BF)
            for g in range(rounds):
                here, there = slots[g % 2], slots[(g + 1) % 2]
                score(b if g + 2 < rounds else later, (g + 2) % rounds, here[0])
                mix(b, many, ones, g, here[1], here[2])
                weigh((g + 1) % rounds, there[0], there[1], there[2])
            return carry

        lax.fori_loop(0, n, entry, 0)

    if last:
        for q in range(quads):
            scaled = 1.0 / level[q, 2:4]
            for pair in range(2):
                mixed = total[q, pair * HD : (pair + 1) * HD, :] * scaled[pair : pair + 1]
                for side in range(2):
                    r = q * QUAD + (2 * pair + side) * HD
                    if r < width:
                        out_ref[r : r + HD, :] = mixed[:, side * tile : (side + 1) * tile].astype(BF)
    else:

        @pl.when((n > 0) | first)
        def _():
            levels[i] = level[...]
            totals[i] = total[...]
            for move in state_moves(i, False):
                move.start()

        @pl.when(i == tiles - 1)
        def _():
            for t in range(tiles):

                @pl.when((found[t] > 0) | first)
                def _():
                    for move in state_moves(t, False):
                        move.wait()


def attend(spans, queries, blocks, held, state, last, waits=()):
    width, tokens = queries.shape
    quads = -(-width // QUAD)
    count = len(blocks)
    tiles, prompts = spans[3].shape
    tile = tokens // tiles
    first = state is None
    setup = (count, first, last, held, len(waits), prompts, width, tokens, tiles)
    level, total = (quads, 4, 2 * tile), (quads, 2 * HD, 2 * tile)
    aliases = {}
    if last:
        outs = [jax.ShapeDtypeStruct((width, tokens), BF)]
        out_specs = [pl.BlockSpec((width, tile), lambda i: (0, i))]
    else:
        outs = [jax.ShapeDtypeStruct((tiles,) + shape, F32) for shape in (level, total)]
        out_specs = [anywhere()] * 2
        if not first:
            at = 5 + 2 * count + len(waits)
            aliases = {at: 0, at + 1: 1}
    keys = [block[0] for block in blocks]
    values = [block[1] for block in blocks]
    scratch = [
        pltpu.VMEM((count, quads, QUAD, QUAD), BF),
        pltpu.VMEM((count, quads * QUAD, QUAD), BF),
        pltpu.VMEM((count, 16, QUAD), BF),
        pltpu.VMEM((tiles, width, tile), BF),
        pltpu.VMEM((quads, QUAD, 2 * tile), BF),
        pltpu.VMEM((tiles,) + level, F32),
        pltpu.VMEM((tiles,) + total, F32),
        pltpu.VMEM(level, F32),
        pltpu.VMEM(total, F32),
    ]
    scratch += [pltpu.VMEM((STEP, 2 * QUAD, 2 * tile), F32)] * 2
    scratch += [pltpu.VMEM((STEP, 2 * QUAD, 2 * tile), BF)] * 2
    scratch += [pltpu.VMEM((STEP, 2, 2 * tile), F32)] * 2
    scratch += [
        pltpu.SMEM((count * tiles + 1,), jnp.int32),
        pltpu.SMEM((tiles,), jnp.int32),
        pltpu.SMEM((count,), jnp.int32),
        pltpu.SMEM((count,), jnp.int32),
        pltpu.SemaphoreType.DMA((count, 2)),
        pltpu.SemaphoreType.DMA((tiles, 5)),
    ]
    area = count * QUAD * tokens
    return pl.pallas_call(
        functools.partial(attend_kernel, setup),
        grid=(tiles,),
        in_specs=[smem()] * 4 + [anywhere()] * (1 + 2 * count + len(waits) + (0 if first else 2)),
        out_specs=out_specs,
        out_shape=outs,
        scratch_shapes=scratch,
        input_output_aliases=aliases,
        cost_estimate=cost(40 * area * width, 4 * width * tokens, area * width // HD),
        compiler_params=pltpu.CompilerParams(vmem_limit_bytes=ROOM),
        name="attend",
    )(
        *spans,
        queries,
        *keys,
        *values,
        *waits,
        *([] if first else state),
    )


def front_kernel(tokens_ref, *refs):
    sources, (own_ref, sent_ref), turned_hbm, refs = refs[:4], refs[4:6], refs[6:8], refs[8:]
    arrays, turned, (in_sems, out_sems) = refs[:4], refs[4:6], refs[6:]
    rows = lax.broadcasted_iota(jnp.int32, (QUAD, QUAD), 0)
    columns = lax.broadcasted_iota(jnp.int32, (QUAD, QUAD), 1)
    width, quads = arrays[0].shape[0], sent_ref.shape[0]
    every = quads // PARTS

    def move_in(n, part):
        at = part_rows(width, quads, part)
        return pltpu.make_async_copy(sources[n].at[at], arrays[n].at[at], in_sems.at[n, part])

    def move_out(n, part):
        at = pl.ds(part * every, every)
        return pltpu.make_async_copy(turned[n].at[at], turned_hbm[n].at[at], out_sems.at[n, part])

    for part in range(PARTS):
        for n in range(2):
            move_in(n, part).start()
    for n in range(2, 4):
        for part in range(PARTS):
            move_in(n, part).start()
    for n in range(2):
        used = QUAD if n else tokens_ref[lax.axis_index("tm")]
        for q in range(quads):
            if q % every == 0:
                move_in(2 + n, q // every).wait()
            turned[n][q] = turned_quad(quad_rows(arrays[2 + n], q, width), used, rows)
            if q % every == every - 1:
                move_out(n, q // every).start()
    for q in range(quads):
        if q % every == 0:
            for n in range(2):
                move_in(n, q // every).wait()
        lifted = jnp.maximum(quad_rows(arrays[0], q, width), 0)
        grown = lax.dot_general(
            quad_rows(arrays[1], q, width), lifted, (((1,), (1,)), ((), ())), preferred_element_type=F32
        )
        grown = jnp.where(rows // HD == columns // HD, grown, 0.0)
        folded = grown[0:HD] + grown[HD : 2 * HD] + grown[2 * HD : 3 * HD] + grown[3 * HD :]
        own_ref[q] = folded
        sent_ref[q] = folded.astype(BF)
    for n in range(2):
        for part in range(PARTS):
            move_out(n, part).wait()


def front(tokens, keys, values, prompt_keys, caption_keys):
    width = keys.shape[0]
    quads = -(-width // QUAD)
    arrays = (keys, values, prompt_keys, caption_keys)
    state, turned = (quads, HD, QUAD), (quads, QUAD, QUAD)
    return pl.pallas_call(
        front_kernel,
        in_specs=[smem()] + [anywhere()] * 4,
        out_specs=[vmem()] * 2 + [anywhere()] * 2,
        out_shape=[jax.ShapeDtypeStruct(state, F32), jax.ShapeDtypeStruct(state, BF)]
        + [jax.ShapeDtypeStruct(turned, BF)] * 2,
        scratch_shapes=[pltpu.VMEM(array.shape, BF) for array in arrays]
        + [pltpu.VMEM(turned, BF)] * 2
        + [pltpu.SemaphoreType.DMA((4, PARTS)), pltpu.SemaphoreType.DMA((2, PARTS))],
        cost_estimate=cost(8 * width * QUAD * keys.shape[1], 4 * keys.size),
        compiler_params=pltpu.CompilerParams(vmem_limit_bytes=ROOM),
        name="front",
    )(tokens, *arrays)


def lower_sum(hop, prior, partners):
    digit = lax.axis_index("tm") // hop % (len(partners) + 1)
    for d, partner in enumerate(partners, 1):
        prior = prior + jnp.where((digit ^ d) < digit, partner.astype(F32), 0.0)
    return prior


def digit_step(own_ref, partners, sent_out):
    for q in range(sent_out.shape[0]):
        whole = own_ref[q]
        for partner in partners:
            whole = whole + partner[q].astype(F32)
        sent_out[q] = whole.astype(BF)


def digit_kernel(own_ref, *refs):
    digit_step(own_ref, refs[:-2], refs[-1])


def digit_sums(own, partners, token):
    return pl.pallas_call(
        digit_kernel,
        in_specs=[vmem()] * (1 + len(partners)) + [anywhere()],
        out_specs=vmem(),
        out_shape=jax.ShapeDtypeStruct(own.shape, BF),
        cost_estimate=cost(0, 8 * own.size),
        compiler_params=pltpu.CompilerParams(vmem_limit_bytes=ROOM),
        name="digit_sums",
    )(own, *partners, token)


def digits_of(size):
    hop, digits = 1, []
    while hop < size:
        radix = LAYER if hop == 1 and size % LAYER == 0 else 2
        digits.append((hop, radix))
        hop *= radix
    return digits


def swapped(block, hop, radix):
    size = lax.axis_size("tm")
    return [sent(block, [(i, i ^ (d * hop)) for i in range(size)]) for d in range(1, radix)]


def norm_kernel(digits, queries_hbm, gain_hbm, own_hbm, *refs):
    count = sum(radix - 1 for _, radix in digits)
    partners_hbm, refs = refs[:count], refs[count + 1 :]
    out_hbm, queries, raw, out, gain_ref, own_ref, partners, in_sems, out_sems, state_sems = refs
    rows = lax.broadcasted_iota(jnp.int32, (QUAD, QUAD), 0) // HD
    columns = lax.broadcasted_iota(jnp.int32, (QUAD, QUAD), 1) // HD
    width = queries.shape[0]
    quads, tokens = raw.shape[0], raw.shape[2]
    every = quads // PARTS

    def move_in(part):
        at = part_rows(width, quads, part)
        return pltpu.make_async_copy(queries_hbm.at[at], queries.at[at], in_sems.at[part])

    def move_out(part):
        at = part_rows(width, quads, part)
        return pltpu.make_async_copy(out.at[at], out_hbm.at[at], out_sems.at[part])

    moves = [
        pltpu.make_async_copy(own_hbm, own_ref, state_sems.at[count]),
        pltpu.make_async_copy(gain_hbm, gain_ref, state_sems.at[count + 1]),
    ]
    for n in range(count):
        moves.append(pltpu.make_async_copy(partners_hbm[n], partners.at[n], state_sems.at[n]))
    for move in moves:
        move.start()
    for part in range(PARTS):
        move_in(part).start()
    for move in moves:
        move.wait()
    squares = jnp.zeros((1, tokens), F32)
    for q in range(quads):
        if q % every == 0:
            move_in(q // every).wait()
        whole, first = own_ref[q], 0
        for hop, radix in digits:
            whole = lower_sum(hop, whole, [partners[first + n, q] for n in range(radix - 1)])
            first += radix - 1
        whole = whole.astype(BF).astype(F32)
        wide = jnp.where(rows == columns, jnp.concatenate([whole] * (QUAD // HD), axis=0), 0.0).astype(BF)
        lifted = jnp.maximum(quad_rows(queries, q, width), 0)
        part = jnp.dot(wide, lifted, preferred_element_type=F32)
        raw[q] = part
        squares = squares + jnp.sum(part * part, axis=0, keepdims=True)
    factor = lax.rsqrt(squares / width + 1e-05)
    for q in range(quads):
        size = min(QUAD, width - q * QUAD)
        gain = gain_ref[:, q * QUAD : q * QUAD + size]
        if size < QUAD:
            gain = jnp.concatenate([gain, jnp.zeros((1, QUAD - size), F32)], axis=1)
        gains = jnp.transpose(jnp.broadcast_to(gain, (QUAD, QUAD)))
        gains = jnp.concatenate([gains] * (tokens // QUAD), axis=1)
        mixed = (raw[q] * factor * gains).astype(BF)
        out[q * QUAD : q * QUAD + size, :] = mixed[:size]
        if q % every == every - 1:
            move_out(q // every).start()
    for part in range(PARTS):
        move_out(part).wait()


def self_mix(queries, own, gain, partners, digits, token):
    width, tokens = queries.shape
    quads = -(-width // QUAD)
    return pl.pallas_call(
        functools.partial(norm_kernel, tuple(digits)),
        in_specs=[anywhere()] * (4 + len(partners)),
        out_specs=anywhere(),
        out_shape=jax.ShapeDtypeStruct((width, tokens), BF),
        scratch_shapes=[
            pltpu.VMEM((width, tokens), BF),
            pltpu.VMEM((quads, QUAD, tokens), F32),
            pltpu.VMEM((width, tokens), BF),
            pltpu.VMEM(gain.shape, F32),
            pltpu.VMEM(own.shape, F32),
            pltpu.VMEM((len(partners),) + own.shape, BF),
            pltpu.SemaphoreType.DMA((PARTS,)),
            pltpu.SemaphoreType.DMA((PARTS,)),
            pltpu.SemaphoreType.DMA((len(partners) + 2,)),
        ],
        cost_estimate=cost(8 * width * QUAD * tokens, 4 * width * tokens),
        compiler_params=pltpu.CompilerParams(vmem_limit_bytes=ROOM),
        name="self_mix",
    )(queries, gain, own, *partners, token)


def sent(block, pairs):
    return lax.ppermute(block, "tm", pairs)


def local(
    queries,
    keys,
    values,
    cross_queries,
    prompt_keys,
    prompt_values,
    caption_keys,
    caption_values,
    span_start,
    span_end,
    prompt_tokens,
    region_mask,
    out_gain,
):
    size = lax.axis_size("tm")
    slots, width = prompt_keys.shape[1:]
    spans = (span_start, span_end, prompt_tokens, jnp.transpose(region_mask))
    turned = lambda block: jnp.transpose(block.reshape(slots, width))
    queries_t = jnp.transpose(cross_queries)
    call = functools.partial(attend, spans, queries_t)

    bases = [LAYER * z for z in range(size // LAYER)]
    beside = [(i, i ^ 1) for i in range(size)]
    up = [(i, (i + LAYER) % size) for i in range(size)]
    swap = [(i, i ^ 2) for i in range(size)]
    onward = [(i, i + LAYER - 1) for i in range(size) if i % 2 and i + LAYER - 1 < size]
    further = [(i, i + 1) for i in range(size) if i % 2 and i + 1 < size]
    spot = lambda c: c % LAYER
    pick = lambda c, *ways: functools.reduce(
        lambda rest, way: jnp.where(spot(c) == way[0], c - way[1], rest), ways, -1
    )
    digits = digits_of(size)

    own_v = turned(prompt_values)
    up_v = sent(own_v, up)
    own_v_beside = sent(own_v, beside)
    own_sums, going, own_k, caption_k = front(
        prompt_tokens,
        jnp.transpose(keys),
        jnp.transpose(values),
        turned(prompt_keys),
        jnp.transpose(caption_keys),
    )
    partners = swapped(going, *digits[0])
    gain_row = out_gain.reshape(1, width)
    state = call([(caption_k, jnp.transpose(caption_values))], lambda c: [None], None, False, waits=[going])

    summed = [own_sums, *partners] if len(digits) > 2 else []
    across_v, up_v, *going = to_cross(own_v, up_v, state[0], own_v_beside, *partners, states=summed)
    swap_v = sent(across_v, swap)
    (late_k,) = after([own_k], state[0])
    up_k = sent(late_k, up)
    own_k_beside = sent(late_k, beside)
    up_v_beside = sent(up_v, beside)
    for place, digit in enumerate(digits[1:-1]):
        if place:
            going = [digit_sums(own_sums, partners, across_v)]
        partners += swapped(going[0], *digit)
    state = call(
        [(late_k, own_v), (own_k_beside, own_v_beside)],
        lambda c: [c, pick(c, (1, 1), (3, 1))],
        state,
        False,
        waits=[across_v, gain_row],
    )

    (swap_v,) = after([swap_v], state[0])
    summed = [own_sums, *partners] if len(digits) > 1 else []
    across_k, up_k, *going = to_cross(late_k, up_k, state[0], up_v_beside, *partners, states=summed)
    swap_k = sent(across_k, swap)
    far_k = sent(up_k, further)
    far_v = sent(swap_v, onward)
    up_k_beside = sent(up_k, beside)
    final = swapped(going[0], *digits[-1]) if len(digits) > 1 else []
    state = call(
        [(up_k, up_v), (up_k_beside, up_v_beside)],
        lambda c: [c - LAYER, pick(c, (0, 3), (2, 3), (1, 5), (3, 5))],
        state,
        False,
        waits=[across_k],
    )

    swap_k, swap_v = after([swap_k, swap_v], state[0], far_v, *final)
    swap_k_beside = sent(swap_k, beside)
    swap_v_beside = sent(swap_v, beside)
    self_mixed = self_mix(jnp.transpose(queries), own_sums, gain_row, partners + final, digits, swap_k)
    cross_mixed = call(
        [(swap_k, swap_v), (swap_k_beside, swap_v_beside), (far_k, far_v)],
        lambda c: [
            c - 2,
            pick(c, (0, 1), (1, 3), (2, 1), (3, 3)),
            pick(c, (0, 5), (2, 5)),
        ],
        state,
        True,
        waits=[self_mixed],
    )[0]
    return (jnp.transpose(self_mixed), jnp.transpose(cross_mixed))


def solution(mesh):
    in_specs = (
        P(("groups", "tm"), None),
        P(("groups", "tm"), None),
        P(("groups", "tm"), None),
        P(("groups", "tm"), None),
        P(("groups", "tm"), None, None),
        P(("groups", "tm"), None, None),
        P("groups", None),
        P("groups", None),
        P("groups"),
        P("groups"),
        P("groups"),
        P("groups", None),
        P(),
    )
    out_specs = (P(("groups", "tm"), None), P(("groups", "tm"), None))
    return jax.shard_map(local, mesh=mesh, in_specs=in_specs, out_specs=out_specs, check_vma=False)
```

```python
import functools
import math

import jax
import jax.numpy as jnp
from jax import lax
from jax.experimental import pallas as pl
from jax.experimental.pallas import tpu as pltpu
from jax.sharding import PartitionSpec as P

HD = 32
SPAN = 6
QUAD = 128
LAYER = 4
BF = jnp.bfloat16
F32 = jnp.float32
EMPTY = -1e30
STEP = 3
PARTS = 3
COPIES = 2
ROOM = 66_900_000


def vmem():
    return pl.BlockSpec(memory_space=pltpu.VMEM)


def smem():
    return pl.BlockSpec(memory_space=pltpu.SMEM)


def anywhere():
    return pl.BlockSpec(memory_space=pl.ANY)


def cost(flops, moved, exps=0):
    flops, moved = flops // 1000, moved // 1000
    return pl.CostEstimate(flops=flops, bytes_accessed=moved, transcendentals=exps)


def quad_rows(ref, q, width):
    if (q + 1) * QUAD <= width:
        return ref[q * QUAD : (q + 1) * QUAD, :]
    part = ref[q * QUAD : width, :]
    fill = jnp.zeros(((q + 1) * QUAD - width, part.shape[1]), part.dtype)
    return jnp.concatenate([part, fill], axis=0)


def part_rows(width, quads, part):
    low = part * (quads // PARTS) * QUAD
    return pl.ds(low, min(quads // PARTS * QUAD, width - low))


def turned_quad(keys, used, rows):
    turned = jnp.transpose(keys.astype(F32))
    return jnp.where(rows < used, turned, turned[0:1, :]).astype(BF)


def no_kernel(*refs):
    del refs


def after(blocks, *tokens):
    return pl.pallas_call(
        no_kernel,
        in_specs=[anywhere()] * (len(blocks) + len(tokens)),
        out_specs=[anywhere()] * len(blocks),
        out_shape=[jax.ShapeDtypeStruct(block.shape, block.dtype) for block in blocks],
        input_output_aliases={place: place for place in range(len(blocks))},
        cost_estimate=cost(0, 0),
        name="after",
    )(*blocks, *tokens)


def across_kernel(waits, count, own_hbm, up_hbm, *refs):
    states_hbm, refs = refs[waits : waits + count], refs[waits + count :]
    across_hbm, _, *refs = refs
    if count:
        sent_hbm, held, in_sems, out_sems, own_state, partners, sent_here, state_sems = refs
    else:
        held, in_sems, out_sems = refs
    lower = lax.axis_index("tm") % LAYER < LAYER // 2
    piece = own_hbm.shape[0] // COPIES

    def move_in(source, part):
        at = pl.ds(part * piece, piece)
        return pltpu.make_async_copy(source.at[at], held.at[at], in_sems.at[part])

    def move_out(part):
        at = pl.ds(part * piece, piece)
        return pltpu.make_async_copy(held.at[at], across_hbm.at[at], out_sems.at[part])

    @pl.when(lower)
    def _():
        for part in range(COPIES):
            move_in(own_hbm, part).start()

    @pl.when(jnp.logical_not(lower))
    def _():
        for part in range(COPIES):
            move_in(up_hbm, part).start()

    moves = []
    for n in range(count):
        into = partners.at[n - 1] if n else own_state
        moves.append(pltpu.make_async_copy(states_hbm[n], into, state_sems.at[n]))
    for move in moves:
        move.start()
    for part in range(COPIES):
        move_in(up_hbm, part).wait()
        move_out(part).start()
    for move in moves:
        move.wait()
    if count:
        digit_step(own_state, [partners.at[n] for n in range(count - 1)], sent_here)
        away = pltpu.make_async_copy(sent_here, sent_hbm, state_sems.at[count])
        away.start()
        away.wait()
    for part in range(COPIES):
        move_out(part).wait()


def to_cross(own, up, *tokens, states=()):
    shape = jax.ShapeDtypeStruct(own.shape, own.dtype)
    outs = [shape, shape]
    scratch = [
        pltpu.VMEM(own.shape, own.dtype),
        pltpu.SemaphoreType.DMA((COPIES,)),
        pltpu.SemaphoreType.DMA((COPIES,)),
    ]
    if states:
        state = states[0].shape
        outs.append(jax.ShapeDtypeStruct(state, BF))
        scratch += [
            pltpu.VMEM(state, F32),
            pltpu.VMEM((len(states) - 1,) + state, BF),
            pltpu.VMEM(state, BF),
            pltpu.SemaphoreType.DMA((len(states) + 1,)),
        ]
    return pl.pallas_call(
        functools.partial(across_kernel, len(tokens), len(states)),
        in_specs=[anywhere()] * (2 + len(tokens) + len(states)),
        out_specs=[anywhere()] * len(outs),
        out_shape=outs,
        input_output_aliases={1: 1},
        scratch_shapes=scratch,
        cost_estimate=cost(0, 4 * own.size),
        compiler_params=pltpu.CompilerParams(vmem_limit_bytes=ROOM),
        name="to_cross",
    )(own, up, *tokens, *states)


def attend_kernel(setup, start_ref, end_ref, tokens_ref, region_ref, *refs):
    count, first, last, held, waits, prompts, width, tokens, tiles = setup
    tile = tokens // tiles
    quads = -(-width // QUAD)
    rounds = quads // STEP
    query_hbm, refs = refs[0], refs[1:]
    key_hbm, refs = refs[:count], refs[count:]
    value_hbm, refs = refs[:count], refs[count + waits :]
    if not first:
        state_in, refs = refs[:2], refs[2:]
    if last:
        out_ref, refs = refs[0], refs[1:]
    else:
        state_out, refs = refs[:2], refs[2:]
    keys, vals, marks, queries, spread, levels, totals, level, total, *refs = refs
    s_a, s_b, p_a, p_b, f_a, f_b, work, found, used, ready, sems, tile_sems = refs
    scale = math.log2(math.e) / math.sqrt(HD)
    none = jnp.zeros((HD, tile), BF)
    i = pl.program_id(0)

    def copies(b, at):
        return (
            pltpu.make_async_copy(key_hbm[b], keys.at[at], sems.at[at, 0]),
            pltpu.make_async_copy(value_hbm[b], vals.at[at, pl.ds(0, width)], sems.at[at, 1]),
        )

    def query_move(t):
        columns = pl.ds(t * tile, tile)
        return pltpu.make_async_copy(query_hbm.at[:, columns], queries.at[t], tile_sems.at[t, 0])

    def state_moves(t, into):
        for place, held_here in enumerate((levels, totals)):
            if into:
                yield pltpu.make_async_copy(state_in[place].at[t], held_here.at[t], tile_sems.at[t, 1 + place])
            else:
                yield pltpu.make_async_copy(held_here.at[t], state_out[place].at[t], tile_sems.at[t, 3 + place])

    @pl.when(i == 0)
    def _():
        if first:
            for t in range(tiles):
                query_move(t).start()
        if last:
            for move in state_moves(0, True):
                move.start()
        stretch = lax.axis_index("tm")
        wanted = []
        lengths = [jnp.int32(0)] * tiles
        for b, owner in enumerate(held(stretch)):
            if owner is None:
                seen = [jnp.int32(1)] * tiles
                used[b] = jnp.int32(QUAD)
            else:
                safe = jnp.clip(owner, 0, prompts - 1)
                covers = (
                    (owner >= 0)
                    & (start_ref[safe] <= stretch)
                    & (stretch < end_ref[safe])
                )
                used[b] = tokens_ref[safe]
                seen = [
                    (covers & (region_ref[t, safe] == 1)).astype(jnp.int32)
                    for t in range(tiles)
                ]
            for t in range(tiles):
                work[t * count + lengths[t]] = jnp.int32(b)
                lengths[t] = lengths[t] + seen[t]
            wanted.append(functools.reduce(jnp.add, seen) > 0)
            ready[b] = jnp.int32(0)

            @pl.when(wanted[b])
            def _():
                for move in copies(b, b):
                    move.start()

        for t in range(tiles):
            found[t] = lengths[t]

            if not first:

                @pl.when(lengths[t] > 0)
                def _():
                    query_move(t).start()

            if not first and not (last and t == 0):

                @pl.when((lengths[t] > 0) | last)
                def _():
                    for move in state_moves(t, True):
                        move.start()

        for q in range(quads):
            for h in range(QUAD // HD):
                off = (1 - h % 2) * tile
                spread[q, h * HD : (h + 1) * HD, off : off + tile] = none
        lanes = lax.broadcasted_iota(jnp.int32, (16, QUAD), 1)
        for b in range(count):
            marks[b] = jnp.where(lanes < used[b], 1.0, 0.0).astype(BF)
            if width < quads * QUAD:
                vals[b, width:, :] = jnp.zeros((quads * QUAD - width, QUAD), BF)

    def arrived(b):
        @pl.when(ready[b] == 0)
        def _():
            for move in copies(0, b):
                move.wait()
            ready[b] = jnp.int32(1)

    low_half = lax.broadcasted_iota(jnp.int32, (QUAD, QUAD), 1) < QUAD // 2
    row16 = lax.broadcasted_iota(jnp.int32, (16, QUAD), 0)
    zeros = jnp.zeros((QUAD // 2, QUAD), BF)

    def score(b, g, s_to):
        for k in range(STEP):
            block = keys[b, g * STEP + k].astype(F32)
            both = jnp.concatenate(
                [jnp.where(low_half, block, 0.0), jnp.where(low_half, 0.0, block)], axis=0
            ).astype(BF)
            s_to[k] = jnp.dot(both, spread[g * STEP + k], preferred_element_type=F32)

    def weigh(g, s_from, p_to, f_to):
        for k in range(STEP):
            q = g * STEP + k
            for pair in range(2):
                at = slice(pair * QUAD, (pair + 1) * QUAD)
                part = s_from[k, at, :]
                old = level[q, pair : pair + 1]
                new = jnp.maximum(old, jnp.max(part, axis=0, keepdims=True))
                p_to[k, at, :] = jnp.exp2((part - new) * scale).astype(BF)
                f_to[k, pair : pair + 1] = jnp.exp2((old - new) * scale)
                level[q, pair : pair + 1] = new

    def mix(b, many, ones, g, p_from, f_from):
        for k in range(STEP):
            q = g * STEP + k
            v = vals[b, q * QUAD : (q + 1) * QUAD, :] * many
            left = jnp.concatenate(
                [
                    jnp.concatenate([v[: QUAD // 2], zeros], axis=1),
                    jnp.concatenate([zeros, v[QUAD // 2 :]], axis=1),
                    ones,
                ],
                axis=0,
            )
            out = jnp.dot(left, p_from[k], preferred_element_type=F32)
            factor = f_from[k]
            level[q, 2:4] = level[q, 2:4] * factor + out[QUAD : QUAD + 2]
            for pair in range(2):
                r = pair * 2 * HD
                added = jnp.concatenate([out[r : r + HD, :tile], out[r + HD : r + 2 * HD, tile:]], axis=1)
                at = slice(pair * HD, (pair + 1) * HD)
                total[q, at, :] = total[q, at, :] * factor[pair : pair + 1] + added

    slots = [(s_a, p_a, f_a), (s_b, p_b, f_b)]
    n = found[i]
    if first:
        level[:, 0:2] = jnp.full((quads, 2, 2 * tile), EMPTY, F32)
        level[:, 2:4] = jnp.zeros((quads, 2, 2 * tile), F32)
        total[...] = jnp.zeros(total.shape, F32)
    else:

        @pl.when((n > 0) | last)
        def _():
            for move in state_moves(i, True):
                move.wait()
            level[...] = levels[i]
            total[...] = totals[i]

    @pl.when(n > 0)
    def _():
        query_move(i).wait()
        for r in range(0, quads * QUAD, HD):
            q, h = r // QUAD, r % QUAD // HD
            on = h % 2 * tile
            piece = queries[i, r : r + HD, :] if r < width else none
            spread[q, h * HD : (h + 1) * HD, on : on + tile] = piece
        b0 = work[i * count]
        arrived(b0)
        score(b0, 0, s_a)
        weigh(0, s_a, p_a, f_a)
        score(b0, 1, s_b)

        def entry(j, carry):
            b = work[i * count + j]
            later = work[i * count + jnp.minimum(j + 1, n - 1)]
            arrived(later)
            mark = marks[b]
            many = jnp.concatenate([mark] * (QUAD // 16), axis=0)
            mark = mark.astype(F32)
            ones = jnp.concatenate(
                [jnp.where(row16 == 0, mark, 0.0), jnp.where(row16 == 1, mark, 0.0)], axis=1
            ).astype(BF)
            for g in range(rounds):
                here, there = slots[g % 2], slots[(g + 1) % 2]
                score(b if g + 2 < rounds else later, (g + 2) % rounds, here[0])
                mix(b, many, ones, g, here[1], here[2])
                weigh((g + 1) % rounds, there[0], there[1], there[2])
            return carry

        lax.fori_loop(0, n, entry, 0)

    if last:
        for q in range(quads):
            scaled = 1.0 / level[q, 2:4]
            for pair in range(2):
                mixed = total[q, pair * HD : (pair + 1) * HD, :] * scaled[pair : pair + 1]
                for side in range(2):
                    r = q * QUAD + (2 * pair + side) * HD
                    if r < width:
                        out_ref[r : r + HD, :] = mixed[:, side * tile : (side + 1) * tile].astype(BF)
    else:

        @pl.when((n > 0) | first)
        def _():
            levels[i] = level[...]
            totals[i] = total[...]
            for move in state_moves(i, False):
                move.start()

        @pl.when(i == tiles - 1)
        def _():
            for t in range(tiles):

                @pl.when((found[t] > 0) | first)
                def _():
                    for move in state_moves(t, False):
                        move.wait()


def attend(spans, queries, blocks, held, state, last, waits=()):
    width, tokens = queries.shape
    quads = -(-width // QUAD)
    count = len(blocks)
    tiles, prompts = spans[3].shape
    tile = tokens // tiles
    first = state is None
    setup = (count, first, last, held, len(waits), prompts, width, tokens, tiles)
    level, total = (quads, 4, 2 * tile), (quads, 2 * HD, 2 * tile)
    aliases = {}
    if last:
        outs = [jax.ShapeDtypeStruct((width, tokens), BF)]
        out_specs = [pl.BlockSpec((width, tile), lambda i: (0, i))]
    else:
        outs = [jax.ShapeDtypeStruct((tiles,) + shape, F32) for shape in (level, total)]
        out_specs = [anywhere()] * 2
        if not first:
            at = 5 + 2 * count + len(waits)
            aliases = {at: 0, at + 1: 1}
    keys = [block[0] for block in blocks]
    values = [block[1] for block in blocks]
    scratch = [
        pltpu.VMEM((count, quads, QUAD, QUAD), BF),
        pltpu.VMEM((count, quads * QUAD, QUAD), BF),
        pltpu.VMEM((count, 16, QUAD), BF),
        pltpu.VMEM((tiles, width, tile), BF),
        pltpu.VMEM((quads, QUAD, 2 * tile), BF),
        pltpu.VMEM((tiles,) + level, F32),
        pltpu.VMEM((tiles,) + total, F32),
        pltpu.VMEM(level, F32),
        pltpu.VMEM(total, F32),
    ]
    scratch += [pltpu.VMEM((STEP, 2 * QUAD, 2 * tile), F32)] * 2
    scratch += [pltpu.VMEM((STEP, 2 * QUAD, 2 * tile), BF)] * 2
    scratch += [pltpu.VMEM((STEP, 2, 2 * tile), F32)] * 2
    scratch += [
        pltpu.SMEM((count * tiles + 1,), jnp.int32),
        pltpu.SMEM((tiles,), jnp.int32),
        pltpu.SMEM((count,), jnp.int32),
        pltpu.SMEM((count,), jnp.int32),
        pltpu.SemaphoreType.DMA((count, 2)),
        pltpu.SemaphoreType.DMA((tiles, 5)),
    ]
    area = count * QUAD * tokens
    return pl.pallas_call(
        functools.partial(attend_kernel, setup),
        grid=(tiles,),
        in_specs=[smem()] * 4 + [anywhere()] * (1 + 2 * count + len(waits) + (0 if first else 2)),
        out_specs=out_specs,
        out_shape=outs,
        scratch_shapes=scratch,
        input_output_aliases=aliases,
        cost_estimate=cost(40 * area * width, 4 * width * tokens, area * width // HD),
        compiler_params=pltpu.CompilerParams(vmem_limit_bytes=ROOM),
        name="attend",
    )(
        *spans,
        queries,
        *keys,
        *values,
        *waits,
        *([] if first else state),
    )


def front_kernel(tokens_ref, *refs):
    sources, (own_ref, sent_ref), turned_hbm, refs = refs[:4], refs[4:6], refs[6:8], refs[8:]
    arrays, turned, (in_sems, out_sems) = refs[:4], refs[4:6], refs[6:]
    rows = lax.broadcasted_iota(jnp.int32, (QUAD, QUAD), 0)
    columns = lax.broadcasted_iota(jnp.int32, (QUAD, QUAD), 1)
    width, quads = arrays[0].shape[0], sent_ref.shape[0]
    every = quads // PARTS

    def move_in(n, part):
        at = part_rows(width, quads, part)
        return pltpu.make_async_copy(sources[n].at[at], arrays[n].at[at], in_sems.at[n, part])

    def move_out(n, part):
        at = pl.ds(part * every, every)
        return pltpu.make_async_copy(turned[n].at[at], turned_hbm[n].at[at], out_sems.at[n, part])

    for part in range(PARTS):
        for n in range(2):
            move_in(n, part).start()
    for n in range(2, 4):
        for part in range(PARTS):
            move_in(n, part).start()
    for n in range(2):
        used = QUAD if n else tokens_ref[lax.axis_index("tm")]
        for q in range(quads):
            if q % every == 0:
                move_in(2 + n, q // every).wait()
            turned[n][q] = turned_quad(quad_rows(arrays[2 + n], q, width), used, rows)
            if q % every == every - 1:
                move_out(n, q // every).start()
    for q in range(quads):
        if q % every == 0:
            for n in range(2):
                move_in(n, q // every).wait()
        lifted = jnp.maximum(quad_rows(arrays[0], q, width), 0)
        grown = lax.dot_general(
            quad_rows(arrays[1], q, width), lifted, (((1,), (1,)), ((), ())), preferred_element_type=F32
        )
        grown = jnp.where(rows // HD == columns // HD, grown, 0.0)
        folded = grown[0:HD] + grown[HD : 2 * HD] + grown[2 * HD : 3 * HD] + grown[3 * HD :]
        own_ref[q] = folded
        sent_ref[q] = folded.astype(BF)
    for n in range(2):
        for part in range(PARTS):
            move_out(n, part).wait()


def front(tokens, keys, values, prompt_keys, caption_keys):
    width = keys.shape[0]
    quads = -(-width // QUAD)
    arrays = (keys, values, prompt_keys, caption_keys)
    state, turned = (quads, HD, QUAD), (quads, QUAD, QUAD)
    return pl.pallas_call(
        front_kernel,
        in_specs=[smem()] + [anywhere()] * 4,
        out_specs=[vmem()] * 2 + [anywhere()] * 2,
        out_shape=[jax.ShapeDtypeStruct(state, F32), jax.ShapeDtypeStruct(state, BF)]
        + [jax.ShapeDtypeStruct(turned, BF)] * 2,
        scratch_shapes=[pltpu.VMEM(array.shape, BF) for array in arrays]
        + [pltpu.VMEM(turned, BF)] * 2
        + [pltpu.SemaphoreType.DMA((4, PARTS)), pltpu.SemaphoreType.DMA((2, PARTS))],
        cost_estimate=cost(8 * width * QUAD * keys.shape[1], 4 * keys.size),
        compiler_params=pltpu.CompilerParams(vmem_limit_bytes=ROOM),
        name="front",
    )(tokens, *arrays)


def lower_sum(hop, prior, partners):
    digit = lax.axis_index("tm") // hop % (len(partners) + 1)
    for d, partner in enumerate(partners, 1):
        prior = prior + jnp.where((digit ^ d) < digit, partner.astype(F32), 0.0)
    return prior


def digit_step(own_ref, partners, sent_out):
    for q in range(sent_out.shape[0]):
        whole = own_ref[q]
        for partner in partners:
            whole = whole + partner[q].astype(F32)
        sent_out[q] = whole.astype(BF)


def digit_kernel(own_ref, *refs):
    digit_step(own_ref, refs[:-2], refs[-1])


def digit_sums(own, partners, token):
    return pl.pallas_call(
        digit_kernel,
        in_specs=[vmem()] * (1 + len(partners)) + [anywhere()],
        out_specs=vmem(),
        out_shape=jax.ShapeDtypeStruct(own.shape, BF),
        cost_estimate=cost(0, 8 * own.size),
        compiler_params=pltpu.CompilerParams(vmem_limit_bytes=ROOM),
        name="digit_sums",
    )(own, *partners, token)


def digits_of(size):
    hop, digits = 1, []
    while hop < size:
        radix = LAYER if hop == 1 and size % LAYER == 0 else 2
        digits.append((hop, radix))
        hop *= radix
    return digits


def swapped(block, hop, radix):
    size = lax.axis_size("tm")
    return [sent(block, [(i, i ^ (d * hop)) for i in range(size)]) for d in range(1, radix)]


def norm_kernel(digits, queries_hbm, gain_hbm, own_hbm, *refs):
    count = sum(radix - 1 for _, radix in digits)
    partners_hbm, refs = refs[:count], refs[count + 1 :]
    out_hbm, queries, raw, out, gain_ref, own_ref, partners, in_sems, out_sems, state_sems = refs
    rows = lax.broadcasted_iota(jnp.int32, (QUAD, QUAD), 0) // HD
    columns = lax.broadcasted_iota(jnp.int32, (QUAD, QUAD), 1) // HD
    width = queries.shape[0]
    quads, tokens = raw.shape[0], raw.shape[2]
    every = quads // PARTS

    def move_in(part):
        at = part_rows(width, quads, part)
        return pltpu.make_async_copy(queries_hbm.at[at], queries.at[at], in_sems.at[part])

    def move_out(part):
        at = part_rows(width, quads, part)
        return pltpu.make_async_copy(out.at[at], out_hbm.at[at], out_sems.at[part])

    moves = [
        pltpu.make_async_copy(own_hbm, own_ref, state_sems.at[count]),
        pltpu.make_async_copy(gain_hbm, gain_ref, state_sems.at[count + 1]),
    ]
    for n in range(count):
        moves.append(pltpu.make_async_copy(partners_hbm[n], partners.at[n], state_sems.at[n]))
    for move in moves:
        move.start()
    for part in range(PARTS):
        move_in(part).start()
    for move in moves:
        move.wait()
    squares = jnp.zeros((1, tokens), F32)
    for q in range(quads):
        if q % every == 0:
            move_in(q // every).wait()
        whole, first = own_ref[q], 0
        for hop, radix in digits:
            whole = lower_sum(hop, whole, [partners[first + n, q] for n in range(radix - 1)])
            first += radix - 1
        whole = whole.astype(BF).astype(F32)
        wide = jnp.where(rows == columns, jnp.concatenate([whole] * (QUAD // HD), axis=0), 0.0).astype(BF)
        lifted = jnp.maximum(quad_rows(queries, q, width), 0)
        part = jnp.dot(wide, lifted, preferred_element_type=F32)
        raw[q] = part
        squares = squares + jnp.sum(part * part, axis=0, keepdims=True)
    factor = lax.rsqrt(squares / width + 1e-05)
    for q in range(quads):
        size = min(QUAD, width - q * QUAD)
        gain = gain_ref[:, q * QUAD : q * QUAD + size]
        if size < QUAD:
            gain = jnp.concatenate([gain, jnp.zeros((1, QUAD - size), F32)], axis=1)
        gains = jnp.transpose(jnp.broadcast_to(gain, (QUAD, QUAD)))
        gains = jnp.concatenate([gains] * (tokens // QUAD), axis=1)
        mixed = (raw[q] * factor * gains).astype(BF)
        out[q * QUAD : q * QUAD + size, :] = mixed[:size]
        if q % every == every - 1:
            move_out(q // every).start()
    for part in range(PARTS):
        move_out(part).wait()


def self_mix(queries, own, gain, partners, digits, token):
    width, tokens = queries.shape
    quads = -(-width // QUAD)
    return pl.pallas_call(
        functools.partial(norm_kernel, tuple(digits)),
        in_specs=[anywhere()] * (4 + len(partners)),
        out_specs=anywhere(),
        out_shape=jax.ShapeDtypeStruct((width, tokens), BF),
        scratch_shapes=[
            pltpu.VMEM((width, tokens), BF),
            pltpu.VMEM((quads, QUAD, tokens), F32),
            pltpu.VMEM((width, tokens), BF),
            pltpu.VMEM(gain.shape, F32),
            pltpu.VMEM(own.shape, F32),
            pltpu.VMEM((len(partners),) + own.shape, BF),
            pltpu.SemaphoreType.DMA((PARTS,)),
            pltpu.SemaphoreType.DMA((PARTS,)),
            pltpu.SemaphoreType.DMA((len(partners) + 2,)),
        ],
        cost_estimate=cost(8 * width * QUAD * tokens, 4 * width * tokens),
        compiler_params=pltpu.CompilerParams(vmem_limit_bytes=ROOM),
        name="self_mix",
    )(queries, gain, own, *partners, token)


def sent(block, pairs):
    return lax.ppermute(block, "tm", pairs)


def local(
    queries,
    keys,
    values,
    cross_queries,
    prompt_keys,
    prompt_values,
    caption_keys,
    caption_values,
    span_start,
    span_end,
    prompt_tokens,
    region_mask,
    out_gain,
):
    size = lax.axis_size("tm")
    slots, width = prompt_keys.shape[1:]
    spans = (span_start, span_end, prompt_tokens, jnp.transpose(region_mask))
    turned = lambda block: jnp.transpose(block.reshape(slots, width))
    queries_t = jnp.transpose(cross_queries)
    call = functools.partial(attend, spans, queries_t)

    bases = [LAYER * z for z in range(size // LAYER)]
    beside = [(i, i ^ 1) for i in range(size)]
    up = [(i, (i + LAYER) % size) for i in range(size)]
    swap = [(i, i ^ 2) for i in range(size)]
    onward = [(i, i + LAYER - 1) for i in range(size) if i % 2 and i + LAYER - 1 < size]
    further = [(i, i + 1) for i in range(size) if i % 2 and i + 1 < size]
    spot = lambda c: c % LAYER
    pick = lambda c, *ways: functools.reduce(
        lambda rest, way: jnp.where(spot(c) == way[0], c - way[1], rest), ways, -1
    )
    digits = digits_of(size)

    own_v = turned(prompt_values)
    up_v = sent(own_v, up)
    own_v_beside = sent(own_v, beside)
    own_sums, going, own_k, caption_k = front(
        prompt_tokens,
        jnp.transpose(keys),
        jnp.transpose(values),
        turned(prompt_keys),
        jnp.transpose(caption_keys),
    )
    partners = swapped(going, *digits[0])
    gain_row = out_gain.reshape(1, width)
    state = call([(caption_k, jnp.transpose(caption_values))], lambda c: [None], None, False, waits=[going])

    summed = [own_sums, *partners] if len(digits) > 2 else []
    across_v, up_v, *going = to_cross(own_v, up_v, state[0], own_v_beside, *partners, states=summed)
    swap_v = sent(across_v, swap)
    (late_k,) = after([own_k], state[0])
    up_k = sent(late_k, up)
    own_k_beside = sent(late_k, beside)
    up_v_beside = sent(up_v, beside)
    for place, digit in enumerate(digits[1:-1]):
        if place:
            going = [digit_sums(own_sums, partners, across_v)]
        partners += swapped(going[0], *digit)
    state = call(
        [(late_k, own_v), (own_k_beside, own_v_beside)],
        lambda c: [c, pick(c, (1, 1), (3, 1))],
        state,
        False,
        waits=[across_v],
    )

    (swap_v,) = after([swap_v], state[0])
    summed = [own_sums, *partners] if len(digits) > 1 else []
    across_k, up_k, *going = to_cross(
        late_k, up_k, state[0], up_v_beside, gain_row, *partners, states=summed
    )
    swap_k = sent(across_k, swap)
    far_k = sent(up_k, further)
    far_v = sent(swap_v, onward)
    up_k_beside = sent(up_k, beside)
    final = swapped(going[0], *digits[-1]) if len(digits) > 1 else []
    state = call(
        [(up_k, up_v), (up_k_beside, up_v_beside)],
        lambda c: [c - LAYER, pick(c, (0, 3), (2, 3), (1, 5), (3, 5))],
        state,
        False,
        waits=[across_k],
    )

    swap_k, swap_v = after([swap_k, swap_v], state[0], far_v, *final)
    swap_k_beside = sent(swap_k, beside)
    swap_v_beside = sent(swap_v, beside)
    self_mixed = self_mix(jnp.transpose(queries), own_sums, gain_row, partners + final, digits, swap_k)
    cross_mixed = call(
        [(swap_k, swap_v), (swap_k_beside, swap_v_beside), (far_k, far_v)],
        lambda c: [
            c - 2,
            pick(c, (0, 1), (1, 3), (2, 1), (3, 3)),
            pick(c, (0, 5), (2, 5)),
        ],
        state,
        True,
        waits=[self_mixed],
    )[0]
    return (jnp.transpose(self_mixed), jnp.transpose(cross_mixed))


def solution(mesh):
    in_specs = (
        P(("groups", "tm"), None),
        P(("groups", "tm"), None),
        P(("groups", "tm"), None),
        P(("groups", "tm"), None),
        P(("groups", "tm"), None, None),
        P(("groups", "tm"), None, None),
        P("groups", None),
        P("groups", None),
        P("groups"),
        P("groups"),
        P("groups"),
        P("groups", None),
        P(),
    )
    out_specs = (P(("groups", "tm"), None), P(("groups", "tm"), None))
    return jax.shard_map(local, mesh=mesh, in_specs=in_specs, out_specs=out_specs, check_vma=False)
```

```python
import functools
import math

import jax
import jax.numpy as jnp
from jax import lax
from jax.experimental import pallas as pl
from jax.experimental.pallas import tpu as pltpu
from jax.sharding import PartitionSpec as P

HD = 32
SPAN = 6
QUAD = 128
LAYER = 4
BF = jnp.bfloat16
F32 = jnp.float32
EMPTY = -1e30
STEP = 3
PARTS = 3
COPIES = 2
ROOM = 66_900_000


def vmem():
    return pl.BlockSpec(memory_space=pltpu.VMEM)


def smem():
    return pl.BlockSpec(memory_space=pltpu.SMEM)


def anywhere():
    return pl.BlockSpec(memory_space=pl.ANY)


def cost(flops, moved, exps=0):
    flops, moved = flops // 1000, moved // 1000
    return pl.CostEstimate(flops=flops, bytes_accessed=moved, transcendentals=exps)


def quad_rows(ref, q, width):
    if (q + 1) * QUAD <= width:
        return ref[q * QUAD : (q + 1) * QUAD, :]
    part = ref[q * QUAD : width, :]
    fill = jnp.zeros(((q + 1) * QUAD - width, part.shape[1]), part.dtype)
    return jnp.concatenate([part, fill], axis=0)


def part_rows(width, quads, part):
    low = part * (quads // PARTS) * QUAD
    return pl.ds(low, min(quads // PARTS * QUAD, width - low))


def turned_quad(keys, used, rows):
    turned = jnp.transpose(keys.astype(F32))
    return jnp.where(rows < used, turned, turned[0:1, :]).astype(BF)


def no_kernel(*refs):
    del refs


def after(blocks, *tokens):
    return pl.pallas_call(
        no_kernel,
        in_specs=[anywhere()] * (len(blocks) + len(tokens)),
        out_specs=[anywhere()] * len(blocks),
        out_shape=[jax.ShapeDtypeStruct(block.shape, block.dtype) for block in blocks],
        input_output_aliases={place: place for place in range(len(blocks))},
        cost_estimate=cost(0, 0),
        name="after",
    )(*blocks, *tokens)


def across_kernel(waits, count, own_hbm, up_hbm, *refs):
    states_hbm, refs = refs[waits : waits + count], refs[waits + count :]
    across_hbm, _, *refs = refs
    if count:
        sent_hbm, held, in_sems, out_sems, own_state, partners, sent_here, state_sems = refs
    else:
        held, in_sems, out_sems = refs
    lower = lax.axis_index("tm") % LAYER < LAYER // 2
    piece = own_hbm.shape[0] // COPIES

    def move_in(source, part):
        at = pl.ds(part * piece, piece)
        return pltpu.make_async_copy(source.at[at], held.at[at], in_sems.at[part])

    def move_out(part):
        at = pl.ds(part * piece, piece)
        return pltpu.make_async_copy(held.at[at], across_hbm.at[at], out_sems.at[part])

    @pl.when(lower)
    def _():
        for part in range(COPIES):
            move_in(own_hbm, part).start()

    @pl.when(jnp.logical_not(lower))
    def _():
        for part in range(COPIES):
            move_in(up_hbm, part).start()

    moves = []
    for n in range(count):
        into = partners.at[n - 1] if n else own_state
        moves.append(pltpu.make_async_copy(states_hbm[n], into, state_sems.at[n]))
    for move in moves:
        move.start()
    for part in range(COPIES):
        move_in(up_hbm, part).wait()
        move_out(part).start()
    for move in moves:
        move.wait()
    if count:
        digit_step(own_state, [partners.at[n] for n in range(count - 1)], sent_here)
        away = pltpu.make_async_copy(sent_here, sent_hbm, state_sems.at[count])
        away.start()
        away.wait()
    for part in range(COPIES):
        move_out(part).wait()


def to_cross(own, up, *tokens, states=()):
    shape = jax.ShapeDtypeStruct(own.shape, own.dtype)
    outs = [shape, shape]
    scratch = [
        pltpu.VMEM(own.shape, own.dtype),
        pltpu.SemaphoreType.DMA((COPIES,)),
        pltpu.SemaphoreType.DMA((COPIES,)),
    ]
    if states:
        state = states[0].shape
        outs.append(jax.ShapeDtypeStruct(state, BF))
        scratch += [
            pltpu.VMEM(state, F32),
            pltpu.VMEM((len(states) - 1,) + state, BF),
            pltpu.VMEM(state, BF),
            pltpu.SemaphoreType.DMA((len(states) + 1,)),
        ]
    return pl.pallas_call(
        functools.partial(across_kernel, len(tokens), len(states)),
        in_specs=[anywhere()] * (2 + len(tokens) + len(states)),
        out_specs=[anywhere()] * len(outs),
        out_shape=outs,
        input_output_aliases={1: 1},
        scratch_shapes=scratch,
        cost_estimate=cost(0, 4 * own.size),
        compiler_params=pltpu.CompilerParams(vmem_limit_bytes=ROOM),
        name="to_cross",
    )(own, up, *tokens, *states)


def attend_kernel(setup, start_ref, end_ref, tokens_ref, region_ref, *refs):
    count, first, last, held, waits, prompts, width, tokens, tiles = setup
    tile = tokens // tiles
    quads = -(-width // QUAD)
    rounds = quads // STEP
    query_hbm, refs = refs[0], refs[1:]
    key_hbm, refs = refs[:count], refs[count:]
    value_hbm, refs = refs[:count], refs[count + waits :]
    if not first:
        state_in, refs = refs[:2], refs[2:]
    if last:
        out_ref, refs = refs[0], refs[1:]
    else:
        state_out, refs = refs[:2], refs[2:]
    keys, vals, marks, queries, spread, levels, totals, level, total, *refs = refs
    s_a, s_b, p_a, p_b, f_a, f_b, work, found, used, ready, sems, tile_sems = refs
    scale = math.log2(math.e) / math.sqrt(HD)
    none = jnp.zeros((HD, tile), BF)
    i = pl.program_id(0)

    def copies(b, at):
        return (
            pltpu.make_async_copy(key_hbm[b], keys.at[at], sems.at[at, 0]),
            pltpu.make_async_copy(value_hbm[b], vals.at[at, pl.ds(0, width)], sems.at[at, 1]),
        )

    def query_move(t):
        columns = pl.ds(t * tile, tile)
        return pltpu.make_async_copy(query_hbm.at[:, columns], queries.at[t], tile_sems.at[t, 0])

    def state_moves(t, into):
        for place, held_here in enumerate((levels, totals)):
            if into:
                yield pltpu.make_async_copy(state_in[place].at[t], held_here.at[t], tile_sems.at[t, 1 + place])
            else:
                yield pltpu.make_async_copy(held_here.at[t], state_out[place].at[t], tile_sems.at[t, 3 + place])

    @pl.when(i == 0)
    def _():
        if first:
            for t in range(tiles):
                query_move(t).start()
        if last:
            for move in state_moves(0, True):
                move.start()
        stretch = lax.axis_index("tm")
        wanted = []
        lengths = [jnp.int32(0)] * tiles
        for b, owner in enumerate(held(stretch)):
            if owner is None:
                seen = [jnp.int32(1)] * tiles
                used[b] = jnp.int32(QUAD)
            else:
                safe = jnp.clip(owner, 0, prompts - 1)
                covers = (
                    (owner >= 0)
                    & (start_ref[safe] <= stretch)
                    & (stretch < end_ref[safe])
                )
                used[b] = tokens_ref[safe]
                seen = [
                    (covers & (region_ref[t, safe] == 1)).astype(jnp.int32)
                    for t in range(tiles)
                ]
            for t in range(tiles):
                work[t * count + lengths[t]] = jnp.int32(b)
                lengths[t] = lengths[t] + seen[t]
            wanted.append(functools.reduce(jnp.add, seen) > 0)
            ready[b] = jnp.int32(0)

            @pl.when(wanted[b])
            def _():
                for move in copies(b, b):
                    move.start()

        for t in range(tiles):
            found[t] = lengths[t]

            if not first:

                @pl.when(lengths[t] > 0)
                def _():
                    query_move(t).start()

            if not first and not (last and t == 0):

                @pl.when((lengths[t] > 0) | last)
                def _():
                    for move in state_moves(t, True):
                        move.start()

        for q in range(quads):
            for h in range(QUAD // HD):
                off = (1 - h % 2) * tile
                spread[q, h * HD : (h + 1) * HD, off : off + tile] = none
        lanes = lax.broadcasted_iota(jnp.int32, (16, QUAD), 1)
        for b in range(count):
            marks[b] = jnp.where(lanes < used[b], 1.0, 0.0).astype(BF)
            if width < quads * QUAD:
                vals[b, width:, :] = jnp.zeros((quads * QUAD - width, QUAD), BF)

    def arrived(b):
        @pl.when(ready[b] == 0)
        def _():
            for move in copies(0, b):
                move.wait()
            ready[b] = jnp.int32(1)

    low_half = lax.broadcasted_iota(jnp.int32, (QUAD, QUAD), 1) < QUAD // 2
    row16 = lax.broadcasted_iota(jnp.int32, (16, QUAD), 0)
    zeros = jnp.zeros((QUAD // 2, QUAD), BF)

    def score(b, g, s_to):
        for k in range(STEP):
            block = keys[b, g * STEP + k].astype(F32)
            both = jnp.concatenate(
                [jnp.where(low_half, block, 0.0), jnp.where(low_half, 0.0, block)], axis=0
            ).astype(BF)
            s_to[k] = jnp.dot(both, spread[g * STEP + k], preferred_element_type=F32)

    def weigh(g, s_from, p_to, f_to):
        for k in range(STEP):
            q = g * STEP + k
            for pair in range(2):
                at = slice(pair * QUAD, (pair + 1) * QUAD)
                part = s_from[k, at, :]
                old = level[q, pair : pair + 1]
                new = jnp.maximum(old, jnp.max(part, axis=0, keepdims=True))
                p_to[k, at, :] = jnp.exp2((part - new) * scale).astype(BF)
                f_to[k, pair : pair + 1] = jnp.exp2((old - new) * scale)
                level[q, pair : pair + 1] = new

    def mix(b, many, ones, g, p_from, f_from):
        for k in range(STEP):
            q = g * STEP + k
            v = vals[b, q * QUAD : (q + 1) * QUAD, :] * many
            left = jnp.concatenate(
                [
                    jnp.concatenate([v[: QUAD // 2], zeros], axis=1),
                    jnp.concatenate([zeros, v[QUAD // 2 :]], axis=1),
                    ones,
                ],
                axis=0,
            )
            out = jnp.dot(left, p_from[k], preferred_element_type=F32)
            factor = f_from[k]
            level[q, 2:4] = level[q, 2:4] * factor + out[QUAD : QUAD + 2]
            for pair in range(2):
                r = pair * 2 * HD
                added = jnp.concatenate([out[r : r + HD, :tile], out[r + HD : r + 2 * HD, tile:]], axis=1)
                at = slice(pair * HD, (pair + 1) * HD)
                total[q, at, :] = total[q, at, :] * factor[pair : pair + 1] + added

    slots = [(s_a, p_a, f_a), (s_b, p_b, f_b)]
    n = found[i]
    if first:
        level[:, 0:2] = jnp.full((quads, 2, 2 * tile), EMPTY, F32)
        level[:, 2:4] = jnp.zeros((quads, 2, 2 * tile), F32)
        total[...] = jnp.zeros(total.shape, F32)
    else:

        @pl.when((n > 0) | last)
        def _():
            for move in state_moves(i, True):
                move.wait()
            level[...] = levels[i]
            total[...] = totals[i]

    @pl.when(n > 0)
    def _():
        query_move(i).wait()
        for r in range(0, quads * QUAD, HD):
            q, h = r // QUAD, r % QUAD // HD
            on = h % 2 * tile
            piece = queries[i, r : r + HD, :] if r < width else none
            spread[q, h * HD : (h + 1) * HD, on : on + tile] = piece
        b0 = work[i * count]
        arrived(b0)
        score(b0, 0, s_a)
        weigh(0, s_a, p_a, f_a)
        score(b0, 1, s_b)

        def entry(j, carry):
            b = work[i * count + j]
            later = work[i * count + jnp.minimum(j + 1, n - 1)]
            arrived(later)
            mark = marks[b]
            many = jnp.concatenate([mark] * (QUAD // 16), axis=0)
            mark = mark.astype(F32)
            ones = jnp.concatenate(
                [jnp.where(row16 == 0, mark, 0.0), jnp.where(row16 == 1, mark, 0.0)], axis=1
            ).astype(BF)
            for g in range(rounds):
                here, there = slots[g % 2], slots[(g + 1) % 2]
                score(b if g + 2 < rounds else later, (g + 2) % rounds, here[0])
                mix(b, many, ones, g, here[1], here[2])
                weigh((g + 1) % rounds, there[0], there[1], there[2])
            return carry

        lax.fori_loop(0, n, entry, 0)

    if last:
        for q in range(quads):
            scaled = 1.0 / level[q, 2:4]
            for pair in range(2):
                mixed = total[q, pair * HD : (pair + 1) * HD, :] * scaled[pair : pair + 1]
                for side in range(2):
                    r = q * QUAD + (2 * pair + side) * HD
                    if r < width:
                        out_ref[r : r + HD, :] = mixed[:, side * tile : (side + 1) * tile].astype(BF)
    else:

        @pl.when((n > 0) | first)
        def _():
            levels[i] = level[...]
            totals[i] = total[...]
            for move in state_moves(i, False):
                move.start()

        @pl.when(i == tiles - 1)
        def _():
            for t in range(tiles):

                @pl.when((found[t] > 0) | first)
                def _():
                    for move in state_moves(t, False):
                        move.wait()


def attend(spans, queries, blocks, held, state, last, waits=()):
    width, tokens = queries.shape
    quads = -(-width // QUAD)
    count = len(blocks)
    tiles, prompts = spans[3].shape
    tile = tokens // tiles
    first = state is None
    setup = (count, first, last, held, len(waits), prompts, width, tokens, tiles)
    level, total = (quads, 4, 2 * tile), (quads, 2 * HD, 2 * tile)
    aliases = {}
    if last:
        outs = [jax.ShapeDtypeStruct((width, tokens), BF)]
        out_specs = [pl.BlockSpec((width, tile), lambda i: (0, i))]
    else:
        outs = [jax.ShapeDtypeStruct((tiles,) + shape, F32) for shape in (level, total)]
        out_specs = [anywhere()] * 2
        if not first:
            at = 5 + 2 * count + len(waits)
            aliases = {at: 0, at + 1: 1}
    keys = [block[0] for block in blocks]
    values = [block[1] for block in blocks]
    scratch = [
        pltpu.VMEM((count, quads, QUAD, QUAD), BF),
        pltpu.VMEM((count, quads * QUAD, QUAD), BF),
        pltpu.VMEM((count, 16, QUAD), BF),
        pltpu.VMEM((tiles, width, tile), BF),
        pltpu.VMEM((quads, QUAD, 2 * tile), BF),
        pltpu.VMEM((tiles,) + level, F32),
        pltpu.VMEM((tiles,) + total, F32),
        pltpu.VMEM(level, F32),
        pltpu.VMEM(total, F32),
    ]
    scratch += [pltpu.VMEM((STEP, 2 * QUAD, 2 * tile), F32)] * 2
    scratch += [pltpu.VMEM((STEP, 2 * QUAD, 2 * tile), BF)] * 2
    scratch += [pltpu.VMEM((STEP, 2, 2 * tile), F32)] * 2
    scratch += [
        pltpu.SMEM((count * tiles + 1,), jnp.int32),
        pltpu.SMEM((tiles,), jnp.int32),
        pltpu.SMEM((count,), jnp.int32),
        pltpu.SMEM((count,), jnp.int32),
        pltpu.SemaphoreType.DMA((count, 2)),
        pltpu.SemaphoreType.DMA((tiles, 5)),
    ]
    area = count * QUAD * tokens
    return pl.pallas_call(
        functools.partial(attend_kernel, setup),
        grid=(tiles,),
        in_specs=[smem()] * 4 + [anywhere()] * (1 + 2 * count + len(waits) + (0 if first else 2)),
        out_specs=out_specs,
        out_shape=outs,
        scratch_shapes=scratch,
        input_output_aliases=aliases,
        cost_estimate=cost(40 * area * width, 4 * width * tokens, area * width // HD),
        compiler_params=pltpu.CompilerParams(vmem_limit_bytes=ROOM),
        name="attend",
    )(
        *spans,
        queries,
        *keys,
        *values,
        *waits,
        *([] if first else state),
    )


def front_kernel(tokens_ref, *refs):
    sources, (own_ref, sent_ref), turned_hbm, refs = refs[:4], refs[4:6], refs[6:8], refs[8:]
    arrays, turned, (in_sems, out_sems) = refs[:4], refs[4:6], refs[6:]
    rows = lax.broadcasted_iota(jnp.int32, (QUAD, QUAD), 0)
    columns = lax.broadcasted_iota(jnp.int32, (QUAD, QUAD), 1)
    width, quads = arrays[0].shape[0], sent_ref.shape[0]
    every = quads // PARTS

    def move_in(n, part):
        at = part_rows(width, quads, part)
        return pltpu.make_async_copy(sources[n].at[at], arrays[n].at[at], in_sems.at[n, part])

    def move_out(n, part):
        at = pl.ds(part * every, every)
        return pltpu.make_async_copy(turned[n].at[at], turned_hbm[n].at[at], out_sems.at[n, part])

    for part in range(PARTS):
        for n in range(2):
            move_in(n, part).start()
    for n in range(2, 4):
        for part in range(PARTS):
            move_in(n, part).start()
    for n in range(2):
        used = QUAD if n else tokens_ref[lax.axis_index("tm")]
        for q in range(quads):
            if q % every == 0:
                move_in(2 + n, q // every).wait()
            turned[n][q] = turned_quad(quad_rows(arrays[2 + n], q, width), used, rows)
            if q % every == every - 1:
                move_out(n, q // every).start()
    for q in range(quads):
        if q % every == 0:
            for n in range(2):
                move_in(n, q // every).wait()
        lifted = jnp.maximum(quad_rows(arrays[0], q, width), 0)
        grown = lax.dot_general(
            quad_rows(arrays[1], q, width), lifted, (((1,), (1,)), ((), ())), preferred_element_type=F32
        )
        grown = jnp.where(rows // HD == columns // HD, grown, 0.0)
        folded = grown[0:HD] + grown[HD : 2 * HD] + grown[2 * HD : 3 * HD] + grown[3 * HD :]
        own_ref[q] = folded
        sent_ref[q] = folded.astype(BF)
    for n in range(2):
        for part in range(PARTS):
            move_out(n, part).wait()


def front(tokens, keys, values, prompt_keys, caption_keys):
    width = keys.shape[0]
    quads = -(-width // QUAD)
    arrays = (keys, values, prompt_keys, caption_keys)
    state, turned = (quads, HD, QUAD), (quads, QUAD, QUAD)
    return pl.pallas_call(
        front_kernel,
        in_specs=[smem()] + [anywhere()] * 4,
        out_specs=[vmem()] * 2 + [anywhere()] * 2,
        out_shape=[jax.ShapeDtypeStruct(state, F32), jax.ShapeDtypeStruct(state, BF)]
        + [jax.ShapeDtypeStruct(turned, BF)] * 2,
        scratch_shapes=[pltpu.VMEM(array.shape, BF) for array in arrays]
        + [pltpu.VMEM(turned, BF)] * 2
        + [pltpu.SemaphoreType.DMA((4, PARTS)), pltpu.SemaphoreType.DMA((2, PARTS))],
        cost_estimate=cost(8 * width * QUAD * keys.shape[1], 4 * keys.size),
        compiler_params=pltpu.CompilerParams(vmem_limit_bytes=ROOM),
        name="front",
    )(tokens, *arrays)


def lower_sum(hop, prior, partners):
    digit = lax.axis_index("tm") // hop % (len(partners) + 1)
    for d, partner in enumerate(partners, 1):
        prior = prior + jnp.where((digit ^ d) < digit, partner.astype(F32), 0.0)
    return prior


def digit_step(own_ref, partners, sent_out):
    for q in range(sent_out.shape[0]):
        whole = own_ref[q]
        for partner in partners:
            whole = whole + partner[q].astype(F32)
        sent_out[q] = whole.astype(BF)


def digit_kernel(own_ref, *refs):
    digit_step(own_ref, refs[:-2], refs[-1])


def digit_sums(own, partners, token):
    return pl.pallas_call(
        digit_kernel,
        in_specs=[vmem()] * (1 + len(partners)) + [anywhere()],
        out_specs=vmem(),
        out_shape=jax.ShapeDtypeStruct(own.shape, BF),
        cost_estimate=cost(0, 8 * own.size),
        compiler_params=pltpu.CompilerParams(vmem_limit_bytes=ROOM),
        name="digit_sums",
    )(own, *partners, token)


def digits_of(size):
    hop, digits = 1, []
    while hop < size:
        radix = LAYER if hop == 1 and size % LAYER == 0 else 2
        digits.append((hop, radix))
        hop *= radix
    return digits


def swapped(block, hop, radix):
    size = lax.axis_size("tm")
    return [sent(block, [(i, i ^ (d * hop)) for i in range(size)]) for d in range(1, radix)]


def norm_kernel(digits, queries_hbm, gain_hbm, own_hbm, *refs):
    count = sum(radix - 1 for _, radix in digits)
    partners_hbm, refs = refs[:count], refs[count + 1 :]
    out_hbm, queries, raw, out, gain_ref, own_ref, partners, in_sems, out_sems, state_sems = refs
    rows = lax.broadcasted_iota(jnp.int32, (QUAD, QUAD), 0) // HD
    columns = lax.broadcasted_iota(jnp.int32, (QUAD, QUAD), 1) // HD
    width = queries.shape[0]
    quads, tokens = raw.shape[0], raw.shape[2]
    every = quads // PARTS

    def move_in(part):
        at = part_rows(width, quads, part)
        return pltpu.make_async_copy(queries_hbm.at[at], queries.at[at], in_sems.at[part])

    def move_out(part):
        at = part_rows(width, quads, part)
        return pltpu.make_async_copy(out.at[at], out_hbm.at[at], out_sems.at[part])

    moves = [
        pltpu.make_async_copy(own_hbm, own_ref, state_sems.at[count]),
        pltpu.make_async_copy(gain_hbm, gain_ref, state_sems.at[count + 1]),
    ]
    for n in range(count):
        moves.append(pltpu.make_async_copy(partners_hbm[n], partners.at[n], state_sems.at[n]))
    for move in moves:
        move.start()
    for part in range(PARTS):
        move_in(part).start()
    for move in moves:
        move.wait()
    squares = jnp.zeros((1, tokens), F32)
    for q in range(quads):
        if q % every == 0:
            move_in(q // every).wait()
        whole, first = own_ref[q], 0
        for hop, radix in digits:
            whole = lower_sum(hop, whole, [partners[first + n, q] for n in range(radix - 1)])
            first += radix - 1
        whole = whole.astype(BF).astype(F32)
        wide = jnp.where(rows == columns, jnp.concatenate([whole] * (QUAD // HD), axis=0), 0.0).astype(BF)
        lifted = jnp.maximum(quad_rows(queries, q, width), 0)
        part = jnp.dot(wide, lifted, preferred_element_type=F32)
        raw[q] = part
        squares = squares + jnp.sum(part * part, axis=0, keepdims=True)
    factor = lax.rsqrt(squares / width + 1e-05)
    for q in range(quads):
        size = min(QUAD, width - q * QUAD)
        gain = gain_ref[:, q * QUAD : q * QUAD + size]
        if size < QUAD:
            gain = jnp.concatenate([gain, jnp.zeros((1, QUAD - size), F32)], axis=1)
        gains = jnp.transpose(jnp.broadcast_to(gain, (QUAD, QUAD)))
        gains = jnp.concatenate([gains] * (tokens // QUAD), axis=1)
        mixed = (raw[q] * factor * gains).astype(BF)
        out[q * QUAD : q * QUAD + size, :] = mixed[:size]
        if q % every == every - 1:
            move_out(q // every).start()
    for part in range(PARTS):
        move_out(part).wait()


def self_mix(queries, own, gain, partners, digits, token):
    width, tokens = queries.shape
    quads = -(-width // QUAD)
    return pl.pallas_call(
        functools.partial(norm_kernel, tuple(digits)),
        in_specs=[anywhere()] * (4 + len(partners)),
        out_specs=anywhere(),
        out_shape=jax.ShapeDtypeStruct((width, tokens), BF),
        scratch_shapes=[
            pltpu.VMEM((width, tokens), BF),
            pltpu.VMEM((quads, QUAD, tokens), F32),
            pltpu.VMEM((width, tokens), BF),
            pltpu.VMEM(gain.shape, F32),
            pltpu.VMEM(own.shape, F32),
            pltpu.VMEM((len(partners),) + own.shape, BF),
            pltpu.SemaphoreType.DMA((PARTS,)),
            pltpu.SemaphoreType.DMA((PARTS,)),
            pltpu.SemaphoreType.DMA((len(partners) + 2,)),
        ],
        cost_estimate=cost(8 * width * QUAD * tokens, 4 * width * tokens),
        compiler_params=pltpu.CompilerParams(vmem_limit_bytes=ROOM),
        name="self_mix",
    )(queries, gain, own, *partners, token)


def sent(block, pairs):
    return lax.ppermute(block, "tm", pairs)


def local(
    queries,
    keys,
    values,
    cross_queries,
    prompt_keys,
    prompt_values,
    caption_keys,
    caption_values,
    span_start,
    span_end,
    prompt_tokens,
    region_mask,
    out_gain,
):
    size = lax.axis_size("tm")
    slots, width = prompt_keys.shape[1:]
    spans = (span_start, span_end, prompt_tokens, jnp.transpose(region_mask))
    turned = lambda block: jnp.transpose(block.reshape(slots, width))
    queries_t = jnp.transpose(cross_queries)
    call = functools.partial(attend, spans, queries_t)

    bases = [LAYER * z for z in range(size // LAYER)]
    beside = [(i, i ^ 1) for i in range(size)]
    up = [(i, (i + LAYER) % size) for i in range(size)]
    swap = [(i, i ^ 2) for i in range(size)]
    onward = [(i, i + LAYER - 1) for i in range(size) if i % 2 and i + LAYER - 1 < size]
    further = [(i, i + 1) for i in range(size) if i % 2 and i + 1 < size]
    spot = lambda c: c % LAYER
    pick = lambda c, *ways: functools.reduce(
        lambda rest, way: jnp.where(spot(c) == way[0], c - way[1], rest), ways, -1
    )
    digits = digits_of(size)

    own_v = turned(prompt_values)
    up_v = sent(own_v, up)
    own_v_beside = sent(own_v, beside)
    own_sums, going, own_k, caption_k = front(
        prompt_tokens,
        jnp.transpose(keys),
        jnp.transpose(values),
        turned(prompt_keys),
        jnp.transpose(caption_keys),
    )
    partners = swapped(going, *digits[0])
    gain_row = out_gain.reshape(1, width)
    state = call([(caption_k, jnp.transpose(caption_values))], lambda c: [None], None, False, waits=[going])

    summed = [own_sums, *partners] if len(digits) > 2 else []
    across_v, up_v, *going = to_cross(own_v, up_v, state[0], own_v_beside, *partners, states=summed)
    swap_v = sent(across_v, swap)
    (late_k,) = after([own_k], state[0])
    up_k = sent(late_k, up)
    own_k_beside = sent(late_k, beside)
    up_v_beside = sent(up_v, beside)
    for place, digit in enumerate(digits[1:-1]):
        if place:
            going = [digit_sums(own_sums, partners, across_v)]
        partners += swapped(going[0], *digit)
    state = call(
        [(late_k, own_v), (own_k_beside, own_v_beside)],
        lambda c: [c, pick(c, (1, 1), (3, 1))],
        state,
        False,
        waits=[across_v],
    )

    (swap_v,) = after([swap_v], state[0])
    summed = [own_sums, *partners] if len(digits) > 1 else []
    across_k, up_k, *going = to_cross(
        late_k, up_k, state[0], up_v_beside, gain_row, *partners, states=summed
    )
    swap_k = sent(across_k, swap)
    far_k = sent(up_k, further)
    far_v = sent(swap_v, onward)
    up_k_beside = sent(up_k, beside)
    final = swapped(going[0], *digits[-1]) if len(digits) > 1 else []
    state = call(
        [(up_k, up_v), (up_k_beside, up_v_beside)],
        lambda c: [c - LAYER, pick(c, (0, 3), (2, 3), (1, 5), (3, 5))],
        state,
        False,
        waits=[across_k],
    )

    swap_k, swap_v = after([swap_k, swap_v], state[0], *final)
    swap_k_beside = sent(swap_k, beside)
    swap_v_beside = sent(swap_v, beside)
    self_mixed = self_mix(jnp.transpose(queries), own_sums, gain_row, partners + final, digits, swap_k)
    cross_mixed = call(
        [(swap_k, swap_v), (swap_k_beside, swap_v_beside), (far_k, far_v)],
        lambda c: [
            c - 2,
            pick(c, (0, 1), (1, 3), (2, 1), (3, 3)),
            pick(c, (0, 5), (2, 5)),
        ],
        state,
        True,
        waits=[self_mixed],
    )[0]
    return (jnp.transpose(self_mixed), jnp.transpose(cross_mixed))


def solution(mesh):
    in_specs = (
        P(("groups", "tm"), None),
        P(("groups", "tm"), None),
        P(("groups", "tm"), None),
        P(("groups", "tm"), None),
        P(("groups", "tm"), None, None),
        P(("groups", "tm"), None, None),
        P("groups", None),
        P("groups", None),
        P("groups"),
        P("groups"),
        P("groups"),
        P("groups", None),
        P(),
    )
    out_specs = (P(("groups", "tm"), None), P(("groups", "tm"), None))
    return jax.shard_map(local, mesh=mesh, in_specs=in_specs, out_specs=out_specs, check_vma=False)
```
